32 devices in a mesh: dp: 32 (over z, y, x, core).
Axes of the slice: x: 2, y: 2, z: 4, core: 2. Of those that a mesh axis runs over, the one named last changes fastest.
Arguments:
- sequence_elements: bfloat16 [5120, 1536], P('dp'), may hold values from -6 to 6
- result_sensitivity: bfloat16 [5120, 1536], P('dp'), may hold values from -6 to 6
- mixer_gain: bfloat16 [1536], replicated, may hold values from 0.5 to 1.5
- mixer_offset: bfloat16 [1536], replicated, may hold values from -1.5 to 1.5
- question_matrix: bfloat16 [1536, 1536], replicated, may hold values from -0.15625 to 0.15625
- lookup_matrix: bfloat16 [1536, 1536], replicated, may hold values from -0.15625 to 0.15625
- content_matrix: bfloat16 [1536, 1536], replicated, may hold values from -0.15625 to 0.15625
- mixer_projection_matrix: bfloat16 [1536, 1536], replicated, may hold values from -0.625 to 0.625
- feedforward_gain: bfloat16 [1536], replicated, may hold values from 0.5 to 1.5
- feedforward_offset: bfloat16 [1536], replicated, may hold values from -1.5 to 1.5
- expand_matrix: bfloat16 [1536, 6144], P('dp'), may hold values from -0.15625 to 0.15625
- inner_neuron_offset: bfloat16 [6144], P('dp'), may hold values from -2.5 to 2.5
- contract_matrix: bfloat16 [6144, 1536], P('dp'), may hold values from -0.15625 to 0.15625
- feedforward_result_offset: bfloat16 [1536], P('dp'), may hold values from -1.5 to 1.5
- sequence_level_choice: int32 [32], P('dp'), may hold values from 0 to 3, as said below
- servers_per_level: int32 [4], replicated, may hold values from 6 to 10, as said below
- accepted_row_limit: int32 [4], replicated, may hold values from 128 to 213, as said below
- server_selection: int32 [32, 160], P('dp'), may hold values from 0 to 318, as said below
Outputs:
- layer_output: bfloat16 [5120, 1536], P('dp')
- layer_input_gradient: bfloat16 [5120, 1536], P('dp')
- leading_norm_gradient: float32 [1536], P('dp')
- leading_bias_gradient: float32 [1536], P('dp')
- query_weight_gradient: float32 [1536, 1536], P('dp')
- key_weight_gradient: float32 [1536, 1536], P('dp')
- value_weight_gradient: float32 [1536, 1536], P('dp')
- attention_output_gradient: float32 [1536, 1536], P('dp')
- middle_norm_gradient: float32 [1536], P('dp')
- middle_bias_gradient: float32 [1536], P('dp')
- up_weight_gradient: float32 [1536, 6144], P('dp')
- hidden_bias_gradient: float32 [6144], P('dp')
- down_weight_gradient: float32 [6144, 1536], P('dp')
- output_bias_gradient: float32 [1536], P('dp')
The draws below stay inside these ranges and needn't reach their ends.
Inputs may be any that keep to these rules, and one draw needn't show every extreme that they name: `sequence_level_choice`: the 1 sequence of one device have different granularity indices. `servers_per_level`: each group holds 3, 4 or 5 sixteenths of the devices, and the groups together hold all devices. `accepted_row_limit`: some prefix has capacity 213. `server_selection`: within each sequence the values are 160 consecutive integers, each once.
All inputs are finite; a program needn't handle non-finite values.
Results may differ from the reference program's by a relative error of at most 0.013.
Values may be sent and summed in bfloat16 or wider, within the bound.
No kernel may reach another device: no remote copies, remote signals or barrier semaphores. Data moves between devices by JAX's collectives and lax.ppermute only.
A program may use at most 384 MiB of HBM per device.

```python
import jax
import jax.numpy as jnp
from jax import lax

EMBED_WIDTH = 1536
HEADS = 12
HEAD_DIM = 128
FF = 6144
LEVELS = 4
SEQ_LEN = 160
SEQ_DEV = 1
SEQS = 32
TOKENS = 5120
CAP_RECV = 213
N_DP = 32


def group_pattern(key):
    key = jax.random.fold_in(key, 101)
    first, second = jax.random.split(key)
    patterns = jnp.array([[3, 4, 4, 5], [3, 3, 5, 5]], dtype=jnp.int32)
    picked = jax.random.randint(first, (), 0, 2)
    chosen = jnp.sum(patterns * (jnp.arange(2)[:, None] == picked).astype(jnp.int32), axis=0)
    return chosen[jax.random.permutation(second, LEVELS)]


def draw_sequence_level_choice(key, part):
    key = jax.random.fold_in(key, 11)
    device_count = SEQS // SEQ_DEV
    scores = jax.random.randint(key, (device_count, LEVELS), 0, 1 << 20) * LEVELS + jnp.arange(LEVELS)[None, :]
    order = jnp.argsort(scores, axis=1)
    return order[:, :SEQ_DEV].reshape(-1).astype(jnp.int32)


def draw_servers_per_level(key, part):
    shares = group_pattern(key)
    unit = SEQS // SEQ_DEV // 16
    return (shares * unit).astype(jnp.int32)


def draw_accepted_row_limit(key, part):
    shares = group_pattern(key)
    key = jax.random.fold_in(key, 13)
    expected = SEQ_DEV * SEQ_LEN * 4 // shares
    extra = jax.random.randint(key, (LEVELS,), 0, 9) * (shares != 5).astype(jnp.int32)
    return jnp.minimum(CAP_RECV, expected + expected * extra // 32).astype(jnp.int32)


def draw_server_selection(key, part):
    key = jax.random.fold_in(key, 14)
    first, second, third = jax.random.split(key, 3)
    scores = jax.random.randint(first, (SEQS, SEQ_LEN), 0, 1 << 20) * SEQ_LEN + jnp.arange(SEQ_LEN)[None, :]
    order = jnp.argsort(scores, axis=1)
    offset = jax.random.randint(second, (SEQS,), 0, SEQ_LEN)
    lowest = jax.random.randint(third, (), 0, SEQS)
    highest = (lowest + 1 + jax.random.randint(jax.random.fold_in(third, 1), (), 0, SEQS - 1)) % SEQS
    offset = jnp.where(jnp.arange(SEQS) == lowest, 0, offset)
    offset = jnp.where(jnp.arange(SEQS) == highest, SEQ_LEN - 1, offset)
    return (order + offset[:, None]).astype(jnp.int32)


def level_of(rng, extent, cuts, least, largest):
    def one(position, shards_of):
        heights = jax.random.uniform(jax.random.fold_in(jax.random.fold_in(rng, 6), position), (shards_of,), jnp.float32, least / len(cuts), largest / len(cuts))
        return jnp.repeat(jnp.exp(heights), extent[position] // shards_of).reshape((-1,) + (1,) * (len(extent) - position - 1))

    level = one(*cuts[0])
    for cut in cuts[1:]:
        level = level * one(*cut)
    return level


def gaussian(stream_key, shape, scale, bound, cuts=(), held_as=jnp.bfloat16):
    values = jax.random.normal(stream_key, shape, jnp.float32) * scale
    if len(cuts) > 0:
        values = level_of(stream_key, shape, cuts, -0.22, 0.18) * values
    return jnp.clip(values, min=-bound, max=bound).astype(held_as)


def setup_inputs(seed: int = 0) -> dict:
    seeds = jax.random.split(jax.random.key(seed), 19)
    sequence_elements = gaussian(seeds[0], (TOKENS, EMBED_WIDTH), 1.0, 6.0, ((0, 32),))
    result_sensitivity = gaussian(seeds[1], (TOKENS, EMBED_WIDTH), 1.0, 6.0, ((0, 32),))
    mixer_gain = jnp.clip(1.0 + 0.1 * jax.random.normal(seeds[2], (EMBED_WIDTH,), jnp.float32), 0.5, 1.5).astype(jnp.bfloat16)
    mixer_offset = gaussian(seeds[3], (EMBED_WIDTH,), 0.3, 1.5)
    question_matrix = gaussian(seeds[4], (EMBED_WIDTH, EMBED_WIDTH), EMBED_WIDTH ** -0.5, 0.15625)
    lookup_matrix = gaussian(seeds[5], (EMBED_WIDTH, EMBED_WIDTH), EMBED_WIDTH ** -0.5, 0.15625)
    content_matrix = gaussian(seeds[6], (EMBED_WIDTH, EMBED_WIDTH), EMBED_WIDTH ** -0.5, 0.15625)
    mixer_projection_matrix = gaussian(seeds[7], (EMBED_WIDTH, EMBED_WIDTH), (EMBED_WIDTH // 16) ** -0.5, 0.625)
    feedforward_gain = jnp.clip(1.0 + 0.1 * jax.random.normal(seeds[8], (EMBED_WIDTH,), jnp.float32), 0.5, 1.5).astype(jnp.bfloat16)
    feedforward_offset = gaussian(seeds[9], (EMBED_WIDTH,), 0.3, 1.5)
    expand_matrix = gaussian(seeds[10], (EMBED_WIDTH, FF), EMBED_WIDTH ** -0.5, 0.15625, ((0, 32),))
    inner_neuron_offset = gaussian(seeds[11], (FF,), 0.5, 2.5, ((0, 32),))
    contract_matrix = gaussian(seeds[12], (FF, EMBED_WIDTH), (FF // 4) ** -0.5, 0.15625, ((0, 32),))
    feedforward_result_offset = gaussian(seeds[13], (EMBED_WIDTH,), 0.3, 1.5, ((0, 32),))
    sequence_level_choice = draw_sequence_level_choice(jax.random.fold_in(seeds[18], 71), 0)
    servers_per_level = draw_servers_per_level(jax.random.fold_in(seeds[18], 71), 0)
    accepted_row_limit = draw_accepted_row_limit(jax.random.fold_in(seeds[18], 71), 0)
    server_selection = draw_server_selection(jax.random.fold_in(seeds[18], 71), 0)
    return dict(sequence_elements=sequence_elements, result_sensitivity=result_sensitivity, mixer_gain=mixer_gain, mixer_offset=mixer_offset, question_matrix=question_matrix, lookup_matrix=lookup_matrix, content_matrix=content_matrix, mixer_projection_matrix=mixer_projection_matrix, feedforward_gain=feedforward_gain, feedforward_offset=feedforward_offset, expand_matrix=expand_matrix, inner_neuron_offset=inner_neuron_offset, contract_matrix=contract_matrix, feedforward_result_offset=feedforward_result_offset, sequence_level_choice=sequence_level_choice, servers_per_level=servers_per_level, accepted_row_limit=accepted_row_limit, server_selection=server_selection)


HIGH = lax.Precision.HIGHEST
EPSILON = 1e-05
NEGATIVE = -1e+30

@jax.custom_vjp
def low(v):
    return lax.optimization_barrier(v.astype(jnp.bfloat16)).astype(jnp.float32)

@jax.custom_vjp
def low_back(v):
    return v

def low_keep(v):
    return (low(v), None)

def low_pass(kept, grad):
    return (grad,)

def back_keep(v):
    return (v, None)

def back_low(kept, grad):
    return (low(grad),)
low.defvjp(low_keep, low_pass)
low_back.defvjp(back_keep, back_low)

def product(left, right):
    return jnp.dot(left, right, precision=HIGH)

def standardize_rows(values, gain, shift):
    center = values - lax.optimization_barrier(jnp.mean(values, axis=-1, keepdims=True))
    spread = lax.optimization_barrier(jnp.mean(center * center, axis=-1, keepdims=True))
    return center * lax.rsqrt(spread + EPSILON) * gain + shift

def rope_tables():
    half = HEAD_DIM // 2
    places = jnp.arange(SEQ_LEN).astype(jnp.float32)
    rates = 10000.0 ** (-(jnp.arange(half).astype(jnp.float32) * 2.0 / HEAD_DIM))
    angles = places[:, None] * rates[None, :]
    return (jnp.cos(angles), jnp.sin(angles))

def rotate(values, cosine, sine):
    half = values.shape[-1] // 2
    first = values[..., :half]
    second = values[..., half:]
    cosine = cosine[None, :, None, :]
    sine = sine[None, :, None, :]
    return jnp.concatenate([first * cosine - second * sine, second * cosine + first * sine], axis=-1)

def block_forward(block_arguments, learned_tensors, block_kept, block_width):
    mixer_gain, mixer_offset, question_matrix, lookup_matrix, content_matrix, mixer_projection_matrix, feedforward_gain, feedforward_offset, expand_matrix, inner_neuron_offset, contract_matrix, feedforward_result_offset = learned_tensors
    row_count = block_arguments.shape[0]
    shape_heads = (row_count // SEQ_LEN, SEQ_LEN, HEADS, HEAD_DIM)
    first_standardized = low(standardize_rows(block_arguments, mixer_gain, mixer_offset))
    query_rows = low_back(product(first_standardized, question_matrix))
    key_rows = low_back(product(first_standardized, lookup_matrix))
    value_rows = low(low_back(product(first_standardized, content_matrix))).reshape(shape_heads)
    cosine, sine = rope_tables()
    query_rot = low(rotate(query_rows.reshape(shape_heads), cosine, sine))
    key_rot = low(rotate(key_rows.reshape(shape_heads), cosine, sine))
    scale = HEAD_DIM ** (-0.5)
    scores = jnp.einsum('slhe,smhe->shlm', query_rot, key_rot, precision=HIGH) * scale
    scores = low_back(scores)
    causal = jnp.arange(SEQ_LEN)[:, None] >= jnp.arange(SEQ_LEN)[None, :]
    scores = jnp.where(causal, scores, NEGATIVE)
    probs = low(jax.nn.softmax(scores, axis=-1))
    context = jnp.einsum('shlm,smhe->slhe', probs, value_rows, precision=HIGH).reshape(row_count, EMBED_WIDTH)
    context = low(low_back(context))
    mixed = block_arguments + low_back(product(context, mixer_projection_matrix))
    normed_second = low(low_back(standardize_rows(mixed, feedforward_gain, feedforward_offset)))
    hidden = low_back(product(normed_second, expand_matrix) + inner_neuron_offset)
    column_ok = (jnp.arange(FF)[None, :] < block_width[:, None]).astype(jnp.float32)
    active = low(jax.nn.gelu(hidden, approximate=True) * column_ok)
    branch = low(low_back(product(active, contract_matrix) + feedforward_result_offset)) * block_kept[:, None]
    return mixed + branch

def reference(sequence_elements, result_sensitivity, mixer_gain, mixer_offset, question_matrix, lookup_matrix, content_matrix, mixer_projection_matrix, feedforward_gain, feedforward_offset, expand_matrix, inner_neuron_offset, contract_matrix, feedforward_result_offset, sequence_level_choice, servers_per_level, accepted_row_limit, server_selection):
    level_rows = jnp.repeat(sequence_level_choice, SEQ_LEN)
    upper = jnp.cumsum(servers_per_level)
    lower = upper - servers_per_level
    target = lower[level_rows] + server_selection.reshape(-1) % servers_per_level[level_rows]
    target_hot = (target[:, None] == jnp.arange(N_DP)[None, :]).astype(jnp.int32)
    arrival = lax.optimization_barrier(jnp.sum((jnp.cumsum(target_hot, axis=0) - target_hot) * target_hot, axis=1))
    kept = (arrival < accepted_row_limit[level_rows]).astype(jnp.float32)
    width_table = jnp.array([FF // 8 * 2 ** level for level in range(LEVELS)], dtype=jnp.int32)
    widths = width_table[level_rows]
    learned_tensors = tuple((present_item.astype(jnp.float32) for present_item in (mixer_gain, mixer_offset, question_matrix, lookup_matrix, content_matrix, mixer_projection_matrix, feedforward_gain, feedforward_offset, expand_matrix, inner_neuron_offset, contract_matrix, feedforward_result_offset)))
    blocks = N_DP // 8
    block_rows = TOKENS // blocks
    block_arguments = sequence_elements.astype(jnp.float32).reshape(blocks, block_rows, EMBED_WIDTH)
    incoming = result_sensitivity.astype(jnp.float32).reshape(blocks, block_rows, EMBED_WIDTH)

    def step(running_totals, pieces):
        block_in, block_cot, block_kept, block_width = pieces

        def forward(values, weights):
            return block_forward(values, weights, block_kept, block_width)
        result, backward = jax.vjp(forward, block_in, learned_tensors)
        block_grad, weight_grads = backward(block_cot)
        return (tuple((total + grad for total, grad in zip(running_totals, weight_grads))), (result, block_grad))
    start = tuple((jnp.zeros(present_item.shape, jnp.float32) for present_item in learned_tensors))
    running_totals, (results, block_grads) = lax.scan(step, start, (block_arguments, incoming, kept.reshape(blocks, block_rows), widths.reshape(blocks, block_rows)))
    leading_norm_gradient, leading_bias_gradient, query_weight_gradient, key_weight_gradient, value_weight_gradient, attention_output_gradient, middle_norm_gradient, middle_bias_gradient, up_weight_gradient, hidden_bias_gradient, down_weight_gradient, output_bias_gradient = running_totals
    layer_output = results.reshape(TOKENS, EMBED_WIDTH).astype(jnp.bfloat16)
    layer_input_gradient = block_grads.reshape(TOKENS, EMBED_WIDTH).astype(jnp.bfloat16)
    return (layer_output, layer_input_gradient, leading_norm_gradient, leading_bias_gradient, query_weight_gradient, key_weight_gradient, value_weight_gradient, attention_output_gradient, middle_norm_gradient, middle_bias_gradient, up_weight_gradient, hidden_bias_gradient, down_weight_gradient, output_bias_gradient)
```

```python
import jax
import jax.numpy as jnp
import numpy as np
from jax import lax
from jax.sharding import PartitionSpec as P

HEAD_DIM = 128
LEVELS = 4
GROUP = 8
EPSILON = 1e-05
NEGATIVE = -1e30
BF = jnp.bfloat16
F32 = jnp.float32


def dot(left, right, dims=((1,), (0,))):
    return lax.dot_general(left, right, (dims, ((), ())), preferred_element_type=F32)


def dot_t(left, right):
    return dot(left, right, ((1,), (1,)))


def t_dot(left, right):
    return dot(left, right, ((0,), (0,)))


def rope_tables(length):
    half = HEAD_DIM // 2
    rates = (10000.0 ** (-(np.arange(half, dtype=np.float64) * 2.0 / HEAD_DIM))).astype(np.float32)
    angles = np.arange(length, dtype=np.float32)[:, None] * rates[None, :]
    return np.cos(angles).astype(np.float32), np.sin(angles).astype(np.float32)


def rotate(values, cosine, sine):
    half = values.shape[-1] // 2
    first, second = values[..., :half], values[..., half:]
    cosine, sine = cosine[:, None, :], sine[:, None, :]
    return jnp.concatenate(
        [first * cosine - second * sine, second * cosine + first * sine], axis=-1
    )


def norm_stats(values):
    center = values - jnp.mean(values, axis=-1, keepdims=True)
    inverse = lax.rsqrt(jnp.mean(center * center, axis=-1, keepdims=True) + EPSILON)
    return center * inverse, inverse


def norm_back(incoming, gain, normal, inverse):
    scaled = incoming * gain
    part = inverse * (
        scaled
        - jnp.mean(scaled, axis=-1, keepdims=True)
        - normal * jnp.mean(scaled * normal, axis=-1, keepdims=True)
    )
    return part, jnp.sum(incoming * normal, axis=0), jnp.sum(incoming, axis=0)


def swap(value, bit):
    count = lax.axis_size("dp")
    return lax.ppermute(value, "dp", [(i, i ^ bit) for i in range(count)])


def hop(value, step, near, far):
    groups = lax.axis_size("dp") // GROUP
    pairs = [
        (z * GROUP + t, (z + step) * GROUP + t)
        for z in range(max(near, 0), min(far, groups))
        if 0 <= z + step < groups
        for t in range(GROUP)
    ]
    return lax.ppermute(value, "dp", pairs)


def sum_all(value):
    bit = 1
    while bit < lax.axis_size("dp"):
        value = value + swap(value, bit)
        bit *= 2
    return value


def plane_gather(own):
    half = own.shape[0] // 2
    slots = [own] + [None] * 7
    slots[2], slots[4], slots[1] = swap(own, 2), swap(own, 4), swap(own, 1)
    slots[6] = jnp.concatenate([swap(slots[2][:half], 4), swap(slots[4][half:], 2)], axis=0)
    for k in (2, 4, 6):
        slots[k + 1] = swap(slots[k], 1)
    return jnp.stack(slots)


def plane_scatter_sum(parts):
    half = parts.shape[1] // 2
    sent = swap(parts[1::2].astype(BF), 1)
    total = [parts[2 * j].astype(F32) + sent[j].astype(F32) for j in range(4)]
    corner = total[3].astype(BF)
    by_x, by_y = swap(corner[:half], 2), swap(corner[half:], 4)
    to_y = jnp.concatenate([total[2][:half] + by_x.astype(F32), total[2][half:]], axis=0)
    to_x = jnp.concatenate([total[1][:half], total[1][half:] + by_y.astype(F32)], axis=0)
    return total[0] + swap(to_x.astype(BF), 2).astype(F32) + swap(to_y.astype(BF), 4).astype(F32)


def plane_exchange(chunks):
    place = lax.axis_index("dp") % GROUP
    got = []
    for k in range(GROUP):
        chunk = lax.dynamic_index_in_dim(chunks, place ^ k, 0, keepdims=False)
        got.append(chunk if k == 0 else swap(chunk, k))
    return jnp.stack(got)


def in_order(slots):
    place = lax.axis_index("dp") % GROUP
    return jnp.take(slots, place ^ jnp.arange(GROUP), axis=0)


def line_gather(own):
    groups = lax.axis_size("dp") // GROUP
    z = lax.axis_index("dp") // GROUP
    up = down = own
    spare = jnp.zeros((groups + 1,) + own.shape, own.dtype)
    found = [(z, own)]
    for s in range(1, groups):
        up = hop(up, 1, s - 1, groups - 1)
        down = hop(down, -1, 1, groups - s + 1)
        found.append((jnp.where(z - s >= 0, z - s, groups), up))
        found.append((jnp.where(z + s < groups, z + s, groups), down))
    for slot, value in found:
        spare = lax.dynamic_update_index_in_dim(spare, value, slot, 0)
    return spare[:groups]


def line_scatter_sum(parts):
    groups = parts.shape[0]
    z = lax.axis_index("dp") // GROUP

    def part(offset):
        slot = jnp.clip(z + offset, 0, groups - 1)
        return lax.dynamic_index_in_dim(parts, slot, 0, keepdims=False).astype(F32)

    up = down = None
    for s in range(1, groups):
        far = groups - s
        up_send, down_send = part(far), part(-far)
        if up is not None:
            up_send, down_send = up_send + up.astype(F32), down_send + down.astype(F32)
        up = hop(up_send.astype(BF), 1, 0, s)
        down = hop(down_send.astype(BF), -1, groups - s, groups)
    return part(0) + up.astype(F32) + down.astype(F32)


def per_device(
    sequence_elements,
    result_sensitivity,
    mixer_gain,
    mixer_offset,
    question_matrix,
    lookup_matrix,
    content_matrix,
    mixer_projection_matrix,
    feedforward_gain,
    feedforward_offset,
    expand_matrix,
    inner_neuron_offset,
    contract_matrix,
    feedforward_result_offset,
    sequence_level_choice,
    servers_per_level,
    accepted_row_limit,
    server_selection,
):
    devices = lax.axis_size("dp")
    me = lax.axis_index("dp")
    groups = devices // GROUP
    z, place = me // GROUP, me % GROUP
    tokens, width = sequence_elements.shape
    heads = width // HEAD_DIM
    rows, feed = expand_matrix.shape
    cols = contract_matrix.shape[0]
    offset_len = feedforward_result_offset.shape[0]
    levels = jnp.arange(LEVELS)

    level = sequence_level_choice[0]
    choice = server_selection.reshape(-1)
    info = jnp.concatenate(
        [
            feedforward_result_offset.astype(F32),
            inner_neuron_offset.astype(F32),
            level.astype(F32)[None],
            jnp.min(choice).astype(F32)[None],
        ]
    )
    info = jnp.pad(info, (0, -info.shape[0] % 128))
    table = sum_all(jnp.where(jnp.arange(devices)[:, None] == me, info[None, :], 0.0))
    result_offset = table[:, :offset_len].reshape(-1)
    hidden_offsets = table[:, offset_len : offset_len + cols]
    all_levels = table[:, offset_len + cols].astype(jnp.int32)
    all_lowest = table[:, offset_len + cols + 1].astype(jnp.int32)

    size = jnp.sum(jnp.where(levels == level, servers_per_level, 0))
    limit = jnp.sum(jnp.where(levels == level, accepted_row_limit, 0))
    server = choice % size
    before = jnp.arange(tokens)[None, :] < jnp.arange(tokens)[:, None]
    local = jnp.sum((before & (server[None, :] == server[:, None])).astype(jnp.int32), axis=1)
    low = all_lowest[None, :]
    seen = (low + tokens - 1 - server[:, None] + size) // size - (low - 1 - server[:, None] + size) // size
    earlier = (jnp.arange(devices) < me) & (all_levels == level)
    arrival = local + jnp.sum(jnp.where(earlier[None, :], seen, 0), axis=1)
    kept = (arrival < limit).astype(F32)[:, None]

    expand_chunks = expand_matrix.reshape(rows, groups, GROUP, cols).transpose(2, 0, 1, 3)
    expand_plane = plane_exchange(expand_chunks.reshape(GROUP, rows, groups * cols))
    expand_plane = in_order(expand_plane).reshape(GROUP * rows, groups * cols)
    first_weight = line_gather(expand_plane).reshape(width, groups * cols)
    second_weight = line_gather(contract_matrix).reshape(groups * cols, width)

    gain_first = mixer_gain.astype(F32)
    gain_second = feedforward_gain.astype(F32)
    values_in = sequence_elements.astype(F32)
    normal_first, inverse_first = norm_stats(values_in)
    normed_first = (normal_first * gain_first + mixer_offset.astype(F32)).astype(BF)
    cosine, sine = rope_tables(tokens)
    scale = HEAD_DIM ** (-0.5)
    shape_heads = (tokens, heads, HEAD_DIM)
    query_rot = rotate(dot(normed_first, question_matrix).reshape(shape_heads), cosine, sine).astype(BF)
    key_rot = rotate(dot(normed_first, lookup_matrix).reshape(shape_heads), cosine, sine).astype(BF)
    value_rows = dot(normed_first, content_matrix).astype(BF).reshape(shape_heads)
    causal = jnp.arange(tokens)[:, None] >= jnp.arange(tokens)[None, :]
    scores = jnp.einsum("lhe,mhe->hlm", query_rot, key_rot, preferred_element_type=F32) * scale
    scores = jnp.where(causal, scores, NEGATIVE)
    weight = jnp.exp(scores - jnp.max(scores, axis=-1, keepdims=True))
    probs = weight / jnp.sum(weight, axis=-1, keepdims=True)
    probs_low = probs.astype(BF)
    context = jnp.einsum("hlm,mhe->lhe", probs_low, value_rows, preferred_element_type=F32)
    context = context.reshape(tokens, width).astype(BF)
    mixed = values_in + dot(context, mixer_projection_matrix)
    normal_second, inverse_second = norm_stats(mixed)
    normed_second = (normal_second * gain_second + feedforward_offset.astype(F32)).astype(BF)

    sensitivity = result_sensitivity.astype(F32)
    kept_sensitivity = (sensitivity * kept).astype(BF)
    group_grad = plane_gather(kept_sensitivity).reshape(GROUP * tokens, width)
    group_rows = plane_gather(normed_second).reshape(GROUP * tokens, width)
    slot_levels = jnp.take(all_levels, z * GROUP + (place ^ jnp.arange(GROUP)))
    starts = (jnp.arange(groups) * GROUP + place) * cols
    active_block = starts[None, :] < (feed // 8) * (1 << slot_levels[:, None])
    mask = jnp.broadcast_to(
        active_block[:, None, :, None], (GROUP, tokens, groups, cols)
    ).reshape(GROUP * tokens, groups * cols)
    hidden_offset = lax.dynamic_index_in_dim(
        hidden_offsets.reshape(groups, GROUP, cols), place, 1, keepdims=False
    ).reshape(-1)
    hidden = dot(group_rows, first_weight) + hidden_offset
    inner = 0.7978845608 * (hidden + 0.044715 * hidden * hidden * hidden)
    bent = jnp.tanh(inner)
    active = jnp.where(mask, 0.5 * hidden * (1.0 + bent), 0.0).astype(BF)
    slope = 0.5 * (1.0 + bent) + 0.5 * hidden * (1.0 - bent * bent) * 0.7978845608 * (
        1.0 + 3.0 * 0.044715 * hidden * hidden
    )
    active_grad = dot_t(group_grad, second_weight)
    hidden_grad = jnp.where(mask, active_grad * slope, 0.0).astype(BF)
    second_parts = dot_t(hidden_grad, first_weight).reshape(GROUP, tokens, width)
    second_grad = plane_scatter_sum(second_parts).astype(BF).astype(F32)
    branch_parts = dot(active, second_weight).reshape(GROUP, tokens, width)
    branch = (plane_scatter_sum(branch_parts) + result_offset).astype(BF).astype(F32)
    layer_output = (mixed + kept * branch).astype(BF)
    contract_part = t_dot(active, group_grad).reshape(groups, cols, width)
    share_contract = line_scatter_sum(contract_part)
    expand_part = t_dot(group_rows, hidden_grad).reshape(groups, GROUP * rows, groups * cols)
    expand_rows = line_scatter_sum(expand_part)
    hidden_sum = jnp.sum(hidden_grad.astype(F32), axis=0)

    def rows_home(summed):
        swapped = plane_exchange(summed.astype(BF).reshape(GROUP, rows, groups * cols))
        return in_order(swapped).astype(F32)

    share_expand = (
        rows_home(expand_rows)
        .reshape(GROUP, rows, groups, cols)
        .transpose(1, 2, 0, 3)
        .reshape(rows, feed)
    )

    mixed_part, midnorm_sum, midshift_sum = norm_back(second_grad, gain_second, normal_second, inverse_second)
    mixed_grad = sensitivity + mixed_part
    mixed_low = mixed_grad.astype(BF)
    context_grad = dot_t(mixed_low, mixer_projection_matrix).astype(BF).reshape(shape_heads)
    value_grad = jnp.einsum("hlm,lhe->mhe", probs_low, context_grad, preferred_element_type=F32)
    value_grad = value_grad.astype(BF).reshape(tokens, width)
    probs_grad = jnp.einsum("lhe,mhe->hlm", context_grad, value_rows, preferred_element_type=F32)
    scores_grad = (probs * (probs_grad - jnp.sum(probs_grad * probs, axis=-1, keepdims=True))).astype(BF)
    query_turned = jnp.einsum("hlm,mhe->lhe", scores_grad, key_rot, preferred_element_type=F32) * scale
    key_turned = jnp.einsum("hlm,lhe->mhe", scores_grad, query_rot, preferred_element_type=F32) * scale
    query_grad = rotate(query_turned, cosine, -sine).astype(BF).reshape(tokens, width)
    key_grad = rotate(key_turned, cosine, -sine).astype(BF).reshape(tokens, width)
    leading = dot_t(query_grad, question_matrix) + dot_t(key_grad, lookup_matrix) + dot_t(value_grad, content_matrix)
    input_part, leadnorm_sum, leadshift_sum = norm_back(leading, gain_first, normal_first, inverse_first)
    layer_input_gradient = (mixed_grad + input_part).astype(BF)

    share = width // GROUP
    group_first = plane_gather(normed_first).reshape(GROUP * tokens, width)
    group_context = plane_gather(context).reshape(GROUP * tokens, width)

    def split_columns(grad):
        chunks = grad.reshape(tokens, GROUP, share).transpose(1, 0, 2)
        return plane_exchange(chunks).reshape(GROUP * tokens, share)

    weight_parts = jnp.concatenate(
        [
            t_dot(group_context, split_columns(mixed_low)),
            t_dot(group_first, split_columns(value_grad)),
            t_dot(group_first, split_columns(key_grad)),
            t_dot(group_first, split_columns(query_grad)),
        ],
        axis=1,
    )
    weight_rows = line_scatter_sum(weight_parts.reshape(groups, GROUP * rows, 4 * share))
    swapped = plane_exchange(weight_rows.astype(BF).reshape(GROUP, rows, 4 * share))
    weight_home = (
        in_order(swapped)
        .astype(F32)
        .reshape(GROUP, rows, 4, share)
        .transpose(2, 1, 0, 3)
        .reshape(4, rows, width)
    )
    share_mixing, share_value, share_key, share_query = (weight_home[i] for i in range(4))

    hidden_spot = (jnp.arange(GROUP)[None, :, None] == place).astype(F32)
    hidden_full = (hidden_spot * hidden_sum.reshape(groups, 1, cols)).reshape(-1)
    result_sum = jnp.sum(kept_sensitivity.astype(F32), axis=0)
    vectors = sum_all(
        jnp.concatenate(
            [midnorm_sum, midshift_sum, leadnorm_sum, leadshift_sum, result_sum, hidden_full]
        ).reshape(-1, 128)
    ).reshape(-1)
    small = vectors[: 5 * width].reshape(5, devices, width // devices)
    small = lax.dynamic_index_in_dim(small, me, 1, keepdims=False)
    share_hidden = lax.dynamic_slice_in_dim(vectors, 5 * width + me * cols, cols)
    return (
        layer_output,
        layer_input_gradient,
        small[2],
        small[3],
        share_query,
        share_key,
        share_value,
        share_mixing,
        small[0],
        small[1],
        share_expand,
        share_hidden,
        share_contract,
        small[4],
    )


def solution(mesh):
    split, line, whole = P("dp", None), P("dp"), P()
    return jax.shard_map(
        per_device,
        mesh=mesh,
        in_specs=(split, split) + (whole,) * 8 + (split, line, split, line, line, whole, whole, split),
        out_specs=(split, split, line, line, split, split, split, split, line, line, split, line, split, line),
        check_vma=False,
    )
```

```python
import jax
import jax.numpy as jnp
import numpy as np
from jax import lax
from jax.sharding import PartitionSpec as P

HEAD_DIM = 128
LEVELS = 4
GROUP = 8
CHIPS = 4
EPSILON = 1e-05
NEGATIVE = -1e30
BF = jnp.bfloat16
F32 = jnp.float32


def dot(left, right, dims=((1,), (0,))):
    return lax.dot_general(left, right, (dims, ((), ())), preferred_element_type=F32)


def dot_t(left, right):
    return dot(left, right, ((1,), (1,)))


def t_dot(left, right):
    return dot(left, right, ((0,), (0,)))


def rope_tables(length):
    half = HEAD_DIM // 2
    rates = (10000.0 ** (-(np.arange(half, dtype=np.float64) * 2.0 / HEAD_DIM))).astype(np.float32)
    angles = np.arange(length, dtype=np.float32)[:, None] * rates[None, :]
    return np.cos(angles).astype(np.float32), np.sin(angles).astype(np.float32)


def rotate(values, cosine, sine):
    half = values.shape[-1] // 2
    first, second = values[..., :half], values[..., half:]
    cosine, sine = cosine[:, None, :], sine[:, None, :]
    return jnp.concatenate(
        [first * cosine - second * sine, second * cosine + first * sine], axis=-1
    )


def norm_stats(values):
    center = values - jnp.mean(values, axis=-1, keepdims=True)
    inverse = lax.rsqrt(jnp.mean(center * center, axis=-1, keepdims=True) + EPSILON)
    return center * inverse, inverse


def norm_back(incoming, gain, normal, inverse):
    scaled = incoming * gain
    part = inverse * (
        scaled
        - jnp.mean(scaled, axis=-1, keepdims=True)
        - normal * jnp.mean(scaled * normal, axis=-1, keepdims=True)
    )
    return part, jnp.sum(incoming * normal, axis=0), jnp.sum(incoming, axis=0)


def swap(value, bit):
    count = lax.axis_size("dp")
    return lax.ppermute(value, "dp", [(i, i ^ bit) for i in range(count)])


def hop(value, step, near, far):
    groups = lax.axis_size("dp") // GROUP
    pairs = [
        (z * GROUP + t, (z + step) * GROUP + t)
        for z in range(max(near, 0), min(far, groups))
        if 0 <= z + step < groups
        for t in range(GROUP)
    ]
    return lax.ppermute(value, "dp", pairs)


def lines():
    groups = lax.axis_size("dp") // GROUP
    return [[z * GROUP + t for z in range(groups)] for t in range(GROUP)]


def spread(own):
    return [own, swap(own, 2), swap(own, 4), swap(own, 6)]


def gather_sum(parts):
    total = parts[0].astype(F32)
    for j in (1, 2, 3):
        total = total + swap(parts[j].astype(BF), 2 * j).astype(F32)
    return total


def exchange(chunks):
    chip = lax.axis_index("dp") % GROUP // 2
    got = []
    for j in range(CHIPS):
        chunk = lax.dynamic_index_in_dim(chunks, chip ^ j, 0, keepdims=False)
        got.append(chunk if j == 0 else swap(chunk, 2 * j))
    return got


def in_order(slots):
    chip = lax.axis_index("dp") % GROUP // 2
    odd, high = chip % 2 == 1, chip // 2 == 1
    a, b, c, d = slots
    a, b, c, d = jnp.where(odd, b, a), jnp.where(odd, a, b), jnp.where(odd, d, c), jnp.where(odd, c, d)
    return [jnp.where(high, c, a), jnp.where(high, d, b), jnp.where(high, a, c), jnp.where(high, b, d)]


def line_gather(own):
    groups = lax.axis_size("dp") // GROUP
    z = lax.axis_index("dp") // GROUP
    ups, downs = [own], [own]
    for s in range(1, groups):
        ups.append(hop(ups[-1], 1, s - 1, groups - 1))
        downs.append(hop(downs[-1], -1, 1, groups - s + 1))
    return jnp.stack(
        [own] + [jnp.where(z + s < groups, downs[s], ups[groups - s]) for s in range(1, groups)]
    )


def line_scatter_sum(parts):
    groups = lax.axis_size("dp") // GROUP
    up = down = None
    for s in range(1, groups):
        up_send, down_send = parts[groups - s].astype(F32), parts[s].astype(F32)
        if up is not None:
            up_send, down_send = up_send + up.astype(F32), down_send + down.astype(F32)
        up = hop(up_send.astype(BF), 1, 0, s)
        down = hop(down_send.astype(BF), -1, groups - s, groups)
    return parts[0].astype(F32) + up.astype(F32) + down.astype(F32)


def turn(value, shift, axis, parts):
    step = value.shape[axis] // parts
    return lax.dynamic_slice_in_dim(
        jnp.concatenate([value, value], axis=axis), shift * step, value.shape[axis], axis
    )


def core_sum(mine, other):
    return mine + swap(other.astype(BF), 1).astype(F32)


def per_device(
    sequence_elements,
    result_sensitivity,
    mixer_gain,
    mixer_offset,
    question_matrix,
    lookup_matrix,
    content_matrix,
    mixer_projection_matrix,
    feedforward_gain,
    feedforward_offset,
    expand_matrix,
    inner_neuron_offset,
    contract_matrix,
    feedforward_result_offset,
    sequence_level_choice,
    servers_per_level,
    accepted_row_limit,
    server_selection,
):
    devices = lax.axis_size("dp")
    me = lax.axis_index("dp")
    groups = devices // GROUP
    z, chip, core = me // GROUP, me % GROUP // 2, me % 2
    tokens, width = sequence_elements.shape
    heads = width // HEAD_DIM
    rows, feed = expand_matrix.shape
    cols = contract_matrix.shape[0]
    offset_len = feedforward_result_offset.shape[0]
    levels = jnp.arange(LEVELS)

    level = sequence_level_choice[0]
    choice = server_selection.reshape(-1)
    info = jnp.concatenate(
        [
            feedforward_result_offset.astype(F32),
            inner_neuron_offset.astype(F32),
            level.astype(F32)[None],
            jnp.min(choice).astype(F32)[None],
        ]
    )
    info = jnp.pad(info, (0, -info.shape[0] % 128))
    table = jnp.broadcast_to(info, (devices, 1) + info.shape)
    table = lax.all_to_all(table, "dp", 0, 0, tiled=True).reshape(devices, -1)
    result_offset = table[:, :offset_len].reshape(-1)
    hidden_offsets = table[:, offset_len : offset_len + cols]
    all_levels = table[:, offset_len + cols].astype(jnp.int32)
    all_lowest = table[:, offset_len + cols + 1].astype(jnp.int32)

    size = jnp.sum(jnp.where(levels == level, servers_per_level, 0))
    limit = jnp.sum(jnp.where(levels == level, accepted_row_limit, 0))
    server = choice % size
    before = jnp.arange(tokens)[None, :] < jnp.arange(tokens)[:, None]
    local = jnp.sum((before & (server[None, :] == server[:, None])).astype(jnp.int32), axis=1)
    low = all_lowest[None, :]
    seen = (low + tokens - 1 - server[:, None] + size) // size - (low - 1 - server[:, None] + size) // size
    earlier = (jnp.arange(devices) < me) & (all_levels == level)
    arrival = local + jnp.sum(jnp.where(earlier[None, :], seen, 0), axis=1)
    kept = (arrival < limit).astype(F32)[:, None]

    block = 2 * cols
    units = groups * block
    expand_chunks = expand_matrix.reshape(rows, groups, CHIPS, block).transpose(2, 0, 1, 3)
    expand_plane = jnp.concatenate(in_order(exchange(expand_chunks.reshape(CHIPS, rows, units))), axis=0)
    expand_mine = line_gather(expand_plane).reshape(groups, CHIPS, rows, units)
    expand_other = swap(expand_mine, 1)
    contract_mine = lax.all_gather(contract_matrix, "dp", axis_index_groups=lines())
    contract_other = swap(contract_mine, 1)
    first_weight = jnp.where(
        core == 0,
        jnp.stack([expand_mine, expand_other], axis=2),
        jnp.stack([expand_other, expand_mine], axis=2),
    ).reshape(width, units)
    second_weight = jnp.where(
        core == 0,
        jnp.stack([contract_mine, contract_other], axis=1),
        jnp.stack([contract_other, contract_mine], axis=1),
    ).reshape(units, width)

    gain_first = mixer_gain.astype(F32)
    gain_second = feedforward_gain.astype(F32)
    values_in = sequence_elements.astype(F32)
    normal_first, inverse_first = norm_stats(values_in)
    normed_first = (normal_first * gain_first + mixer_offset.astype(F32)).astype(BF)
    cosine, sine = rope_tables(tokens)
    scale = HEAD_DIM ** (-0.5)
    shape_heads = (tokens, heads, HEAD_DIM)
    query_rot = rotate(dot(normed_first, question_matrix).reshape(shape_heads), cosine, sine).astype(BF)
    key_rot = rotate(dot(normed_first, lookup_matrix).reshape(shape_heads), cosine, sine).astype(BF)
    value_rows = dot(normed_first, content_matrix).astype(BF).reshape(shape_heads)
    causal = jnp.arange(tokens)[:, None] >= jnp.arange(tokens)[None, :]
    scores = jnp.einsum("lhe,mhe->hlm", query_rot, key_rot, preferred_element_type=F32) * scale
    scores = jnp.where(causal, scores, NEGATIVE)
    weight = jnp.exp(scores - jnp.max(scores, axis=-1, keepdims=True))
    probs = weight / jnp.sum(weight, axis=-1, keepdims=True)
    probs_low = probs.astype(BF)
    context = jnp.einsum("hlm,mhe->lhe", probs_low, value_rows, preferred_element_type=F32)
    context = context.reshape(tokens, width).astype(BF)
    mixed = values_in + dot(context, mixer_projection_matrix)
    normal_second, inverse_second = norm_stats(mixed)
    normed_second = (normal_second * gain_second + feedforward_offset.astype(F32)).astype(BF)

    sensitivity = result_sensitivity.astype(F32)
    kept_sensitivity = (sensitivity * kept).astype(BF)
    group_grad = jnp.concatenate(spread(kept_sensitivity), axis=0)
    group_rows = jnp.concatenate(spread(turn(normed_second, z, 1, groups)), axis=0)
    slot_levels = jnp.take(all_levels, me ^ (2 * jnp.arange(CHIPS)))
    starts = (jnp.arange(groups) * CHIPS + chip) * block
    active_block = starts[None, :] < (feed // 8) * (1 << slot_levels[:, None])
    mask = jnp.broadcast_to(
        active_block[:, None, :, None], (CHIPS, tokens, groups, block)
    ).reshape(CHIPS * tokens, units)
    hidden_offset = lax.dynamic_index_in_dim(
        hidden_offsets.reshape(groups, CHIPS, block), chip, 1, keepdims=False
    ).reshape(-1)
    hidden = dot(group_rows, first_weight) + hidden_offset
    inner = 0.7978845608 * (hidden + 0.044715 * hidden * hidden * hidden)
    bent = jnp.tanh(inner)
    active = jnp.where(mask, 0.5 * hidden * (1.0 + bent), 0.0).astype(BF)
    slope = 0.5 * (1.0 + bent) + 0.5 * hidden * (1.0 - bent * bent) * 0.7978845608 * (
        1.0 + 3.0 * 0.044715 * hidden * hidden
    )
    active_grad = dot_t(group_grad, second_weight)
    hidden_grad = jnp.where(mask, active_grad * slope, 0.0).astype(BF)
    second_parts = dot_t(hidden_grad, first_weight).reshape(CHIPS, tokens, width)
    second_grad = turn(gather_sum(second_parts), (groups - z) % groups, 1, groups)
    second_grad = second_grad.astype(BF).astype(F32)
    branch_parts = dot(active, second_weight).reshape(CHIPS, tokens, width)
    branch = (gather_sum(branch_parts) + result_offset).astype(BF).astype(F32)
    layer_output = (mixed + kept * branch).astype(BF)
    contract_part = t_dot(active, group_grad).reshape(groups, 2, cols, width)
    contract_sum = core_sum(
        lax.dynamic_index_in_dim(contract_part, core, 1, keepdims=False),
        lax.dynamic_index_in_dim(contract_part, 1 - core, 1, keepdims=False),
    ).astype(BF)
    share_contract = lax.psum_scatter(
        contract_sum, "dp", scatter_dimension=0, axis_index_groups=lines()
    ).astype(F32)

    def rows_home(part):
        part = part.reshape(groups, CHIPS, 2, rows, part.shape[1])
        both = core_sum(
            lax.dynamic_index_in_dim(part, core, 2, keepdims=False),
            lax.dynamic_index_in_dim(part, 1 - core, 2, keepdims=False),
        )
        return in_order(exchange(line_scatter_sum(both).astype(BF)))

    expand_home = rows_home(t_dot(group_rows, hidden_grad))
    share_expand = (
        jnp.stack([piece.reshape(rows, groups, block) for piece in expand_home], axis=2)
        .astype(F32)
        .reshape(rows, feed)
    )
    hidden_sum = jnp.sum(hidden_grad.astype(F32), axis=0)

    mixed_part, midnorm_sum, midshift_sum = norm_back(second_grad, gain_second, normal_second, inverse_second)
    mixed_grad = sensitivity + mixed_part
    mixed_low = mixed_grad.astype(BF)
    context_grad = dot_t(mixed_low, mixer_projection_matrix).astype(BF).reshape(shape_heads)
    value_grad = jnp.einsum("hlm,lhe->mhe", probs_low, context_grad, preferred_element_type=F32)
    value_grad = value_grad.astype(BF).reshape(tokens, width)
    probs_grad = jnp.einsum("lhe,mhe->hlm", context_grad, value_rows, preferred_element_type=F32)
    scores_grad = (probs * (probs_grad - jnp.sum(probs_grad * probs, axis=-1, keepdims=True))).astype(BF)
    query_turned = jnp.einsum("hlm,mhe->lhe", scores_grad, key_rot, preferred_element_type=F32) * scale
    key_turned = jnp.einsum("hlm,lhe->mhe", scores_grad, query_rot, preferred_element_type=F32) * scale
    query_grad = rotate(query_turned, cosine, -sine).astype(BF).reshape(tokens, width)
    key_grad = rotate(key_turned, cosine, -sine).astype(BF).reshape(tokens, width)
    leading = dot_t(query_grad, question_matrix) + dot_t(key_grad, lookup_matrix) + dot_t(value_grad, content_matrix)
    input_part, leadnorm_sum, leadshift_sum = norm_back(leading, gain_first, normal_first, inverse_first)
    layer_input_gradient = (mixed_grad + input_part).astype(BF)

    share = width // CHIPS
    group_first = jnp.concatenate(spread(turn(normed_first, z, 1, groups)), axis=0)
    group_context = jnp.concatenate(spread(turn(context, z, 1, groups)), axis=0)

    def split_columns(*grads):
        chunks = jnp.concatenate([grad.reshape(tokens, CHIPS, share) for grad in grads], axis=2)
        return jnp.concatenate(exchange(chunks.transpose(1, 0, 2)), axis=0)

    first_pair = split_columns(mixed_low, value_grad)
    second_pair = split_columns(key_grad, query_grad)
    early = rows_home(
        jnp.concatenate(
            [t_dot(group_context, first_pair[:, :share]), t_dot(group_first, first_pair[:, share:])], axis=1
        )
    )
    late = rows_home(t_dot(group_first, second_pair))

    def join(pieces, low):
        return jnp.concatenate([piece[:, low : low + share] for piece in pieces], axis=1).astype(F32)

    share_mixing, share_value = join(early, 0), join(early, share)
    share_key, share_query = join(late, 0), join(late, share)

    hidden_spot = (jnp.arange(CHIPS)[None, :, None] == chip).astype(F32)
    hidden_full = hidden_spot * hidden_sum.reshape(groups, 1, block)
    result_sum = jnp.sum(kept_sensitivity.astype(F32), axis=0)
    vectors = [midnorm_sum, midshift_sum, leadnorm_sum, leadshift_sum, result_sum, hidden_full]
    vectors = jnp.concatenate([vector.reshape(devices, -1) for vector in vectors], axis=1)
    vectors = jnp.pad(vectors, ((0, 0), (0, -vectors.shape[1] % 128)))
    vectors = lax.all_to_all(vectors[:, None, :], "dp", 0, 0, tiled=True)
    vectors = jnp.sum(vectors, axis=(0, 1))
    small = [vectors[i * offset_len : (i + 1) * offset_len] for i in range(5)]
    share_hidden = vectors[5 * offset_len : 5 * offset_len + cols]
    return (
        layer_output,
        layer_input_gradient,
        small[2],
        small[3],
        share_query,
        share_key,
        share_value,
        share_mixing,
        small[0],
        small[1],
        share_expand,
        share_hidden,
        share_contract,
        small[4],
    )


def solution(mesh):
    split, line, whole = P("dp", None), P("dp"), P()
    return jax.shard_map(
        per_device,
        mesh=mesh,
        in_specs=(split, split) + (whole,) * 8 + (split, line, split, line, line, whole, whole, split),
        out_specs=(split, split, line, line, split, split, split, split, line, line, split, line, split, line),
        check_vma=False,
    )
```

```python
import jax
import jax.numpy as jnp
import numpy as np
from jax import lax
from jax.experimental import pallas as pl
from jax.experimental.pallas import tpu as pltpu
from jax.sharding import PartitionSpec as P

HEAD_DIM = 128
LEVELS = 4
GROUP = 8
CHIPS = 4
EPSILON = 1e-05
NEGATIVE = -1e30
BF = jnp.bfloat16
F32 = jnp.float32
WIDE = 512
VMEM_BYTES = 56 * 1024 * 1024


def dot(left, right, dims=((1,), (0,))):
    return lax.dot_general(left, right, (dims, ((), ())), preferred_element_type=F32)


def dot_t(left, right):
    return dot(left, right, ((1,), (1,)))


def t_dot(left, right):
    return dot(left, right, ((0,), (0,)))


def rope_tables(length):
    half = HEAD_DIM // 2
    rates = (10000.0 ** (-(np.arange(half, dtype=np.float64) * 2.0 / HEAD_DIM))).astype(np.float32)
    angles = np.arange(length, dtype=np.float32)[:, None] * rates[None, :]
    cosine, sine = np.cos(angles).astype(np.float32), np.sin(angles).astype(np.float32)
    return np.concatenate([cosine, cosine], axis=1), np.concatenate([-sine, sine], axis=1)


def norm_stats(values):
    center = values - jnp.mean(values, axis=-1, keepdims=True)
    inverse = lax.rsqrt(jnp.mean(center * center, axis=-1, keepdims=True) + EPSILON)
    return center * inverse, inverse


def norm_back(incoming, gain, normal, inverse):
    scaled = incoming * gain
    part = inverse * (
        scaled
        - jnp.mean(scaled, axis=-1, keepdims=True)
        - normal * jnp.mean(scaled * normal, axis=-1, keepdims=True)
    )
    return part, jnp.sum(incoming * normal, axis=0, keepdims=True), jnp.sum(incoming, axis=0, keepdims=True)


def swap(value, bit):
    count = lax.axis_size("dp")
    return lax.ppermute(value, "dp", [(i, i ^ bit) for i in range(count)])


def hop(value, step, near, far):
    groups = lax.axis_size("dp") // GROUP
    pairs = [
        (z * GROUP + t, (z + step) * GROUP + t)
        for z in range(max(near, 0), min(far, groups))
        if 0 <= z + step < groups
        for t in range(GROUP)
    ]
    return lax.ppermute(value, "dp", pairs)


def sum_all(value):
    bit = 1
    while bit < lax.axis_size("dp"):
        value = value + swap(value, bit)
        bit *= 2
    return value


def lines():
    groups = lax.axis_size("dp") // GROUP
    return [[z * GROUP + t for z in range(groups)] for t in range(GROUP)]


def spread(own):
    return [own, swap(own, 2), swap(own, 4), swap(own, 6)]


def gather_sum(parts):
    total = parts[0].astype(F32)
    for j in (1, 2, 3):
        total = total + swap(parts[j].astype(BF), 2 * j).astype(F32)
    return total


def exchange(chunks):
    chip = lax.axis_index("dp") % GROUP // 2
    got = []
    for j in range(CHIPS):
        chunk = lax.dynamic_index_in_dim(chunks, chip ^ j, 0, keepdims=False)
        got.append(chunk if j == 0 else swap(chunk, 2 * j))
    return got


def in_order(slots):
    chip = lax.axis_index("dp") % GROUP // 2
    odd, high = chip % 2 == 1, chip // 2 == 1
    a, b, c, d = slots
    a, b, c, d = jnp.where(odd, b, a), jnp.where(odd, a, b), jnp.where(odd, d, c), jnp.where(odd, c, d)
    return [jnp.where(high, c, a), jnp.where(high, d, b), jnp.where(high, a, c), jnp.where(high, b, d)]


def line_step(sides, own, s):
    groups = lax.axis_size("dp") // GROUP
    up, down = sides if s > 1 else (own, own)
    return hop(up, 1, s - 1, groups - 1), hop(down, -1, 1, groups - s + 1)


def line_stack(own, steps):
    groups = lax.axis_size("dp") // GROUP
    z = lax.axis_index("dp") // GROUP
    return jnp.stack(
        [own]
        + [jnp.where(z + s < groups, steps[s - 1][1], steps[groups - s - 1][0]) for s in range(1, groups)]
    )


def line_sum(parts):
    groups = lax.axis_size("dp") // GROUP
    total = parts[0].astype(F32)
    for s in range(1, groups):
        pairs = [
            (z * GROUP + t, (z + s) % groups * GROUP + t) for z in range(groups) for t in range(GROUP)
        ]
        total = total + lax.ppermute(parts[s].astype(BF), "dp", pairs).astype(F32)
    return total


def after(value, *others):
    return lax.optimization_barrier((value,) + others)[0]


def turn(value, shift, axis, parts):
    step = value.shape[axis] // parts
    return lax.dynamic_slice_in_dim(
        jnp.concatenate([value, value], axis=axis), shift * step, value.shape[axis], axis
    )


def core_sum(mine, other):
    return mine + swap(other.astype(BF), 1).astype(F32)


ANY = pl.BlockSpec(memory_space=pl.ANY)
VMEM = pl.BlockSpec(memory_space=pltpu.VMEM)
SMEM = pl.BlockSpec(memory_space=pltpu.SMEM)


def call(kernel, outs, args, places, scratch=(), flops=0, moved=0):
    return pl.pallas_call(
        kernel,
        out_shape=tuple(jax.ShapeDtypeStruct(shape, kind) for shape, kind in outs),
        in_specs=list(places),
        out_specs=tuple(VMEM for _ in outs),
        scratch_shapes=list(scratch),
        compiler_params=pltpu.CompilerParams(vmem_limit_bytes=VMEM_BYTES),
        cost_estimate=pl.CostEstimate(flops=flops, bytes_accessed=moved, transcendentals=0),
    )(*args)


def fetch(source, target, sem):
    copy = pltpu.make_async_copy(source, target, sem)
    copy.start()
    return copy


def turned(values, cosine, sine):
    return values * cosine + pltpu.roll(values, HEAD_DIM // 2, 1) * sine


def project_kernel(
    x_ref, gain_ref, shift_ref, cos_ref, sin_ref, wq, wk, wv, normed_ref, q_ref, k_ref, v_ref, w_ref, sems
):
    copies = [fetch(w, w_ref.at[i], sems.at[i]) for i, w in enumerate((wq, wk, wv))]
    normal, _ = norm_stats(x_ref[...].astype(F32))
    normed_ref[...] = (normal * gain_ref[...] + shift_ref[...]).astype(BF)
    cosine, sine = cos_ref[...], sin_ref[...]
    for i, out in enumerate((q_ref, k_ref, v_ref)):
        copies[i].wait()
        for low in range(0, out.shape[1], WIDE):
            raw = dot(normed_ref[...], w_ref[i, :, low : low + WIDE])
            for h in range(0, WIDE, HEAD_DIM):
                head = raw[:, h : h + HEAD_DIM]
                if i < 2:
                    head = turned(head, cosine, sine)
                out[:, low + h : low + h + HEAD_DIM] = head.astype(BF)


def attend_kernel(
    q_ref, k_ref, v_ref, x_ref, gain_ref, shift_ref, wo, context_ref, mixed_ref, normed_ref, probs_ref, w_ref, sem
):
    copy = fetch(wo, w_ref, sem)
    tokens, width = q_ref.shape
    row = lax.broadcasted_iota(jnp.int32, (tokens, tokens), 0)
    causal = row >= lax.broadcasted_iota(jnp.int32, (tokens, tokens), 1)
    for h in range(width // HEAD_DIM):
        span = slice(h * HEAD_DIM, (h + 1) * HEAD_DIM)
        scores = dot_t(q_ref[:, span], k_ref[:, span]) * HEAD_DIM**-0.5
        scores = jnp.where(causal, scores, NEGATIVE)
        weight = jnp.exp(scores - jnp.max(scores, axis=-1, keepdims=True))
        probs = weight / jnp.sum(weight, axis=-1, keepdims=True)
        probs_ref[h] = probs
        context_ref[:, span] = dot(probs.astype(BF), v_ref[:, span]).astype(BF)
    copy.wait()
    for low in range(0, width, WIDE):
        span = slice(low, low + WIDE)
        mixed_ref[:, span] = x_ref[:, span].astype(F32) + dot(context_ref[...], w_ref[:, span])
    normal, _ = norm_stats(mixed_ref[...])
    normed_ref[...] = (normal * gain_ref[...] + shift_ref[...]).astype(BF)


def hidden_kernel(*refs):
    xs, gs = refs[:CHIPS], refs[CHIPS : 2 * CHIPS]
    w_ref, bias_ref, mask_ref, active_ref, slope_ref, down_ref = refs[2 * CHIPS :]
    x = jnp.concatenate([x[...] for x in xs], axis=0)
    tokens = xs[0].shape[0]
    for low in range(0, w_ref.shape[1], WIDE):
        span = slice(low, low + WIDE)
        hidden = dot(x, w_ref[:, span]) + bias_ref[:, span]
        square = hidden * hidden
        bent = jnp.tanh(0.7978845608 * hidden * (1.0 + 0.044715 * square))
        slope = 0.5 * (1.0 + bent) + (0.5 * 0.7978845608) * hidden * (1.0 - bent * bent) * (
            1.0 + 3.0 * 0.044715 * square
        )
        value = 0.5 * hidden * (1.0 + bent)
        for j in range(CHIPS):
            part = slice(j * tokens, (j + 1) * tokens)
            keep = mask_ref[j : j + 1, span]
            active_ref[part, span] = (value[part] * keep).astype(BF)
            slope_ref[part, span] = slope[part] * keep
    grad = jnp.concatenate([g[...] for g in gs], axis=0)
    for low in range(0, w_ref.shape[1], WIDE):
        down_ref[low : low + WIDE, :] = t_dot(active_ref[:, low : low + WIDE], grad).astype(BF)


def reverse_kernel(*refs):
    gs = refs[:CHIPS]
    w1_ref, w2_ref, slope_ref, grad_ref, sum_ref, own_ref = refs[CHIPS : CHIPS + 6]
    sent = refs[CHIPS + 6 :]
    tokens = gs[0].shape[0]
    grad = jnp.concatenate([g[...] for g in gs], axis=0)
    for low in range(0, w2_ref.shape[0], WIDE):
        span = slice(low, low + WIDE)
        value = (dot_t(grad, w2_ref[span, :]) * slope_ref[:, span]).astype(BF)
        grad_ref[:, span] = value
        sum_ref[:, span] = jnp.sum(value.astype(F32), axis=0, keepdims=True)
    for low in range(0, w1_ref.shape[0], WIDE):
        span = slice(low, low + WIDE)
        part = dot_t(grad_ref[...], w1_ref[span, :])
        own_ref[:, span] = part[:tokens]
        for j in range(1, CHIPS):
            sent[j - 1][:, span] = part[j * tokens : (j + 1) * tokens].astype(BF)


def finish_kernel(*refs):
    xs = refs[:CHIPS]
    active_ref, grad_ref, w2_ref, up_ref, own_ref = refs[CHIPS : CHIPS + 5]
    sent = refs[CHIPS + 5 :]
    tokens = xs[0].shape[0]
    for low in range(0, w2_ref.shape[1], WIDE):
        span = slice(low, low + WIDE)
        part = dot(active_ref[...], w2_ref[:, span])
        own_ref[:, span] = part[:tokens]
        for j in range(1, CHIPS):
            sent[j - 1][:, span] = part[j * tokens : (j + 1) * tokens].astype(BF)
    for low in range(0, xs[0].shape[1], WIDE):
        x = jnp.concatenate([x[:, low : low + WIDE] for x in xs], axis=0)
        up_ref[low : low + WIDE, :] = t_dot(x, grad_ref[...]).astype(BF)


def mixed_kernel(
    second_ref, mixed_ref, sens_ref, gain_ref, wo, v_ref, probs_ref,
    mixgrad_ref, low_ref, cgrad_ref, vgrad_ref, norm_ref, shift_ref, w_ref, sem
):
    copy = fetch(wo, w_ref, sem)
    normal, inverse = norm_stats(mixed_ref[...])
    part, norm_sum, shift_sum = norm_back(second_ref[...].astype(F32), gain_ref[...], normal, inverse)
    norm_ref[...], shift_ref[...] = norm_sum, shift_sum
    mixed_grad = sens_ref[...].astype(F32) + part
    mixgrad_ref[...] = mixed_grad
    low_ref[...] = mixed_grad.astype(BF)
    copy.wait()
    width = v_ref.shape[1]
    for low in range(0, width, WIDE):
        cgrad_ref[:, low : low + WIDE] = dot_t(low_ref[...], w_ref[low : low + WIDE, :]).astype(BF)
    for h in range(width // HEAD_DIM):
        span = slice(h * HEAD_DIM, (h + 1) * HEAD_DIM)
        vgrad_ref[:, span] = t_dot(probs_ref[h].astype(BF), cgrad_ref[:, span]).astype(BF)


def score_kernel(cgrad_ref, q_ref, k_ref, v_ref, probs_ref, cos_ref, sin_ref, qgrad_ref, kgrad_ref):
    cosine, sine = cos_ref[...], -sin_ref[...]
    for h in range(v_ref.shape[1] // HEAD_DIM):
        span = slice(h * HEAD_DIM, (h + 1) * HEAD_DIM)
        probs = probs_ref[h]
        probs_grad = dot_t(cgrad_ref[:, span], v_ref[:, span])
        inner = jnp.sum(probs_grad * probs, axis=-1, keepdims=True)
        scores_grad = (probs * (probs_grad - inner)).astype(BF)
        scale = HEAD_DIM**-0.5
        qgrad_ref[:, span] = turned(dot(scores_grad, k_ref[:, span]) * scale, cosine, sine).astype(BF)
        kgrad_ref[:, span] = turned(t_dot(scores_grad, q_ref[:, span]) * scale, cosine, sine).astype(BF)


def leading_kernel(
    qgrad_ref, kgrad_ref, vgrad_ref, x_ref, gain_ref, mixgrad_ref, wq, wk, wv,
    out_ref, norm_ref, shift_ref, w_ref, lead_ref, sems
):
    copies = [fetch(w, w_ref.at[i], sems.at[i]) for i, w in enumerate((wq, wk, wv))]
    normal, inverse = norm_stats(x_ref[...].astype(F32))
    for copy in copies:
        copy.wait()
    for low in range(0, x_ref.shape[1], WIDE):
        span = slice(low, low + WIDE)
        lead_ref[:, span] = (
            dot_t(qgrad_ref[...], w_ref[0, span, :])
            + dot_t(kgrad_ref[...], w_ref[1, span, :])
            + dot_t(vgrad_ref[...], w_ref[2, span, :])
        )
    part, norm_sum, shift_sum = norm_back(lead_ref[...], gain_ref[...], normal, inverse)
    norm_ref[...], shift_ref[...] = norm_sum, shift_sum
    out_ref[...] = (mixgrad_ref[...] + part).astype(BF)


def outer_kernel(*refs):
    kinds = (len(refs) - 1) // CHIPS - 1
    rights, out_ref = refs[kinds * CHIPS : -1], refs[-1]
    right = jnp.concatenate([r[...] for r in rights], axis=0)
    share = right.shape[1] // kinds
    for i in range(kinds):
        lefts = refs[i * CHIPS : (i + 1) * CHIPS]
        for low in range(0, lefts[0].shape[1], WIDE):
            left = jnp.concatenate([l[:, low : low + WIDE] for l in lefts], axis=0)
            out_ref[low : low + WIDE, i * share : (i + 1) * share] = t_dot(
                left, right[:, i * share : (i + 1) * share]
            ).astype(BF)


def per_device(
    sequence_elements,
    result_sensitivity,
    mixer_gain,
    mixer_offset,
    question_matrix,
    lookup_matrix,
    content_matrix,
    mixer_projection_matrix,
    feedforward_gain,
    feedforward_offset,
    expand_matrix,
    inner_neuron_offset,
    contract_matrix,
    feedforward_result_offset,
    sequence_level_choice,
    servers_per_level,
    accepted_row_limit,
    server_selection,
):
    devices = lax.axis_size("dp")
    me = lax.axis_index("dp")
    groups = devices // GROUP
    z, chip, core = me // GROUP, me % GROUP // 2, me % 2
    tokens, width = sequence_elements.shape
    heads = width // HEAD_DIM
    rows, feed = expand_matrix.shape
    cols = contract_matrix.shape[0]
    offset_len = feedforward_result_offset.shape[0]
    levels = jnp.arange(LEVELS)
    block = 2 * cols
    units = groups * block
    gain_first, shift_first, gain_second, shift_second = (
        v.astype(F32)[None, :] for v in (mixer_gain, mixer_offset, feedforward_gain, feedforward_offset)
    )
    cosine, sine = (jnp.asarray(t) for t in rope_tables(tokens))
    flat, wide = (tokens, width), (1, width)
    square = (width, width)
    all_rows = (CHIPS * tokens, units)
    weight_space = pltpu.VMEM(square, BF)
    triple_space = pltpu.VMEM((3,) + square, BF)
    dma, dmas = pltpu.SemaphoreType.DMA, pltpu.SemaphoreType.DMA((3,))
    flops = 2 * tokens * width * width
    moved = 2 * width * width

    contract_full = lax.all_gather(contract_matrix, "dp", axis_index_groups=lines())
    expand_chunks = expand_matrix.reshape(rows, groups, CHIPS, block).transpose(2, 0, 1, 3)
    expand_pieces = exchange(expand_chunks.reshape(CHIPS, rows, units))
    level = sequence_level_choice[0]
    choice = server_selection.reshape(-1)
    info = jnp.concatenate(
        [
            feedforward_result_offset.astype(F32),
            inner_neuron_offset.astype(F32),
            level.astype(F32)[None],
            jnp.min(choice).astype(F32)[None],
        ]
    )
    info = jnp.pad(info, (0, -info.shape[0] % 128))
    table = jnp.where(jnp.arange(devices)[:, None] == me, info[None, :], 0.0)
    normed_first, query_rot, key_rot, value_rows = call(
        project_kernel,
        [(flat, BF)] * 4,
        (sequence_elements, gain_first, shift_first, cosine, sine, question_matrix, lookup_matrix, content_matrix),
        [VMEM] * 5 + [ANY] * 3,
        [triple_space, dmas],
        3 * flops,
        3 * moved,
    )
    query_rot, key_rot, value_rows, expand_pieces = lax.optimization_barrier(
        (query_rot, key_rot, value_rows, expand_pieces)
    )

    expand_plane = jnp.concatenate(in_order(expand_pieces), axis=0)
    expand_steps = [line_step(None, expand_plane, 1)]
    context, mixed, normed_second, probs = call(
        attend_kernel,
        [(flat, BF), (flat, F32), (flat, BF), ((heads, tokens, tokens), F32)],
        (query_rot, key_rot, value_rows, sequence_elements, gain_second, shift_second, mixer_projection_matrix),
        [VMEM] * 6 + [ANY],
        [weight_space, dma],
        2 * flops,
        moved,
    )
    normed_second, expand_steps[0] = lax.optimization_barrier((normed_second, expand_steps[0]))

    row_slots = spread(turn(normed_second, z, 1, groups))
    for s in range(2, groups):
        expand_steps.append(line_step(expand_steps[-1], expand_plane, s))
    table = sum_all(table)
    result_offset = table[:, :offset_len].reshape(-1)
    hidden_offsets = table[:, offset_len : offset_len + cols]
    all_levels = table[:, offset_len + cols].astype(jnp.int32)
    all_lowest = table[:, offset_len + cols + 1].astype(jnp.int32)
    size = jnp.sum(jnp.where(levels == level, servers_per_level, 0))
    limit = jnp.sum(jnp.where(levels == level, accepted_row_limit, 0))
    server = choice % size
    before = jnp.arange(tokens)[None, :] < jnp.arange(tokens)[:, None]
    local = jnp.sum((before & (server[None, :] == server[:, None])).astype(jnp.int32), axis=1)
    low = all_lowest[None, :]
    seen = (low + tokens - 1 - server[:, None] + size) // size - (low - 1 - server[:, None] + size) // size
    earlier = (jnp.arange(devices) < me) & (all_levels == level)
    arrival = local + jnp.sum(jnp.where(earlier[None, :], seen, 0), axis=1)
    kept = (arrival < limit).astype(F32)[:, None]
    kept_sensitivity = (result_sensitivity.astype(F32) * kept).astype(BF)
    grad_slots = spread(kept_sensitivity)
    slot_levels = jnp.take(all_levels, me ^ (2 * jnp.arange(CHIPS)))
    starts = (jnp.arange(groups) * CHIPS + chip) * block
    active_block = starts[None, :] < (feed // 8) * (1 << slot_levels[:, None])
    mask = jnp.repeat(active_block.astype(F32), block, axis=1)
    hidden_offset = lax.dynamic_index_in_dim(
        hidden_offsets.reshape(groups, CHIPS, block), chip, 1, keepdims=False
    ).reshape(1, -1)
    expand_mine = line_stack(expand_plane, expand_steps).reshape(groups, CHIPS, rows, units)
    expand_other = swap(expand_mine, 1)
    first_weight = jnp.where(
        core == 0,
        jnp.stack([expand_mine, expand_other], axis=2),
        jnp.stack([expand_other, expand_mine], axis=2),
    ).reshape(width, units)

    active, slope, down_part = call(
        hidden_kernel,
        [(all_rows, BF), (all_rows, F32), ((units, width), BF)],
        (*row_slots, *grad_slots, first_weight, hidden_offset, mask),
        [VMEM] * (2 * CHIPS + 3),
        (),
        8 * flops,
        6 * moved,
    )
    contract_other = swap(contract_full, 1)
    second_weight = jnp.where(
        core == 0,
        jnp.stack([contract_full, contract_other], axis=1),
        jnp.stack([contract_other, contract_full], axis=1),
    ).reshape(units, width)
    down_part = down_part.reshape(groups, 2, cols, width)
    down_other = swap(lax.dynamic_index_in_dim(down_part, 1 - core, 1, keepdims=False), 1)
    first_slots = spread(after(turn(normed_first, z, 1, groups), row_slots))
    hidden_grad, hidden_sum, second_own, *second_sent = call(
        reverse_kernel,
        [(all_rows, BF), ((1, units), F32), (flat, F32)] + [(flat, BF)] * 3,
        (*grad_slots, first_weight, second_weight, slope),
        [VMEM] * (CHIPS + 3),
        (),
        8 * flops,
        6 * moved,
    )
    second_got = [swap(second_sent[j - 1], 2 * j) for j in range(1, CHIPS)]
    contract_sum = (
        lax.dynamic_index_in_dim(down_part, core, 1, keepdims=False).astype(F32) + down_other.astype(F32)
    ).astype(BF)
    share_contract = lax.psum_scatter(
        contract_sum, "dp", scatter_dimension=0, axis_index_groups=lines()
    ).astype(F32)
    up_part, branch_own, *branch_sent = call(
        finish_kernel,
        [((width, units), BF), (flat, F32)] + [(flat, BF)] * 3,
        (*row_slots, active, hidden_grad, second_weight),
        [VMEM] * (CHIPS + 3),
        (),
        8 * flops,
        6 * moved,
    )

    def rows_both(part):
        part = part.reshape(groups, CHIPS, 2, rows, part.shape[1])
        got = swap(lax.dynamic_index_in_dim(part, 1 - core, 2, keepdims=False), 1)
        return lax.dynamic_index_in_dim(part, core, 2, keepdims=False).astype(F32) + got.astype(F32)

    expand_both = rows_both(up_part)
    second_sum = second_own + second_got[0].astype(F32) + second_got[1].astype(F32) + second_got[2].astype(F32)
    second_grad = turn(second_sum.astype(BF), (groups - z) % groups, 1, groups)
    second_grad, expand_both, branch_sent = lax.optimization_barrier((second_grad, expand_both, branch_sent))

    expand_rows = line_sum(expand_both)
    mixed_grad, mixed_low, context_grad, value_grad, midnorm_sum, midshift_sum = call(
        mixed_kernel,
        [(flat, F32), (flat, BF), (flat, BF), (flat, BF), (wide, F32), (wide, F32)],
        (second_grad, mixed, result_sensitivity, gain_second, mixer_projection_matrix, value_rows, probs),
        [VMEM] * 4 + [ANY] + [VMEM] * 2,
        [weight_space, dma],
        flops,
        moved,
    )
    share = width // CHIPS

    def split_columns(*grads):
        chunks = jnp.concatenate([grad.reshape(tokens, CHIPS, share) for grad in grads], axis=2)
        return exchange(chunks.transpose(1, 0, 2))

    context_slots = spread(after(turn(context, z, 1, groups), first_slots))
    first_pair = split_columns(mixed_low, value_grad)
    query_grad, key_grad = call(
        score_kernel,
        [(flat, BF)] * 2,
        (context_grad, query_rot, key_rot, value_rows, probs, cosine, sine),
        [VMEM] * 7,
        (),
        flops,
        moved,
    )
    second_pair = split_columns(key_grad, query_grad)
    branch_got = [swap(branch_sent[j - 1], 2 * j) for j in range(1, CHIPS)]
    branch = branch_own + branch_got[0].astype(F32) + branch_got[1].astype(F32) + branch_got[2].astype(F32)
    branch = (branch + result_offset).astype(BF).astype(F32)
    layer_output = (mixed + kept * branch).astype(BF)
    layer_input_gradient, leadnorm_sum, leadshift_sum = call(
        leading_kernel,
        [(flat, BF), (wide, F32), (wide, F32)],
        (
            query_grad, key_grad, value_grad, sequence_elements, gain_first, mixed_grad,
            question_matrix, lookup_matrix, content_matrix,
        ),
        [VMEM] * 6 + [ANY] * 3,
        [triple_space, pltpu.VMEM(flat, F32), dmas],
        3 * flops,
        3 * moved,
    )

    def outer(lefts, right):
        (part,) = call(
            outer_kernel,
            [((width, 2 * share), BF)],
            (*lefts, *right),
            [VMEM] * (len(lefts) + CHIPS),
            (),
            2 * flops,
            2 * moved,
        )
        return part

    early = line_sum(rows_both(outer(context_slots + first_slots, first_pair)))
    late = line_sum(rows_both(outer(first_slots, second_pair)))

    def home(summed):
        return in_order(exchange(summed.astype(BF)))

    expand_home = home(expand_rows)
    share_expand = (
        jnp.stack([piece.reshape(rows, groups, block) for piece in expand_home], axis=2)
        .astype(F32)
        .reshape(rows, feed)
    )
    early, late = home(early), home(late)

    def join(pieces, low):
        return jnp.concatenate([piece[:, low : low + share] for piece in pieces], axis=1).astype(F32)

    share_mixing, share_value = join(early, 0), join(early, share)
    share_key, share_query = join(late, 0), join(late, share)

    hidden_spot = (jnp.arange(CHIPS)[None, :, None] == chip).astype(F32)
    hidden_full = hidden_spot * hidden_sum.reshape(groups, 1, block)
    result_sum = jnp.sum(kept_sensitivity.astype(F32), axis=0)
    vectors = [midnorm_sum, midshift_sum, leadnorm_sum, leadshift_sum, result_sum, hidden_full]
    vectors = jnp.concatenate([vector.reshape(devices, -1) for vector in vectors], axis=1)
    vectors = jnp.pad(vectors, ((0, 0), (0, -vectors.shape[1] % 128)))
    vectors = lax.all_to_all(vectors[:, None, :], "dp", 0, 0, tiled=True)
    vectors = jnp.sum(vectors, axis=(0, 1))
    small = [vectors[i * offset_len : (i + 1) * offset_len] for i in range(5)]
    share_hidden = vectors[5 * offset_len : 5 * offset_len + cols]
    return (
        layer_output,
        layer_input_gradient,
        small[2],
        small[3],
        share_query,
        share_key,
        share_value,
        share_mixing,
        small[0],
        small[1],
        share_expand,
        share_hidden,
        share_contract,
        small[4],
    )


def solution(mesh):
    split, line, whole = P("dp", None), P("dp"), P()
    return jax.shard_map(
        per_device,
        mesh=mesh,
        in_specs=(split, split) + (whole,) * 8 + (split, line, split, line, line, whole, whole, split),
        out_specs=(split, split, line, line, split, split, split, split, line, line, split, line, split, line),
        check_vma=False,
    )
```

```python
import jax
import jax.numpy as jnp
import numpy as np
from jax import lax
from jax.experimental import pallas as pl
from jax.experimental.pallas import tpu as pltpu
from jax.sharding import PartitionSpec as P

HEAD_DIM = 128
LEVELS = 4
GROUP = 8
CHIPS = 4
EPSILON = 1e-05
NEGATIVE = -1e30
BF = jnp.bfloat16
F32 = jnp.float32
WIDE = 512
VMEM_BYTES = 56 * 1024 * 1024


def dot(left, right, dims=((1,), (0,))):
    return lax.dot_general(left, right, (dims, ((), ())), preferred_element_type=F32)


def dot_t(left, right):
    return dot(left, right, ((1,), (1,)))


def t_dot(left, right):
    return dot(left, right, ((0,), (0,)))


def rope_tables(length):
    half = HEAD_DIM // 2
    rates = (10000.0 ** (-(np.arange(half, dtype=np.float64) * 2.0 / HEAD_DIM))).astype(np.float32)
    angles = np.arange(length, dtype=np.float32)[:, None] * rates[None, :]
    cosine, sine = np.cos(angles).astype(np.float32), np.sin(angles).astype(np.float32)
    return np.concatenate([cosine, cosine], axis=1), np.concatenate([-sine, sine], axis=1)


def norm_stats(values):
    center = values - jnp.mean(values, axis=-1, keepdims=True)
    inverse = lax.rsqrt(jnp.mean(center * center, axis=-1, keepdims=True) + EPSILON)
    return center * inverse, inverse


def norm_back(incoming, gain, normal, inverse):
    scaled = incoming * gain
    part = inverse * (
        scaled
        - jnp.mean(scaled, axis=-1, keepdims=True)
        - normal * jnp.mean(scaled * normal, axis=-1, keepdims=True)
    )
    return part, jnp.sum(incoming * normal, axis=0, keepdims=True), jnp.sum(incoming, axis=0, keepdims=True)


def swap(value, bit):
    count = lax.axis_size("dp")
    return lax.ppermute(value, "dp", [(i, i ^ bit) for i in range(count)])


def hop(value, step, near, far):
    groups = lax.axis_size("dp") // GROUP
    pairs = [
        (z * GROUP + t, (z + step) * GROUP + t)
        for z in range(max(near, 0), min(far, groups))
        if 0 <= z + step < groups
        for t in range(GROUP)
    ]
    return lax.ppermute(value, "dp", pairs)


def sum_all(value):
    bit = 1
    while bit < lax.axis_size("dp"):
        value = value + swap(value, bit)
        bit *= 2
    return value


def lines():
    groups = lax.axis_size("dp") // GROUP
    return [[z * GROUP + t for z in range(groups)] for t in range(GROUP)]


def spread(own):
    return [own, swap(own, 2), swap(own, 4), swap(own, 6)]


def gather_sum(parts):
    total = parts[0].astype(F32)
    for j in (1, 2, 3):
        total = total + swap(parts[j].astype(BF), 2 * j).astype(F32)
    return total


def exchange(chunks):
    chip = lax.axis_index("dp") % GROUP // 2
    got = []
    for j in range(CHIPS):
        chunk = lax.dynamic_index_in_dim(chunks, chip ^ j, 0, keepdims=False)
        got.append(chunk if j == 0 else swap(chunk, 2 * j))
    return got


def quads():
    count = lax.axis_size("dp")
    return [
        [first + 2 * c + core for c in range(CHIPS)] for first in range(0, count, GROUP) for core in range(2)
    ]


def trade(chunks):
    return lax.all_to_all(chunks, "dp", 0, 0, tiled=True, axis_index_groups=quads())


def share_out(own):
    return trade(jnp.broadcast_to(own, (CHIPS,) + own.shape))


def in_order(slots):
    chip = lax.axis_index("dp") % GROUP // 2
    odd, high = chip % 2 == 1, chip // 2 == 1
    a, b, c, d = slots
    a, b, c, d = jnp.where(odd, b, a), jnp.where(odd, a, b), jnp.where(odd, d, c), jnp.where(odd, c, d)
    return [jnp.where(high, c, a), jnp.where(high, d, b), jnp.where(high, a, c), jnp.where(high, b, d)]


def line_step(sides, own, s):
    groups = lax.axis_size("dp") // GROUP
    up, down = sides if s > 1 else (own, own)
    return hop(up, 1, s - 1, groups - 1), hop(down, -1, 1, groups - s + 1)


def line_stack(own, steps):
    groups = lax.axis_size("dp") // GROUP
    z = lax.axis_index("dp") // GROUP
    return jnp.stack(
        [own]
        + [jnp.where(z + s < groups, steps[s - 1][1], steps[groups - s - 1][0]) for s in range(1, groups)]
    )


def line_sum(parts):
    groups = lax.axis_size("dp") // GROUP
    total = parts[0].astype(F32)
    for s in range(1, groups):
        pairs = [
            (z * GROUP + t, (z + s) % groups * GROUP + t) for z in range(groups) for t in range(GROUP)
        ]
        total = total + lax.ppermute(parts[s].astype(BF), "dp", pairs).astype(F32)
    return total


def sum_step(parts, sides, s):
    groups = parts.shape[0]
    up, down = parts[groups - s], parts[s]
    if sides is not None:
        up = (up.astype(F32) + sides[0].astype(F32)).astype(BF)
        down = (down.astype(F32) + sides[1].astype(F32)).astype(BF)
    return hop(up, 1, 0, s), hop(down, -1, groups - s, groups)


def sum_end(parts, sides):
    return parts[0].astype(F32) + sides[0].astype(F32) + sides[1].astype(F32)


def after(value, *others):
    return lax.optimization_barrier((value,) + others)[0]


def turn(value, shift, axis, parts):
    step = value.shape[axis] // parts
    return lax.dynamic_slice_in_dim(
        jnp.concatenate([value, value], axis=axis), shift * step, value.shape[axis], axis
    )


def core_sum(mine, other):
    return mine + swap(other.astype(BF), 1).astype(F32)


ANY = pl.BlockSpec(memory_space=pl.ANY)
VMEM = pl.BlockSpec(memory_space=pltpu.VMEM)
SMEM = pl.BlockSpec(memory_space=pltpu.SMEM)


def call(kernel, outs, args, places, scratch=(), micros=1):
    return pl.pallas_call(
        kernel,
        out_shape=tuple(jax.ShapeDtypeStruct(shape, kind) for shape, kind in outs),
        in_specs=list(places),
        out_specs=tuple(VMEM for _ in outs),
        scratch_shapes=list(scratch),
        compiler_params=pltpu.CompilerParams(vmem_limit_bytes=VMEM_BYTES),
        cost_estimate=pl.CostEstimate(flops=micros * 1000000000, bytes_accessed=1000, transcendentals=0),
    )(*args)


def fetch(source, target, sem):
    copy = pltpu.make_async_copy(source, target, sem)
    copy.start()
    return copy


def turned(values, cosine, sine):
    return values * cosine + pltpu.roll(values, HEAD_DIM // 2, 1) * sine


def project_kernel(
    x_ref, gain_ref, shift_ref, cos_ref, sin_ref, wq, wk, wv, normed_ref, q_ref, k_ref, v_ref, w_ref, sems
):
    copies = [fetch(w, w_ref.at[i], sems.at[i]) for i, w in enumerate((wq, wk, wv))]
    normal, _ = norm_stats(x_ref[...].astype(F32))
    normed_ref[...] = (normal * gain_ref[...] + shift_ref[...]).astype(BF)
    cosine, sine = cos_ref[...], sin_ref[...]
    for i, out in enumerate((q_ref, k_ref, v_ref)):
        copies[i].wait()
        for low in range(0, out.shape[1], WIDE):
            raw = dot(normed_ref[...], w_ref[i, :, low : low + WIDE])
            for h in range(0, WIDE, HEAD_DIM):
                head = raw[:, h : h + HEAD_DIM]
                if i < 2:
                    head = turned(head, cosine, sine)
                out[:, low + h : low + h + HEAD_DIM] = head.astype(BF)


def attend_kernel(
    q_ref, k_ref, v_ref, x_ref, gain_ref, shift_ref, wo, context_ref, mixed_ref, normed_ref, probs_ref, w_ref, sem
):
    copy = fetch(wo, w_ref, sem)
    tokens, width = q_ref.shape
    row = lax.broadcasted_iota(jnp.int32, (tokens, tokens), 0)
    causal = row >= lax.broadcasted_iota(jnp.int32, (tokens, tokens), 1)
    for h in range(width // HEAD_DIM):
        span = slice(h * HEAD_DIM, (h + 1) * HEAD_DIM)
        scores = dot_t(q_ref[:, span], k_ref[:, span]) * HEAD_DIM**-0.5
        scores = jnp.where(causal, scores, NEGATIVE)
        weight = jnp.exp(scores - jnp.max(scores, axis=-1, keepdims=True))
        probs = weight / jnp.sum(weight, axis=-1, keepdims=True)
        probs_ref[h] = probs
        context_ref[:, span] = dot(probs.astype(BF), v_ref[:, span]).astype(BF)
    copy.wait()
    for low in range(0, width, WIDE):
        span = slice(low, low + WIDE)
        mixed_ref[:, span] = x_ref[:, span].astype(F32) + dot(context_ref[...], w_ref[:, span])
    normal, _ = norm_stats(mixed_ref[...])
    normed_ref[...] = (normal * gain_ref[...] + shift_ref[...]).astype(BF)


def place_first(weights, w_ref, sems, core):
    if len(weights) == 1:
        return [fetch(weights[0], w_ref, sems.at[0])]
    groups, rows = weights[0].shape[0], weights[0].shape[1] // CHIPS
    copies = []
    for k, source in enumerate(weights):
        side = core if k == 0 else 1 - core
        for g in range(groups):
            for c in range(CHIPS):
                low = pl.multiple_of(((g * CHIPS + c) * 2 + side) * rows, 16)
                copies.append(
                    fetch(
                        source.at[g, c * rows : (c + 1) * rows],
                        w_ref.at[pl.ds(low, rows)],
                        sems.at[len(copies)],
                    )
                )
    return copies


def place_second(weights, w_ref, sems, z, core):
    groups, cols, _ = weights[0].shape
    copies = []
    for k, source in enumerate(weights):
        side = core if k == 0 else 1 - core
        for g in range(groups):
            low = pl.multiple_of((side * groups + lax.rem(z + g, groups)) * cols, 16)
            copies.append(fetch(source.at[g], w_ref.at[pl.ds(low, cols)], sems.at[len(copies)]))
    return copies


def by_slot(array_ref, chip):
    return jnp.concatenate([array_ref[chip ^ j] for j in range(CHIPS)], axis=0)


def split_rows(value, out_ref, low, core, at):
    _, groups, held, _ = out_ref.shape
    rows = held // CHIPS
    for pair in range(value.shape[0] // rows // 2):
        g, c = divmod(low // rows // 2 + pair, CHIPS)
        first = value[2 * pair * rows : (2 * pair + 1) * rows]
        second = value[(2 * pair + 1) * rows : (2 * pair + 2) * rows]
        spot = slice(c * rows, (c + 1) * rows)
        out_ref[0, g, spot, at] = jnp.where(core == 0, first, second)
        out_ref[1, g, spot, at] = jnp.where(core == 0, second, first)


def hidden_kernel(*refs):
    place, xs = refs[0], refs[1 : 1 + CHIPS]
    bias_ref, mask_ref = refs[1 + CHIPS : 3 + CHIPS]
    weights = refs[3 + CHIPS : -4]
    active_ref, slope_ref, w_ref, sems = refs[-4:]
    copies = place_first(weights, w_ref, sems, place[2])
    x = jnp.concatenate([x[...] for x in xs], axis=0)
    tokens = xs[0].shape[0]
    for copy in copies:
        copy.wait()
    for low in range(0, w_ref.shape[1], WIDE):
        span = slice(low, low + WIDE)
        hidden = dot(x, w_ref[:, span]) + bias_ref[:, span]
        square = hidden * hidden
        bent = jnp.tanh(0.7978845608 * hidden * (1.0 + 0.044715 * square))
        slope = 0.5 * (1.0 + bent) + (0.5 * 0.7978845608) * hidden * (1.0 - bent * bent) * (
            1.0 + 3.0 * 0.044715 * square
        )
        value = 0.5 * hidden * (1.0 + bent)
        for j in range(CHIPS):
            part = slice(j * tokens, (j + 1) * tokens)
            keep = mask_ref[j : j + 1, span]
            active_ref[part, span] = (value[part] * keep).astype(BF)
            slope_ref[part, span] = slope[part] * keep


def down_kernel(place, active_ref, grad_ref, out_ref):
    z, chip, core = place[0], place[1], place[2]
    _, groups, cols, width = out_ref.shape
    grad = by_slot(grad_ref, chip)
    half = groups * cols
    for k in range(2):
        low = pl.multiple_of((core ^ k) * half, 128)
        for at in range(0, width, WIDE):
            value = t_dot(active_ref[:, pl.ds(low, half)], grad[:, at : at + WIDE]).astype(BF)
            for g in range(groups):
                slot = lax.rem(g + groups - z, groups)
                out_ref[k, slot, :, at : at + WIDE] = value[g * cols : (g + 1) * cols]


def reverse_kernel(*refs):
    place, grads_ref, slope_ref, near2, far2 = refs[:5]
    weights = refs[5:-10]
    grad_ref, sum_ref, own_ref = refs[-10:-7]
    sent = refs[-7:-4]
    w1_ref, w2_ref, sems1, sems2 = refs[-4:]
    second = place_second((near2, far2), w2_ref, sems2, place[0], place[2])
    first = place_first(weights, w1_ref, sems1, place[2])
    tokens = grads_ref.shape[1]
    grad = by_slot(grads_ref, place[1])
    for copy in second:
        copy.wait()
    for low in range(0, w2_ref.shape[0], WIDE):
        span = slice(low, low + WIDE)
        value = (dot_t(grad, w2_ref[span, :]) * slope_ref[:, span]).astype(BF)
        grad_ref[:, span] = value
        sum_ref[:, span] = jnp.sum(value.astype(F32), axis=0, keepdims=True)
    for copy in first:
        copy.wait()
    for low in range(0, w1_ref.shape[0], WIDE):
        span = slice(low, low + WIDE)
        part = dot_t(grad_ref[...], w1_ref[span, :])
        own_ref[:, span] = part[:tokens]
        for j in range(1, CHIPS):
            sent[j - 1][:, span] = part[j * tokens : (j + 1) * tokens].astype(BF)


def finish_kernel(*refs):
    place, xs = refs[0], refs[1 : 1 + CHIPS]
    active_ref, grad_ref, near2, far2, up_ref, own_ref = refs[1 + CHIPS : 7 + CHIPS]
    sent = refs[7 + CHIPS : 10 + CHIPS]
    w2_ref, sems = refs[-2:]
    second = place_second((near2, far2), w2_ref, sems, place[0], place[2])
    tokens, width = xs[0].shape
    step = width // CHIPS
    for low in range(0, width, step):
        x = jnp.concatenate([x[:, low : low + step] for x in xs], axis=0)
        value = t_dot(x, grad_ref[...]).astype(BF)
        if len(up_ref.shape) == 2:
            up_ref[low : low + step, :] = value
        else:
            split_rows(value, up_ref, low, place[2], slice(None))
    for copy in second:
        copy.wait()
    for low in range(0, width, WIDE):
        span = slice(low, low + WIDE)
        part = dot(active_ref[...], w2_ref[:, span])
        own_ref[:, span] = part[:tokens]
        for j in range(1, CHIPS):
            sent[j - 1][:, span] = part[j * tokens : (j + 1) * tokens].astype(BF)


def mixed_kernel(
    second_ref, mixed_ref, sens_ref, gain_ref, wo, v_ref, probs_ref,
    mixgrad_ref, low_ref, cgrad_ref, vgrad_ref, norm_ref, shift_ref, w_ref, sem
):
    copy = fetch(wo, w_ref, sem)
    normal, inverse = norm_stats(mixed_ref[...])
    part, norm_sum, shift_sum = norm_back(second_ref[...].astype(F32), gain_ref[...], normal, inverse)
    norm_ref[...], shift_ref[...] = norm_sum, shift_sum
    mixed_grad = sens_ref[...].astype(F32) + part
    mixgrad_ref[...] = mixed_grad
    low_ref[...] = mixed_grad.astype(BF)
    copy.wait()
    width = v_ref.shape[1]
    for low in range(0, width, WIDE):
        cgrad_ref[:, low : low + WIDE] = dot_t(low_ref[...], w_ref[low : low + WIDE, :]).astype(BF)
    for h in range(width // HEAD_DIM):
        span = slice(h * HEAD_DIM, (h + 1) * HEAD_DIM)
        vgrad_ref[:, span] = t_dot(probs_ref[h].astype(BF), cgrad_ref[:, span]).astype(BF)


def score_kernel(cgrad_ref, q_ref, k_ref, v_ref, probs_ref, cos_ref, sin_ref, qgrad_ref, kgrad_ref):
    cosine, sine = cos_ref[...], -sin_ref[...]
    for h in range(v_ref.shape[1] // HEAD_DIM):
        span = slice(h * HEAD_DIM, (h + 1) * HEAD_DIM)
        probs = probs_ref[h]
        probs_grad = dot_t(cgrad_ref[:, span], v_ref[:, span])
        inner = jnp.sum(probs_grad * probs, axis=-1, keepdims=True)
        scores_grad = (probs * (probs_grad - inner)).astype(BF)
        scale = HEAD_DIM**-0.5
        qgrad_ref[:, span] = turned(dot(scores_grad, k_ref[:, span]) * scale, cosine, sine).astype(BF)
        kgrad_ref[:, span] = turned(t_dot(scores_grad, q_ref[:, span]) * scale, cosine, sine).astype(BF)


def leading_kernel(
    qgrad_ref, kgrad_ref, vgrad_ref, x_ref, gain_ref, mixgrad_ref, wq, wk, wv,
    out_ref, norm_ref, shift_ref, w_ref, lead_ref, sems
):
    copies = [fetch(w, w_ref.at[i], sems.at[i]) for i, w in enumerate((wq, wk, wv))]
    normal, inverse = norm_stats(x_ref[...].astype(F32))
    for copy in copies:
        copy.wait()
    for low in range(0, x_ref.shape[1], WIDE):
        span = slice(low, low + WIDE)
        lead_ref[:, span] = (
            dot_t(qgrad_ref[...], w_ref[0, span, :])
            + dot_t(kgrad_ref[...], w_ref[1, span, :])
            + dot_t(vgrad_ref[...], w_ref[2, span, :])
        )
    part, norm_sum, shift_sum = norm_back(lead_ref[...], gain_ref[...], normal, inverse)
    norm_ref[...], shift_ref[...] = norm_sum, shift_sum
    out_ref[...] = (mixgrad_ref[...] + part).astype(BF)


def outer_kernel(place, *refs):
    lefts, right_ref, out_ref = refs[:-2], refs[-2], refs[-1]
    tokens, width = lefts[0].shape[1:]
    right = right_ref[...].reshape(CHIPS * tokens, right_ref.shape[2])
    share = right.shape[1] // len(lefts)
    step = width // CHIPS
    for i, left_ref in enumerate(lefts):
        at = slice(i * share, (i + 1) * share)
        for low in range(0, width, step):
            left = left_ref[:, :, low : low + step].reshape(CHIPS * tokens, step)
            value = t_dot(left, right[:, at]).astype(BF)
            if len(out_ref.shape) == 2:
                out_ref[low : low + step, at] = value
            else:
                split_rows(value, out_ref, low, place[2], at)


def per_device(
    sequence_elements,
    result_sensitivity,
    mixer_gain,
    mixer_offset,
    question_matrix,
    lookup_matrix,
    content_matrix,
    mixer_projection_matrix,
    feedforward_gain,
    feedforward_offset,
    expand_matrix,
    inner_neuron_offset,
    contract_matrix,
    feedforward_result_offset,
    sequence_level_choice,
    servers_per_level,
    accepted_row_limit,
    server_selection,
):
    devices = lax.axis_size("dp")
    me = lax.axis_index("dp")
    groups = devices // GROUP
    z, chip, core = me // GROUP, me % GROUP // 2, me % 2
    tokens, width = sequence_elements.shape
    heads = width // HEAD_DIM
    rows, feed = expand_matrix.shape
    cols = contract_matrix.shape[0]
    offset_len = feedforward_result_offset.shape[0]
    levels = jnp.arange(LEVELS)
    block = 2 * cols
    units = groups * block
    gain_first, shift_first, gain_second, shift_second = (
        v.astype(F32)[None, :] for v in (mixer_gain, mixer_offset, feedforward_gain, feedforward_offset)
    )
    cosine, sine = (jnp.asarray(t) for t in rope_tables(tokens))
    flat, wide = (tokens, width), (1, width)
    square = (width, width)
    all_rows = (CHIPS * tokens, units)
    weight_space = pltpu.VMEM(square, BF)
    triple_space = pltpu.VMEM((3,) + square, BF)
    hidden_space = pltpu.VMEM((width, units), BF)
    dma, dmas = pltpu.SemaphoreType.DMA, pltpu.SemaphoreType.DMA((3,))
    aligned = rows % 16 == 0
    firsts = pltpu.SemaphoreType.DMA((2 * groups * CHIPS if aligned else 1,))
    seconds = pltpu.SemaphoreType.DMA((2 * groups,))
    place = jnp.stack([z, chip, core]).astype(jnp.int32)
    fence = lax.optimization_barrier

    expand_chunks = expand_matrix.reshape(rows, groups, CHIPS, 2, cols).transpose(2, 0, 3, 1, 4)
    expand_pieces = exchange(expand_chunks.reshape(CHIPS, rows, units))
    contract_steps = [line_step(None, contract_matrix, 1)]
    normed_first, query_rot, key_rot, value_rows = call(
        project_kernel,
        [(flat, BF)] * 4,
        (sequence_elements, gain_first, shift_first, cosine, sine, question_matrix, lookup_matrix, content_matrix),
        [VMEM] * 5 + [ANY] * 3,
        [triple_space, dmas], micros=8)
    normed_first, query_rot, key_rot, value_rows, expand_pieces = fence(
        (normed_first, query_rot, key_rot, value_rows, expand_pieces)
    )

    expand_plane = jnp.concatenate(in_order(expand_pieces), axis=0)
    expand_steps = [line_step(None, expand_plane, 1)]
    group_first = share_out(turn(normed_first, z, 1, groups))
    context, mixed, normed_second, probs = call(
        attend_kernel,
        [(flat, BF), (flat, F32), (flat, BF), ((heads, tokens, tokens), F32)],
        (query_rot, key_rot, value_rows, sequence_elements, gain_second, shift_second, mixer_projection_matrix),
        [VMEM] * 6 + [ANY],
        [weight_space, dma], micros=6)
    context, mixed, normed_second, contract_steps = fence((context, mixed, normed_second, contract_steps))

    row_slots = spread(turn(normed_second, z, 1, groups))
    expand_steps, group_first = fence((expand_steps, group_first))
    level = sequence_level_choice[0]
    choice = server_selection.reshape(-1)
    info = jnp.concatenate(
        [
            feedforward_result_offset.astype(F32),
            inner_neuron_offset.astype(F32),
            level.astype(F32)[None],
            jnp.min(choice).astype(F32)[None],
        ]
    )
    info = jnp.pad(info, (0, -info.shape[0] % 128))
    table = after(jnp.broadcast_to(info, (devices, 1) + info.shape), group_first)
    table = lax.all_to_all(table, "dp", 0, 0, tiled=True).reshape(devices, -1)
    expand_steps.append(line_step(expand_steps[-1], expand_plane, 2))
    expand_steps, table = fence((expand_steps, table))
    for s in range(3, groups):
        expand_steps.append(line_step(expand_steps[-1], expand_plane, s))
    result_offset = table[:, :offset_len].reshape(-1)
    hidden_offsets = table[:, offset_len : offset_len + cols]
    all_levels = table[:, offset_len + cols].astype(jnp.int32)
    all_lowest = table[:, offset_len + cols + 1].astype(jnp.int32)
    size = jnp.sum(jnp.where(levels == level, servers_per_level, 0))
    limit = jnp.sum(jnp.where(levels == level, accepted_row_limit, 0))
    server = choice % size
    before = jnp.arange(tokens)[None, :] < jnp.arange(tokens)[:, None]
    local = jnp.sum((before & (server[None, :] == server[:, None])).astype(jnp.int32), axis=1)
    low = all_lowest[None, :]
    seen = (low + tokens - 1 - server[:, None] + size) // size - (low - 1 - server[:, None] + size) // size
    earlier = (jnp.arange(devices) < me) & (all_levels == level)
    arrival = local + jnp.sum(jnp.where(earlier[None, :], seen, 0), axis=1)
    kept = (arrival < limit).astype(F32)[:, None]
    kept_sensitivity = (result_sensitivity.astype(F32) * kept).astype(BF)
    slot_levels = jnp.take(all_levels, me ^ (2 * jnp.arange(CHIPS)))
    starts = (jnp.arange(groups) * CHIPS + chip) * block
    active_block = starts[None, :] < (feed // 8) * (1 << slot_levels[:, None])
    mask = jnp.tile(jnp.repeat(active_block.astype(F32), cols, axis=1), (1, 2))
    hidden_offset = lax.dynamic_index_in_dim(
        hidden_offsets.reshape(groups, CHIPS, 2, cols), chip, 1, keepdims=False
    )
    hidden_offset = hidden_offset.transpose(1, 0, 2).reshape(1, -1)
    row_slots, kept_sensitivity = fence((row_slots, kept_sensitivity))
    group_grad = share_out(kept_sensitivity)
    expand_steps, kept_sensitivity = fence((expand_steps, kept_sensitivity))
    expand_mine = line_stack(expand_plane, expand_steps)
    expand_other = swap(expand_mine, 1)
    contract_steps[0] = after(contract_steps[0], expand_mine)
    for s in range(2, groups):
        contract_steps.append(line_step(contract_steps[-1], contract_matrix, s))
    if aligned:
        first_weight = (expand_mine, expand_other)
    else:
        pair = jnp.stack([expand_mine, expand_other]).reshape(2, groups, CHIPS, rows, units)
        first_weight = (jnp.where(core == 0, pair, pair[::-1]).transpose(1, 2, 0, 3, 4).reshape(width, units),)

    active, slope = call(
        hidden_kernel,
        [(all_rows, BF), (all_rows, F32)],
        (place, *row_slots, hidden_offset, mask, *first_weight),
        [SMEM] + [VMEM] * (CHIPS + 2) + [ANY] * len(first_weight),
        [hidden_space, firsts], micros=12)
    if groups > 2:
        active, contract_steps[1] = fence((active, contract_steps[1]))
        for s in range(3, groups):
            contract_steps[s - 1] = line_step(contract_steps[s - 2], contract_matrix, s)
    down_part, = call(
        down_kernel,
        [((2, groups, cols, width), BF)],
        (place, active, group_grad),
        [SMEM] + [VMEM] * 2, micros=8)
    down_part, contract_steps = fence((down_part, contract_steps))
    contract_mine = line_stack(contract_matrix, contract_steps)
    contract_other = swap(contract_mine, 1)
    down_got = swap(down_part[1], 1)
    contract_both = (down_part[0].astype(F32) + down_got.astype(F32)).astype(BF)
    contract_other, contract_both = fence((contract_other, contract_both))
    contract_sides = sum_step(contract_both, None, 1)
    hidden_grad, hidden_sum, second_own, *second_sent = call(
        reverse_kernel,
        [(all_rows, BF), ((1, units), F32), (flat, F32)] + [(flat, BF)] * 3,
        (place, group_grad, slope, contract_mine, contract_other, *first_weight),
        [SMEM] + [VMEM] * 2 + [ANY] * (2 + len(first_weight)),
        [hidden_space, pltpu.VMEM((units, width), BF), firsts, seconds], micros=15)
    hidden_grad, second_sent, contract_sides = fence((hidden_grad, second_sent, contract_sides))
    second_got = [swap(second_sent[j - 1], 2 * j) for j in range(1, CHIPS)]
    contract_sides = sum_step(contract_both, contract_sides, 2)
    both_shape = (2, groups, CHIPS * rows) if aligned else (width,)
    up_part, branch_own, *branch_sent = call(
        finish_kernel,
        [(both_shape + (units,), BF), (flat, F32)] + [(flat, BF)] * 3,
        (place, *row_slots, active, hidden_grad, contract_mine, contract_other),
        [SMEM] + [VMEM] * (CHIPS + 2) + [ANY] * 2,
        [pltpu.VMEM((units, width), BF), seconds], micros=13)
    up_part, branch_sent, contract_sides = fence((up_part, branch_sent, contract_sides))
    for s in range(3, groups):
        contract_sides = sum_step(contract_both, contract_sides, s)

    def rows_both(part):
        if not aligned:
            part = part.reshape(groups, CHIPS, 2, rows, part.shape[1])
            part = jnp.stack(
                [lax.dynamic_index_in_dim(part, core ^ k, 2, keepdims=False) for k in range(2)]
            ).reshape(2, groups, CHIPS * rows, part.shape[4])
        return (part[0].astype(F32) + swap(part[1], 1).astype(F32)).astype(BF)

    second_sum = second_own + second_got[0].astype(F32) + second_got[1].astype(F32) + second_got[2].astype(F32)
    second_grad = turn(second_sum.astype(BF), (groups - z) % groups, 1, groups)
    expand_both = rows_both(up_part)

    mixed_grad, mixed_low, context_grad, value_grad, midnorm_sum, midshift_sum = call(
        mixed_kernel,
        [(flat, F32), (flat, BF), (flat, BF), (flat, BF), (wide, F32), (wide, F32)],
        (second_grad, mixed, result_sensitivity, gain_second, mixer_projection_matrix, value_rows, probs),
        [VMEM] * 4 + [ANY] + [VMEM] * 2,
        [weight_space, dma], micros=8)
    mixed_low, context_grad, value_grad, contract_sides, expand_both = fence(
        (mixed_low, context_grad, value_grad, contract_sides, expand_both)
    )
    share_contract = sum_end(contract_both, contract_sides)
    share = width // CHIPS

    def split_columns(*grads):
        chunks = jnp.concatenate([grad.reshape(tokens, CHIPS, share) for grad in grads], axis=2)
        return trade(chunks.transpose(1, 0, 2))

    expand_sides = sum_step(expand_both, None, 1)
    group_context = share_out(after(turn(context, z, 1, groups), hidden_grad))
    first_pair = split_columns(mixed_low, value_grad)
    branch_got = [swap(branch_sent[j - 1], 2 * j) for j in range(1, CHIPS)]
    query_grad, key_grad = call(
        score_kernel,
        [(flat, BF)] * 2,
        (context_grad, query_rot, key_rot, value_rows, probs, cosine, sine),
        [VMEM] * 7, micros=7)
    query_grad, key_grad, expand_sides, first_pair, group_context = fence(
        (query_grad, key_grad, expand_sides, first_pair, group_context)
    )
    second_pair = split_columns(key_grad, query_grad)
    expand_sides = sum_step(expand_both, expand_sides, 2)

    def outer(lefts, right):
        (part,) = call(
            outer_kernel,
            [(both_shape + (2 * share,), BF)],
            (place, *lefts, right),
            [SMEM] + [VMEM] * (len(lefts) + 1), micros=6)
        return part

    early = outer((group_context, group_first), first_pair)
    early, branch_got = fence((early, branch_got))
    early_both = rows_both(early)
    branch = branch_own + branch_got[0].astype(F32) + branch_got[1].astype(F32) + branch_got[2].astype(F32)
    branch = (branch + result_offset).astype(BF).astype(F32)
    layer_output = (mixed + kept * branch).astype(BF)
    layer_input_gradient, leadnorm_sum, leadshift_sum = call(
        leading_kernel,
        [(flat, BF), (wide, F32), (wide, F32)],
        (
            query_grad, key_grad, value_grad, sequence_elements, gain_first, mixed_grad,
            question_matrix, lookup_matrix, content_matrix,
        ),
        [VMEM] * 6 + [ANY] * 3,
        [triple_space, pltpu.VMEM(flat, F32), dmas], micros=13)
    leadnorm_sum, expand_sides, early_both, second_pair = fence(
        (leadnorm_sum, expand_sides, early_both, second_pair)
    )
    for s in range(3, groups):
        expand_sides = sum_step(expand_both, expand_sides, s)
    early_sum = line_sum(early_both)
    late = outer((group_first,), second_pair)
    late, expand_sides = fence((late, expand_sides))
    late_both = rows_both(late)
    late_sum = line_sum(late_both)

    def home(summed):
        return trade(summed.astype(BF).reshape(CHIPS, rows, -1))

    hidden_spot = (jnp.arange(CHIPS)[None, :, None, None] == chip).astype(F32)
    hidden_full = hidden_spot * hidden_sum.reshape(2, groups, cols).transpose(1, 0, 2)[:, None]
    result_sum = jnp.sum(kept_sensitivity.astype(F32), axis=0)
    vectors = [midnorm_sum, midshift_sum, leadnorm_sum, leadshift_sum, result_sum, hidden_full]
    vectors = jnp.concatenate([vector.reshape(devices, -1) for vector in vectors], axis=1)
    vectors = jnp.pad(vectors, ((0, 0), (0, -vectors.shape[1] % 128)))
    vectors = lax.all_to_all(vectors[:, None, :], "dp", 0, 0, tiled=True)
    vectors = jnp.sum(vectors, axis=(0, 1))
    small = [vectors[i * offset_len : (i + 1) * offset_len] for i in range(5)]
    share_hidden = vectors[5 * offset_len : 5 * offset_len + cols]

    expand_home = home(sum_end(expand_both, expand_sides))
    share_expand = (
        expand_home.reshape(CHIPS, rows, 2, groups, cols).transpose(1, 3, 0, 2, 4).reshape(rows, feed).astype(F32)
    )
    early_home, late_home = home(early_sum), home(late_sum)

    def join(pieces, low):
        return pieces[:, :, low : low + share].transpose(1, 0, 2).reshape(rows, width).astype(F32)

    share_mixing, share_value = join(early_home, 0), join(early_home, share)
    share_key, share_query = join(late_home, 0), join(late_home, share)
    return (
        layer_output,
        layer_input_gradient,
        small[2],
        small[3],
        share_query,
        share_key,
        share_value,
        share_mixing,
        small[0],
        small[1],
        share_expand,
        share_hidden,
        share_contract,
        small[4],
    )


def solution(mesh):
    split, line, whole = P("dp", None), P("dp"), P()
    return jax.shard_map(
        per_device,
        mesh=mesh,
        in_specs=(split, split) + (whole,) * 8 + (split, line, split, line, line, whole, whole, split),
        out_specs=(split, split, line, line, split, split, split, split, line, line, split, line, split, line),
        check_vma=False,
    )
```

```python
import jax
import jax.numpy as jnp
import numpy as np
from jax import lax
from jax.experimental import pallas as pl
from jax.experimental.pallas import tpu as pltpu
from jax.sharding import PartitionSpec as P

HEAD_DIM = 128
LEVELS = 4
GROUP = 8
CHIPS = 4
EPSILON = 1e-05
NEGATIVE = -1e30
BF = jnp.bfloat16
F32 = jnp.float32
WIDE = 512
VMEM_BYTES = 56 * 1024 * 1024


def dot(left, right, dims=((1,), (0,))):
    return lax.dot_general(left, right, (dims, ((), ())), preferred_element_type=F32)


def dot_t(left, right):
    return dot(left, right, ((1,), (1,)))


def t_dot(left, right):
    return dot(left, right, ((0,), (0,)))


def rope_tables(length):
    half = HEAD_DIM // 2
    rates = (10000.0 ** (-(np.arange(half, dtype=np.float64) * 2.0 / HEAD_DIM))).astype(np.float32)
    angles = np.arange(length, dtype=np.float32)[:, None] * rates[None, :]
    cosine, sine = np.cos(angles).astype(np.float32), np.sin(angles).astype(np.float32)
    return np.concatenate([cosine, cosine], axis=1), np.concatenate([-sine, sine], axis=1)


def norm_stats(values):
    center = values - jnp.mean(values, axis=-1, keepdims=True)
    inverse = lax.rsqrt(jnp.mean(center * center, axis=-1, keepdims=True) + EPSILON)
    return center * inverse, inverse


def norm_back(incoming, gain, normal, inverse):
    scaled = incoming * gain
    part = inverse * (
        scaled
        - jnp.mean(scaled, axis=-1, keepdims=True)
        - normal * jnp.mean(scaled * normal, axis=-1, keepdims=True)
    )
    return part, jnp.sum(incoming * normal, axis=0, keepdims=True), jnp.sum(incoming, axis=0, keepdims=True)


def swap(value, bit):
    count = lax.axis_size("dp")
    return lax.ppermute(value, "dp", [(i, i ^ bit) for i in range(count)])


def hop(value, step, near, far):
    groups = lax.axis_size("dp") // GROUP
    pairs = [
        (z * GROUP + t, (z + step) * GROUP + t)
        for z in range(max(near, 0), min(far, groups))
        if 0 <= z + step < groups
        for t in range(GROUP)
    ]
    return lax.ppermute(value, "dp", pairs)


def scatter_all(parts):
    count = lax.axis_size("dp")
    parts = jnp.take(parts, lax.axis_index("dp") ^ jnp.arange(count), axis=0)
    bit = count // 2
    while bit:
        parts = parts[:bit] + swap(parts[bit:], bit)
        bit //= 2
    return parts


def lines():
    groups = lax.axis_size("dp") // GROUP
    return [[z * GROUP + t for z in range(groups)] for t in range(GROUP)]


def spread(own):
    return [own, swap(own, 2), swap(own, 4), swap(own, 6)]


def exchange(chunks):
    chip = lax.axis_index("dp") % GROUP // 2
    got = []
    for j in range(CHIPS):
        chunk = lax.dynamic_index_in_dim(chunks, chip ^ j, 0, keepdims=False)
        got.append(chunk if j == 0 else swap(chunk, 2 * j))
    return got


def quads():
    count = lax.axis_size("dp")
    return [
        [first + 2 * c + core for c in range(CHIPS)] for first in range(0, count, GROUP) for core in range(2)
    ]


def trade(chunks):
    return lax.all_to_all(chunks, "dp", 0, 0, tiled=True, axis_index_groups=quads())


def share_out(own):
    return trade(jnp.broadcast_to(own, (CHIPS,) + own.shape))


def in_order(slots):
    chip = lax.axis_index("dp") % GROUP // 2
    odd, high = chip % 2 == 1, chip // 2 == 1
    a, b, c, d = slots
    a, b, c, d = jnp.where(odd, b, a), jnp.where(odd, a, b), jnp.where(odd, d, c), jnp.where(odd, c, d)
    return [jnp.where(high, c, a), jnp.where(high, d, b), jnp.where(high, a, c), jnp.where(high, b, d)]


def line_step(sides, own, s):
    groups = lax.axis_size("dp") // GROUP
    up, down = sides if s > 1 else (own, own)
    return hop(up, 1, s - 1, groups - 1), hop(down, -1, 1, groups - s + 1)


def line_stack(own, steps):
    groups = lax.axis_size("dp") // GROUP
    z = lax.axis_index("dp") // GROUP
    return jnp.stack(
        [own]
        + [jnp.where(z + s < groups, steps[s - 1][1], steps[groups - s - 1][0]) for s in range(1, groups)]
    )


def line_sum(parts):
    groups = lax.axis_size("dp") // GROUP
    total = parts[0].astype(F32)
    for s in range(1, groups):
        pairs = [
            (z * GROUP + t, (z + s) % groups * GROUP + t) for z in range(groups) for t in range(GROUP)
        ]
        total = total + lax.ppermute(parts[s].astype(BF), "dp", pairs).astype(F32)
    return total


def after(value, *others):
    return lax.optimization_barrier((value,) + others)[0]


def core_sum(mine, other):
    return mine + swap(other.astype(BF), 1).astype(F32)


ANY = pl.BlockSpec(memory_space=pl.ANY)
VMEM = pl.BlockSpec(memory_space=pltpu.VMEM)
SMEM = pl.BlockSpec(memory_space=pltpu.SMEM)


def call(kernel, outs, args, places, scratch=(), micros=1):
    return pl.pallas_call(
        kernel,
        out_shape=tuple(jax.ShapeDtypeStruct(shape, kind) for shape, kind in outs),
        in_specs=list(places),
        out_specs=tuple(VMEM for _ in outs),
        scratch_shapes=list(scratch),
        compiler_params=pltpu.CompilerParams(vmem_limit_bytes=VMEM_BYTES),
        cost_estimate=pl.CostEstimate(flops=micros * 1000000000, bytes_accessed=1000, transcendentals=0),
    )(*args)


def fetch(source, target, sem):
    copy = pltpu.make_async_copy(source, target, sem)
    copy.start()
    return copy


def turned(values, cosine, sine):
    return values * cosine + pltpu.roll(values, HEAD_DIM // 2, 1) * sine


def project_kernel(
    x_ref, gain_ref, shift_ref, cos_ref, sin_ref, wq, wk, wv, normed_ref, q_ref, k_ref, v_ref, w_ref, sems
):
    copies = [fetch(w, w_ref.at[i], sems.at[i]) for i, w in enumerate((wq, wk, wv))]
    normal, _ = norm_stats(x_ref[...].astype(F32))
    normed_ref[...] = (normal * gain_ref[...] + shift_ref[...]).astype(BF)
    cosine, sine = cos_ref[...], sin_ref[...]
    for i, out in enumerate((q_ref, k_ref, v_ref)):
        copies[i].wait()
        for low in range(0, out.shape[1], WIDE):
            raw = dot(normed_ref[...], w_ref[i, :, low : low + WIDE])
            for h in range(0, WIDE, HEAD_DIM):
                head = raw[:, h : h + HEAD_DIM]
                if i < 2:
                    head = turned(head, cosine, sine)
                out[:, low + h : low + h + HEAD_DIM] = head.astype(BF)


def attend_kernel(
    q_ref, k_ref, v_ref, x_ref, gain_ref, shift_ref, first_ref, wo,
    both_ref, mixed_ref, normed_ref, probs_ref, w_ref, sem
):
    copy = fetch(wo, w_ref, sem)
    tokens, width = q_ref.shape
    both_ref[:tokens] = first_ref[...]
    row = lax.broadcasted_iota(jnp.int32, (tokens, tokens), 0)
    causal = row >= lax.broadcasted_iota(jnp.int32, (tokens, tokens), 1)
    for h in range(width // HEAD_DIM):
        span = slice(h * HEAD_DIM, (h + 1) * HEAD_DIM)
        scores = dot_t(q_ref[:, span], k_ref[:, span]) * HEAD_DIM**-0.5
        scores = jnp.where(causal, scores, NEGATIVE)
        weight = jnp.exp(scores - jnp.max(scores, axis=-1, keepdims=True))
        probs = weight / jnp.sum(weight, axis=-1, keepdims=True)
        probs_ref[h] = probs
        both_ref[tokens:, span] = dot(probs.astype(BF), v_ref[:, span]).astype(BF)
    copy.wait()
    for low in range(0, width, WIDE):
        span = slice(low, low + WIDE)
        mixed_ref[:, span] = x_ref[:, span].astype(F32) + dot(both_ref[tokens:], w_ref[:, span])
    normal, _ = norm_stats(mixed_ref[...])
    normed_ref[...] = (normal * gain_ref[...] + shift_ref[...]).astype(BF)


def place_first(weights, w_ref, sems, z, core):
    if len(weights) == 1:
        return [fetch(weights[0], w_ref, sems.at[0])]
    groups, rows = weights[0].shape[0], weights[0].shape[1] // CHIPS
    copies = []
    for k, source in enumerate(weights):
        side = core if k == 0 else 1 - core
        for g in range(groups):
            for c in range(CHIPS):
                low = pl.multiple_of(((lax.rem(z + g, groups) * CHIPS + c) * 2 + side) * rows, 16)
                copies.append(
                    fetch(
                        source.at[g, c * rows : (c + 1) * rows],
                        w_ref.at[pl.ds(low, rows)],
                        sems.at[len(copies)],
                    )
                )
    return copies


def place_second(weights, w_ref, sems, z, core):
    groups, cols, _ = weights[0].shape
    copies = []
    for k, source in enumerate(weights):
        side = core if k == 0 else 1 - core
        for g in range(groups):
            low = pl.multiple_of((side * groups + lax.rem(z + g, groups)) * cols, 16)
            copies.append(fetch(source.at[g], w_ref.at[pl.ds(low, cols)], sems.at[len(copies)]))
    return copies


def by_slot(array_ref, chip):
    return jnp.concatenate([array_ref[chip ^ j] for j in range(CHIPS)], axis=0)


def put_rows(value, outs, low, core, at):
    if len(outs) == 1:
        outs[0][low : low + value.shape[0], at] = value
        return
    rows = outs[0].shape[1] // CHIPS
    for pair in range(value.shape[0] // rows // 2):
        g, c = divmod(low // rows // 2 + pair, CHIPS)
        first = value[2 * pair * rows : (2 * pair + 1) * rows]
        second = value[(2 * pair + 1) * rows : (2 * pair + 2) * rows]
        spot = slice(c * rows, (c + 1) * rows)
        outs[0][g, spot, at] = jnp.where(core == 0, first, second)
        outs[1][g, spot, at] = jnp.where(core == 0, second, first)


def hidden_kernel(*refs):
    place, xs = refs[0], refs[1 : 1 + CHIPS]
    bias_ref, mask_ref = refs[1 + CHIPS : 3 + CHIPS]
    weights = refs[3 + CHIPS : -4]
    active_ref, slope_ref, w_ref, sems = refs[-4:]
    copies = place_first(weights, w_ref, sems, place[0], place[2])
    x = jnp.concatenate([x[...] for x in xs], axis=0)
    tokens = xs[0].shape[0]
    for copy in copies:
        copy.wait()
    for low in range(0, w_ref.shape[1], WIDE):
        span = slice(low, low + WIDE)
        hidden = dot(x, w_ref[:, span]) + bias_ref[:, span]
        square = hidden * hidden
        bent = jnp.tanh(0.7978845608 * hidden * (1.0 + 0.044715 * square))
        slope = 0.5 * (1.0 + bent) + (0.5 * 0.7978845608) * hidden * (1.0 - bent * bent) * (
            1.0 + 3.0 * 0.044715 * square
        )
        value = 0.5 * hidden * (1.0 + bent)
        for j in range(CHIPS):
            part = slice(j * tokens, (j + 1) * tokens)
            keep = mask_ref[j : j + 1, span]
            active_ref[part, span] = (value[part] * keep).astype(BF)
            slope_ref[part, span] = slope[part] * keep


def down_kernel(place, active_ref, grad_ref, *outs):
    chip, core = place[1], place[2]
    groups, cols, width = outs[0].shape
    grad = by_slot(grad_ref, chip)
    half = groups * cols
    for k, out_ref in enumerate(outs):
        low = pl.multiple_of((core ^ k) * half, 128)
        for at in range(0, width, WIDE):
            value = t_dot(active_ref[:, pl.ds(low, half)], grad[:, at : at + WIDE]).astype(BF)
            for g in range(groups):
                out_ref[g, :, at : at + WIDE] = value[g * cols : (g + 1) * cols]


def reverse_kernel(*refs):
    place, grads_ref, slope_ref, near2, far2 = refs[:5]
    weights = refs[5:-10]
    grad_ref, sum_ref, own_ref = refs[-10:-7]
    sent = refs[-7:-4]
    w1_ref, w2_ref, sems1, sems2 = refs[-4:]
    second = place_second((near2, far2), w2_ref, sems2, place[0], place[2])
    first = place_first(weights, w1_ref, sems1, place[0], place[2])
    tokens = grads_ref.shape[1]
    grad = by_slot(grads_ref, place[1])
    for copy in second:
        copy.wait()
    for low in range(0, w2_ref.shape[0], WIDE):
        span = slice(low, low + WIDE)
        value = (dot_t(grad, w2_ref[span, :]) * slope_ref[:, span]).astype(BF)
        grad_ref[:, span] = value
        sum_ref[:, span] = jnp.sum(value.astype(F32), axis=0, keepdims=True)
    for copy in first:
        copy.wait()
    for low in range(0, w1_ref.shape[0], WIDE):
        span = slice(low, low + WIDE)
        part = dot_t(grad_ref[...], w1_ref[span, :])
        own_ref[:, span] = part[:tokens]
        for j in range(1, CHIPS):
            sent[j - 1][:, span] = part[j * tokens : (j + 1) * tokens].astype(BF)


def finish_kernel(*refs):
    place, xs = refs[0], refs[1 : 1 + CHIPS]
    active_ref, grad_ref, near2, far2 = refs[1 + CHIPS : 5 + CHIPS]
    ups, (out_ref, w2_ref, sems) = refs[5 + CHIPS : -3], refs[-3:]
    second = place_second((near2, far2), w2_ref, sems, place[0], place[2])
    tokens, width = xs[0].shape
    step = width // CHIPS
    for low in range(0, width, step):
        x = jnp.concatenate([x[:, low : low + step] for x in xs], axis=0)
        put_rows(t_dot(x, grad_ref[...]).astype(BF), ups, low, place[2], slice(None))
    for copy in second:
        copy.wait()
    for low in range(0, width, WIDE):
        span = slice(low, low + WIDE)
        part = dot(active_ref[...], w2_ref[:, span])
        for j in range(CHIPS):
            out_ref[place[1] ^ j, :, span] = part[j * tokens : (j + 1) * tokens].astype(BF)


def mixed_kernel(
    own_ref, got1, got2, got3, mixed_ref, sens_ref, gain_ref, wo, v_ref, probs_ref,
    mixgrad_ref, cgrad_ref, vgrad_ref, pair_ref, norm_ref, shift_ref, w_ref, low_ref, sem
):
    copy = fetch(wo, w_ref, sem)
    normal, inverse = norm_stats(mixed_ref[...])
    second = own_ref[...] + got1[...].astype(F32) + got2[...].astype(F32) + got3[...].astype(F32)
    second = second.astype(BF).astype(F32)
    part, norm_sum, shift_sum = norm_back(second, gain_ref[...], normal, inverse)
    norm_ref[...], shift_ref[...] = norm_sum, shift_sum
    mixed_grad = sens_ref[...].astype(F32) + part
    mixgrad_ref[...] = mixed_grad
    low_ref[...] = mixed_grad.astype(BF)
    copy.wait()
    width = v_ref.shape[1]
    share = width // CHIPS
    for low in range(0, width, WIDE):
        cgrad_ref[:, low : low + WIDE] = dot_t(low_ref[...], w_ref[low : low + WIDE, :]).astype(BF)
    for h in range(width // HEAD_DIM):
        span = slice(h * HEAD_DIM, (h + 1) * HEAD_DIM)
        vgrad_ref[:, span] = t_dot(probs_ref[h].astype(BF), cgrad_ref[:, span]).astype(BF)
    for c in range(CHIPS):
        pair_ref[c, :, :share] = low_ref[:, c * share : (c + 1) * share]
        pair_ref[c, :, share:] = vgrad_ref[:, c * share : (c + 1) * share]


def score_kernel(
    place, cgrad_ref, q_ref, k_ref, v_ref, probs_ref, cos_ref, sin_ref, qgrad_ref, kgrad_ref, *pieces
):
    cosine, sine = cos_ref[...], -sin_ref[...]
    width = v_ref.shape[1]
    for h in range(width // HEAD_DIM):
        span = slice(h * HEAD_DIM, (h + 1) * HEAD_DIM)
        probs = probs_ref[h]
        probs_grad = dot_t(cgrad_ref[:, span], v_ref[:, span])
        inner = jnp.sum(probs_grad * probs, axis=-1, keepdims=True)
        scores_grad = (probs * (probs_grad - inner)).astype(BF)
        scale = HEAD_DIM**-0.5
        qgrad_ref[:, span] = turned(dot(scores_grad, k_ref[:, span]) * scale, cosine, sine).astype(BF)
        kgrad_ref[:, span] = turned(t_dot(scores_grad, q_ref[:, span]) * scale, cosine, sine).astype(BF)
    share = width // CHIPS
    for j, piece in enumerate(pieces):
        low = pl.multiple_of((place[1] ^ j) * share, HEAD_DIM)
        piece[:, :share] = kgrad_ref[:, pl.ds(low, share)]
        piece[:, share:] = qgrad_ref[:, pl.ds(low, share)]


def leading_kernel(
    qgrad_ref, kgrad_ref, vgrad_ref, x_ref, gain_ref, mixgrad_ref, wq, wk, wv,
    out_ref, norm_ref, shift_ref, w_ref, lead_ref, sems
):
    copies = [fetch(w, w_ref.at[i], sems.at[i]) for i, w in enumerate((wq, wk, wv))]
    normal, inverse = norm_stats(x_ref[...].astype(F32))
    for copy in copies:
        copy.wait()
    for low in range(0, x_ref.shape[1], WIDE):
        span = slice(low, low + WIDE)
        lead_ref[:, span] = (
            dot_t(qgrad_ref[...], w_ref[0, span, :])
            + dot_t(kgrad_ref[...], w_ref[1, span, :])
            + dot_t(vgrad_ref[...], w_ref[2, span, :])
        )
    part, norm_sum, shift_sum = norm_back(lead_ref[...], gain_ref[...], normal, inverse)
    norm_ref[...], shift_ref[...] = norm_sum, shift_sum
    out_ref[...] = (mixgrad_ref[...] + part).astype(BF)


def outer_into(lefts, rights, outs, core):
    width, share = lefts[0].shape[1], rights[0].shape[1]
    step = width // CHIPS
    for i, (left_ref, right) in enumerate(zip(lefts, rights)):
        for low in range(0, width, step):
            value = t_dot(left_ref[:, low : low + step], right).astype(BF)
            put_rows(value, outs, low, core, slice(i * share, (i + 1) * share))


def early_kernel(place, both_ref, right_ref, *refs):
    outs, lefts = refs[:-2], refs[-2:]
    tokens = right_ref.shape[1]
    for i, left_ref in enumerate(lefts):
        for j in range(CHIPS):
            left_ref[j * tokens : (j + 1) * tokens] = both_ref[j, (1 - i) * tokens : (2 - i) * tokens]
    right = right_ref[...].reshape(CHIPS * tokens, right_ref.shape[2])
    share = right.shape[1] // 2
    outer_into(lefts, (right[:, :share], right[:, share:]), outs, place[2])


def late_kernel(place, both_ref, *refs):
    pieces, outs, left_ref = refs[:CHIPS], refs[CHIPS:-1], refs[-1]
    tokens = pieces[0].shape[0]
    for j in range(CHIPS):
        left_ref[j * tokens : (j + 1) * tokens] = both_ref[place[1] ^ j, :tokens]
    right = jnp.concatenate([piece[...] for piece in pieces], axis=0)
    outer_into((left_ref,), (right,), outs, place[2])


def per_device(
    sequence_elements,
    result_sensitivity,
    mixer_gain,
    mixer_offset,
    question_matrix,
    lookup_matrix,
    content_matrix,
    mixer_projection_matrix,
    feedforward_gain,
    feedforward_offset,
    expand_matrix,
    inner_neuron_offset,
    contract_matrix,
    feedforward_result_offset,
    sequence_level_choice,
    servers_per_level,
    accepted_row_limit,
    server_selection,
):
    devices = lax.axis_size("dp")
    me = lax.axis_index("dp")
    groups = devices // GROUP
    z, chip, core = me // GROUP, me % GROUP // 2, me % 2
    tokens, width = sequence_elements.shape
    heads = width // HEAD_DIM
    rows, feed = expand_matrix.shape
    cols = contract_matrix.shape[0]
    offset_len = feedforward_result_offset.shape[0]
    levels = jnp.arange(LEVELS)
    block = 2 * cols
    units = groups * block
    gain_first, shift_first, gain_second, shift_second = (
        v.astype(F32)[None, :] for v in (mixer_gain, mixer_offset, feedforward_gain, feedforward_offset)
    )
    cosine, sine = (jnp.asarray(t) for t in rope_tables(tokens))
    flat, wide = (tokens, width), (1, width)
    square = (width, width)
    all_rows = (CHIPS * tokens, units)
    weight_space = pltpu.VMEM(square, BF)
    triple_space = pltpu.VMEM((3,) + square, BF)
    hidden_space = pltpu.VMEM((width, units), BF)
    dma, dmas = pltpu.SemaphoreType.DMA, pltpu.SemaphoreType.DMA((3,))
    aligned = rows % 16 == 0
    firsts = pltpu.SemaphoreType.DMA((2 * groups * CHIPS if aligned else 1,))
    seconds = pltpu.SemaphoreType.DMA((2 * groups,))
    place = jnp.stack([z, chip, core]).astype(jnp.int32)
    fence = lax.optimization_barrier

    expand_chunks = expand_matrix.reshape(rows, groups, CHIPS, 2, cols).transpose(2, 0, 3, 1, 4)
    expand_pieces = exchange(expand_chunks.reshape(CHIPS, rows, units))
    contract_steps = [line_step(None, contract_matrix, 1)]
    normed_first, query_rot, key_rot, value_rows = call(
        project_kernel,
        [(flat, BF)] * 4,
        (sequence_elements, gain_first, shift_first, cosine, sine, question_matrix, lookup_matrix, content_matrix),
        [VMEM] * 5 + [ANY] * 3,
        [triple_space, dmas], micros=8)
    normed_first, query_rot, key_rot, value_rows, expand_pieces = fence(
        (normed_first, query_rot, key_rot, value_rows, expand_pieces)
    )

    expand_plane = jnp.concatenate(in_order(expand_pieces), axis=0)
    expand_steps = [line_step(None, expand_plane, 1)]
    both_rows, mixed, normed_second, probs = call(
        attend_kernel,
        [((2 * tokens, width), BF), (flat, F32), (flat, BF), ((heads, tokens, tokens), F32)],
        (
            query_rot, key_rot, value_rows, sequence_elements, gain_second, shift_second, normed_first,
            mixer_projection_matrix,
        ),
        [VMEM] * 7 + [ANY],
        [weight_space, dma], micros=6)
    both_rows, mixed, normed_second, contract_steps = fence((both_rows, mixed, normed_second, contract_steps))

    row_slots = spread(normed_second)
    expand_steps, _ = fence((expand_steps, normed_second))
    expand_steps.append(line_step(expand_steps[-1], expand_plane, 2))
    level = sequence_level_choice[0]
    choice = server_selection.reshape(-1)
    info = jnp.concatenate(
        [
            feedforward_result_offset.astype(F32),
            inner_neuron_offset.astype(F32),
            level.astype(F32)[None],
            jnp.min(choice).astype(F32)[None],
        ]
    )
    info = jnp.pad(info, (0, -info.shape[0] % 128))
    table = after(jnp.broadcast_to(info, (devices, 1) + info.shape), row_slots[1])
    table = lax.all_to_all(table, "dp", 0, 0, tiled=True).reshape(devices, -1)
    for s in range(3, groups):
        expand_steps.append(line_step(expand_steps[-1], expand_plane, s))
    result_offset = table[:, :offset_len].reshape(-1)
    hidden_offsets = table[:, offset_len : offset_len + cols]
    all_levels = table[:, offset_len + cols].astype(jnp.int32)
    all_lowest = table[:, offset_len + cols + 1].astype(jnp.int32)
    size = jnp.sum(jnp.where(levels == level, servers_per_level, 0))
    limit = jnp.sum(jnp.where(levels == level, accepted_row_limit, 0))
    server = choice % size
    before = jnp.arange(tokens)[None, :] < jnp.arange(tokens)[:, None]
    local = jnp.sum((before & (server[None, :] == server[:, None])).astype(jnp.int32), axis=1)
    low = all_lowest[None, :]
    seen = (low + tokens - 1 - server[:, None] + size) // size - (low - 1 - server[:, None] + size) // size
    earlier = (jnp.arange(devices) < me) & (all_levels == level)
    arrival = local + jnp.sum(jnp.where(earlier[None, :], seen, 0), axis=1)
    kept = (arrival < limit).astype(F32)[:, None]
    kept_sensitivity = (result_sensitivity.astype(F32) * kept).astype(BF)
    slot_levels = jnp.take(all_levels, me ^ (2 * jnp.arange(CHIPS)))
    starts = (jnp.arange(groups) * CHIPS + chip) * block
    active_block = starts[None, :] < (feed // 8) * (1 << slot_levels[:, None])
    mask = jnp.tile(jnp.repeat(active_block.astype(F32), cols, axis=1), (1, 2))
    hidden_offset = lax.dynamic_index_in_dim(
        hidden_offsets.reshape(groups, CHIPS, 2, cols), chip, 1, keepdims=False
    )
    hidden_offset = hidden_offset.transpose(1, 0, 2).reshape(1, -1)
    row_slots, kept_sensitivity = fence((row_slots, kept_sensitivity))
    group_grad = share_out(kept_sensitivity)
    group_both = lax.all_gather(after(both_rows, row_slots), "dp", axis_index_groups=quads())
    expand_steps, kept_sensitivity = fence((expand_steps, kept_sensitivity))
    expand_mine = line_stack(expand_plane, expand_steps)
    expand_other = swap(expand_mine, 1)
    contract_steps[0] = after(contract_steps[0], expand_mine)
    for s in range(2, groups):
        contract_steps.append(line_step(contract_steps[-1], contract_matrix, s))
    if aligned:
        first_weight = (expand_mine, expand_other)
    else:
        pair = jnp.stack([expand_mine, expand_other]).reshape(2, groups, CHIPS, rows, units)
        pair = jnp.take(pair, (jnp.arange(groups) - z) % groups, axis=1)
        first_weight = (jnp.where(core == 0, pair, pair[::-1]).transpose(1, 2, 0, 3, 4).reshape(width, units),)

    active, slope = call(
        hidden_kernel,
        [(all_rows, BF), (all_rows, F32)],
        (place, *row_slots, hidden_offset, mask, *first_weight),
        [SMEM] + [VMEM] * (CHIPS + 2) + [ANY] * len(first_weight),
        [hidden_space, firsts], micros=1)
    if groups > 2:
        active, contract_steps[1] = fence((active, contract_steps[1]))
        for s in range(3, groups):
            contract_steps[s - 1] = line_step(contract_steps[s - 2], contract_matrix, s)
    sides = 2 if aligned else 1
    down_mine, down_other = call(
        down_kernel, [((groups, cols, width), BF)] * 2, (place, active, group_grad), [SMEM] + [VMEM] * 2, micros=8
    )
    down_mine, down_other, contract_steps = fence((down_mine, down_other, contract_steps))
    down_got = swap(down_other, 1)
    contract_mine = line_stack(contract_matrix, contract_steps)
    contract_other = swap(contract_mine, 1)
    hidden_grad, hidden_sum, second_own, *second_sent = call(
        reverse_kernel,
        [(all_rows, BF), ((1, units), F32), (flat, F32)] + [(flat, BF)] * 3,
        (place, group_grad, slope, contract_mine, contract_other, *first_weight),
        [SMEM] + [VMEM] * 2 + [ANY] * (2 + len(first_weight)),
        [hidden_space, pltpu.VMEM((units, width), BF), firsts, seconds],
        micros=15,
    )
    hidden_grad, second_sent, down_got = fence((hidden_grad, second_sent, down_got))
    second_got = [swap(second_sent[j - 1], 2 * j) for j in range(1, CHIPS)]
    contract_both = (down_mine.astype(F32) + down_got.astype(F32)).astype(BF)
    share_contract = lax.psum_scatter(contract_both, "dp", scatter_dimension=0, axis_index_groups=lines())
    half_shape = (groups, CHIPS * rows) if aligned else (width,)
    *up_part, branch_sent = call(
        finish_kernel,
        [(half_shape + (units,), BF)] * sides + [((CHIPS,) + flat, BF)],
        (place, *row_slots, active, hidden_grad, contract_mine, contract_other),
        [SMEM] + [VMEM] * (CHIPS + 2) + [ANY] * 2,
        [pltpu.VMEM((units, width), BF), seconds],
        micros=13,
    )
    up_part, second_got, contract_both = fence((up_part, second_got, contract_both))

    def by_sides(parts):
        if aligned:
            return parts
        part = parts[0].reshape(groups, CHIPS, 2, rows, -1)
        return [
            lax.dynamic_index_in_dim(part, core ^ k, 2, keepdims=False).reshape(groups, CHIPS * rows, -1)
            for k in range(2)
        ]

    def add(mine, got):
        return (mine.astype(F32) + got.astype(F32)).astype(BF)

    up_mine, up_other = by_sides(up_part)
    up_got = swap(up_other, 1)

    share = width // CHIPS
    pair_shape = (tokens, 2 * share)
    mixed_grad, context_grad, value_grad, first_pair, midnorm_sum, midshift_sum = call(
        mixed_kernel,
        [(flat, F32), (flat, BF), (flat, BF), ((CHIPS,) + pair_shape, BF), (wide, F32), (wide, F32)],
        (
            second_own, *second_got, mixed, result_sensitivity, gain_second, mixer_projection_matrix,
            value_rows, probs,
        ),
        [VMEM] * 7 + [ANY] + [VMEM] * 2,
        [weight_space, pltpu.VMEM(flat, BF), dma],
        micros=8,
    )
    first_pair, context_grad, value_grad, up_got = fence((first_pair, context_grad, value_grad, up_got))
    first_pair = trade(first_pair)
    query_grad, key_grad, *second_pair = call(
        score_kernel,
        [(flat, BF)] * 2 + [(pair_shape, BF)] * CHIPS,
        (place, context_grad, query_rot, key_rot, value_rows, probs, cosine, sine),
        [SMEM] + [VMEM] * 7,
        micros=1,
    )
    expand_both = add(up_mine, after(up_got, query_grad))
    expand_rows = lax.psum_scatter(expand_both, "dp", scatter_dimension=0, axis_index_groups=lines())
    second_pair = [piece if j == 0 else swap(piece, 2 * j) for j, piece in enumerate(second_pair)]
    query_grad, key_grad, first_pair, group_both, expand_both = fence(
        (query_grad, key_grad, first_pair, group_both, expand_both)
    )

    outer_shape = [(half_shape + (2 * share,), BF)] * sides
    left_space = pltpu.VMEM((CHIPS * tokens, width), BF)
    early = call(
        early_kernel, outer_shape, (place, group_both, first_pair), [SMEM] + [VMEM] * 2, [left_space] * 2, micros=6
    )
    early_mine, early_other = by_sides(early)
    early_both = add(early_mine, swap(early_other, 1))
    early_both, query_grad = fence((early_both, query_grad))
    early_sum = lax.psum_scatter(early_both, "dp", scatter_dimension=0, axis_index_groups=lines())
    layer_input_gradient, leadnorm_sum, leadshift_sum = call(
        leading_kernel,
        [(flat, BF), (wide, F32), (wide, F32)],
        (
            query_grad, key_grad, value_grad, sequence_elements, gain_first, mixed_grad,
            question_matrix, lookup_matrix, content_matrix,
        ),
        [VMEM] * 6 + [ANY] * 3,
        [triple_space, pltpu.VMEM(flat, F32), dmas],
        micros=13,
    )
    leadnorm_sum, second_pair = fence((leadnorm_sum, second_pair))
    late = call(
        late_kernel, outer_shape, (place, group_both, *second_pair), [SMEM] + [VMEM] * 5, [left_space], micros=1
    )
    late_mine, late_other = by_sides(late)
    branch = jnp.sum(trade(after(branch_sent, leadnorm_sum)).astype(F32), axis=0)
    late_both = add(late_mine, swap(late_other, 1))
    late_sum = line_sum(
        [lax.dynamic_index_in_dim(late_both, (z + s) % groups, 0, keepdims=False) for s in range(groups)]
    )
    branch = (branch + result_offset).astype(BF).astype(F32)
    layer_output = (mixed + kept * branch).astype(BF)

    def home(summed):
        return trade(summed.astype(BF).reshape(CHIPS, rows, -1))

    hidden_spot = (jnp.arange(CHIPS)[None, :, None, None] == chip).astype(F32)
    hidden_full = hidden_spot * hidden_sum.reshape(2, groups, cols).transpose(1, 0, 2)[:, None]
    result_sum = jnp.sum(kept_sensitivity.astype(F32), axis=0)
    vectors = [midnorm_sum, midshift_sum, leadnorm_sum, leadshift_sum, result_sum, hidden_full]
    vectors = jnp.concatenate([vector.reshape(devices, -1) for vector in vectors], axis=1)
    vectors = jnp.pad(vectors, ((0, 0), (0, -vectors.shape[1] % 128)))
    vectors = after(vectors, late_both)
    vectors = scatter_all(vectors.reshape(devices, -1, 128)).reshape(-1)
    small = [vectors[i * offset_len : (i + 1) * offset_len] for i in range(5)]
    share_hidden = vectors[5 * offset_len : 5 * offset_len + cols]

    expand_home = home(after(expand_rows, layer_output))
    share_expand = (
        expand_home.reshape(CHIPS, rows, 2, groups, cols).transpose(1, 3, 0, 2, 4).reshape(rows, feed).astype(F32)
    )
    last = jnp.concatenate([early_sum, after(late_sum.astype(BF), expand_home)], axis=1)
    last = home(last)

    def join(at):
        piece = last[:, :, at * share : (at + 1) * share]
        return piece.transpose(1, 0, 2).reshape(rows, width).astype(F32)

    share_mixing, share_value, share_key, share_query = (join(at) for at in range(4))
    return (
        layer_output,
        layer_input_gradient,
        small[2],
        small[3],
        share_query,
        share_key,
        share_value,
        share_mixing,
        small[0],
        small[1],
        share_expand,
        share_hidden,
        share_contract.astype(F32),
        small[4],
    )


def solution(mesh):
    split, line, whole = P("dp", None), P("dp"), P()
    return jax.shard_map(
        per_device,
        mesh=mesh,
        in_specs=(split, split) + (whole,) * 8 + (split, line, split, line, line, whole, whole, split),
        out_specs=(split, split, line, line, split, split, split, split, line, line, split, line, split, line),
        check_vma=False,
    )
```

```python
import jax
import jax.numpy as jnp
import numpy as np
from jax import lax
from jax.experimental import pallas as pl
from jax.experimental.pallas import tpu as pltpu
from jax.sharding import PartitionSpec as P

HEAD_DIM = 128
LEVELS = 4
GROUP = 8
CHIPS = 4
EPSILON = 1e-05
NEGATIVE = -1e30
BF = jnp.bfloat16
F32 = jnp.float32
WIDE = 512
SPACE = 6
PIECES = 7
VMEM_BYTES = 56 * 1024 * 1024


def dot(left, right, dims=((1,), (0,))):
    return lax.dot_general(left, right, (dims, ((), ())), preferred_element_type=F32)


def dot_t(left, right):
    return dot(left, right, ((1,), (1,)))


def t_dot(left, right):
    return dot(left, right, ((0,), (0,)))


def rope_tables(length):
    half = HEAD_DIM // 2
    rates = (10000.0 ** (-(np.arange(half, dtype=np.float64) * 2.0 / HEAD_DIM))).astype(np.float32)
    angles = np.arange(length, dtype=np.float32)[:, None] * rates[None, :]
    cosine, sine = np.cos(angles).astype(np.float32), np.sin(angles).astype(np.float32)
    return np.concatenate([cosine, cosine], axis=1), np.concatenate([-sine, sine], axis=1)


def norm_stats(values):
    center = values - jnp.mean(values, axis=-1, keepdims=True)
    inverse = lax.rsqrt(jnp.mean(center * center, axis=-1, keepdims=True) + EPSILON)
    return center * inverse, inverse


def norm_back(incoming, gain, normal, inverse):
    scaled = incoming * gain
    part = inverse * (
        scaled
        - jnp.mean(scaled, axis=-1, keepdims=True)
        - normal * jnp.mean(scaled * normal, axis=-1, keepdims=True)
    )
    return part, jnp.sum(incoming * normal, axis=0, keepdims=True), jnp.sum(incoming, axis=0, keepdims=True)


def swap(value, bit):
    count = lax.axis_size("dp")
    return lax.ppermute(value, "dp", [(i, i ^ bit) for i in range(count)])


def hop(value, step, near, far):
    groups = lax.axis_size("dp") // GROUP
    pairs = [
        (z * GROUP + t, (z + step) * GROUP + t)
        for z in range(max(near, 0), min(far, groups))
        if 0 <= z + step < groups
        for t in range(GROUP)
    ]
    return lax.ppermute(value, "dp", pairs)


def scatter_all(parts):
    count = lax.axis_size("dp")
    parts = jnp.take(parts, lax.axis_index("dp") ^ jnp.arange(count), axis=0)
    bit = count // 2
    while bit:
        parts = parts[:bit] + swap(parts[bit:], bit)
        bit //= 2
    return parts


def lines():
    groups = lax.axis_size("dp") // GROUP
    return [[z * GROUP + t for z in range(groups)] for t in range(GROUP)]


def spread(own):
    return [own, swap(own, 2), swap(own, 4), swap(own, 6)]


def exchange(chunks):
    chip = lax.axis_index("dp") % GROUP // 2
    got = []
    for j in range(CHIPS):
        chunk = lax.dynamic_index_in_dim(chunks, chip ^ j, 0, keepdims=False)
        got.append(chunk if j == 0 else swap(chunk, 2 * j))
    return got


def quads():
    count = lax.axis_size("dp")
    return [
        [first + 2 * c + core for c in range(CHIPS)] for first in range(0, count, GROUP) for core in range(2)
    ]


def trade(chunks):
    return lax.all_to_all(chunks, "dp", 0, 0, tiled=True, axis_index_groups=quads())


def share_out(own):
    return trade(jnp.broadcast_to(own, (CHIPS,) + own.shape))


def in_order(slots):
    chip = lax.axis_index("dp") % GROUP // 2
    odd, high = chip % 2 == 1, chip // 2 == 1
    a, b, c, d = slots
    a, b, c, d = jnp.where(odd, b, a), jnp.where(odd, a, b), jnp.where(odd, d, c), jnp.where(odd, c, d)
    return [jnp.where(high, c, a), jnp.where(high, d, b), jnp.where(high, a, c), jnp.where(high, b, d)]


def line_step(sides, own, s):
    groups = lax.axis_size("dp") // GROUP
    up, down = sides if s > 1 else (own, own)
    return hop(up, 1, s - 1, groups - 1), hop(down, -1, 1, groups - s + 1)


def line_stack(own, steps):
    groups = lax.axis_size("dp") // GROUP
    z = lax.axis_index("dp") // GROUP
    return jnp.stack(
        [own]
        + [jnp.where(z + s < groups, steps[s - 1][1], steps[groups - s - 1][0]) for s in range(1, groups)]
    )


def line_sum(parts):
    groups = lax.axis_size("dp") // GROUP
    total = parts[0].astype(F32)
    for s in range(1, groups):
        pairs = [
            (z * GROUP + t, (z + s) % groups * GROUP + t) for z in range(groups) for t in range(GROUP)
        ]
        total = total + lax.ppermute(parts[s].astype(BF), "dp", pairs).astype(F32)
    return total


def after(value, *others):
    return lax.optimization_barrier((value,) + others)[0]


def core_sum(mine, other):
    return mine + swap(other.astype(BF), 1).astype(F32)


ANY = pl.BlockSpec(memory_space=pl.ANY)
VMEM = pl.BlockSpec(memory_space=pltpu.VMEM)
SMEM = pl.BlockSpec(memory_space=pltpu.SMEM)


def call(kernel, outs, args, places, scratch=(), micros=1):
    return pl.pallas_call(
        kernel,
        out_shape=tuple(jax.ShapeDtypeStruct(shape, kind) for shape, kind in outs),
        in_specs=list(places),
        out_specs=tuple(VMEM for _ in outs),
        scratch_shapes=list(scratch),
        compiler_params=pltpu.CompilerParams(vmem_limit_bytes=VMEM_BYTES),
        cost_estimate=pl.CostEstimate(flops=micros * 1000000000, bytes_accessed=1000, transcendentals=0),
    )(*args)


def fetch(source, target, sem):
    copy = pltpu.make_async_copy(source, target, sem)
    copy.start()
    return copy


def turned(values, cosine, sine):
    return values * cosine + pltpu.roll(values, HEAD_DIM // 2, 1) * sine


def pass_kernel(in_ref, out_ref):
    out_ref[...] = in_ref[...]


def pause(mark, *others):
    (mark,) = call(pass_kernel, [(mark.shape, mark.dtype)], (mark,), [VMEM], micros=SPACE)
    return lax.optimization_barrier((mark,) + others)


def project_kernel(
    x_ref, gain_ref, shift_ref, cos_ref, sin_ref, wq, wk, wv, normed_ref, q_ref, k_ref, v_ref, w_ref, sems
):
    copies = [fetch(w, w_ref.at[i], sems.at[i]) for i, w in enumerate((wq, wk, wv))]
    normal, _ = norm_stats(x_ref[...].astype(F32))
    normed_ref[...] = (normal * gain_ref[...] + shift_ref[...]).astype(BF)
    cosine, sine = cos_ref[...], sin_ref[...]
    for i, out in enumerate((q_ref, k_ref, v_ref)):
        copies[i].wait()
        for low in range(0, out.shape[1], WIDE):
            raw = dot(normed_ref[...], w_ref[i, :, low : low + WIDE])
            for h in range(0, WIDE, HEAD_DIM):
                head = raw[:, h : h + HEAD_DIM]
                if i < 2:
                    head = turned(head, cosine, sine)
                out[:, low + h : low + h + HEAD_DIM] = head.astype(BF)


def attend_kernel(
    q_ref, k_ref, v_ref, x_ref, gain_ref, shift_ref, first_ref, wo,
    both_ref, mixed_ref, normed_ref, probs_ref, w_ref, sem
):
    copy = fetch(wo, w_ref, sem)
    tokens, width = q_ref.shape
    both_ref[:tokens] = first_ref[...]
    row = lax.broadcasted_iota(jnp.int32, (tokens, tokens), 0)
    causal = row >= lax.broadcasted_iota(jnp.int32, (tokens, tokens), 1)
    for h in range(width // HEAD_DIM):
        span = slice(h * HEAD_DIM, (h + 1) * HEAD_DIM)
        scores = dot_t(q_ref[:, span], k_ref[:, span]) * HEAD_DIM**-0.5
        scores = jnp.where(causal, scores, NEGATIVE)
        weight = jnp.exp(scores - jnp.max(scores, axis=-1, keepdims=True))
        probs = weight / jnp.sum(weight, axis=-1, keepdims=True)
        probs_ref[h] = probs
        both_ref[tokens:, span] = dot(probs.astype(BF), v_ref[:, span]).astype(BF)
    copy.wait()
    for low in range(0, width, WIDE):
        span = slice(low, low + WIDE)
        mixed_ref[:, span] = x_ref[:, span].astype(F32) + dot(both_ref[tokens:], w_ref[:, span])
    normal, _ = norm_stats(mixed_ref[...])
    normed_ref[...] = (normal * gain_ref[...] + shift_ref[...]).astype(BF)


def place_first(weights, w_ref, sems, z, core):
    if len(weights) == 1:
        return [fetch(weights[0], w_ref, sems.at[0])]
    groups, rows = weights[0].shape[0], weights[0].shape[1] // CHIPS
    copies = []
    for k, source in enumerate(weights):
        side = core if k == 0 else 1 - core
        for g in range(groups):
            for c in range(CHIPS):
                low = pl.multiple_of(((lax.rem(z + g, groups) * CHIPS + c) * 2 + side) * rows, 16)
                copies.append(
                    fetch(
                        source.at[g, c * rows : (c + 1) * rows],
                        w_ref.at[pl.ds(low, rows)],
                        sems.at[len(copies)],
                    )
                )
    return copies


def place_second(weights, w_ref, sems, z, core):
    groups, cols, _ = weights[0].shape
    copies = []
    for k, source in enumerate(weights):
        side = core if k == 0 else 1 - core
        for g in range(groups):
            low = pl.multiple_of((side * groups + lax.rem(z + g, groups)) * cols, 16)
            copies.append(fetch(source.at[g], w_ref.at[pl.ds(low, cols)], sems.at[len(copies)]))
    return copies


def by_slot(array_ref, chip):
    return jnp.concatenate([array_ref[chip ^ j] for j in range(CHIPS)], axis=0)


def put_rows(value, outs, low, core, at):
    if len(outs) == 1:
        outs[0][low : low + value.shape[0], at] = value
        return
    rows = outs[0].shape[1] // CHIPS
    for pair in range(value.shape[0] // rows // 2):
        g, c = divmod(low // rows // 2 + pair, CHIPS)
        first = value[2 * pair * rows : (2 * pair + 1) * rows]
        second = value[(2 * pair + 1) * rows : (2 * pair + 2) * rows]
        spot = slice(c * rows, (c + 1) * rows)
        outs[0][g, spot, at] = jnp.where(core == 0, first, second)
        outs[1][g, spot, at] = jnp.where(core == 0, second, first)


def hidden_kernel(*refs):
    place, xs = refs[0], refs[1 : 1 + PIECES]
    bias_ref, mask_ref = refs[1 + PIECES : 3 + PIECES]
    weights = refs[3 + PIECES : -4]
    active_ref, slope_ref, w_ref, sems = refs[-4:]
    copies = place_first(weights, w_ref, sems, place[0], place[2])
    x = jnp.concatenate([x[...] for x in xs], axis=0)
    tokens = xs[0].shape[0]
    for copy in copies:
        copy.wait()
    for low in range(0, w_ref.shape[1], WIDE):
        span = slice(low, low + WIDE)
        hidden = dot(x, w_ref[:, span]) + bias_ref[:, span]
        square = hidden * hidden
        bent = jnp.tanh(0.7978845608 * hidden * (1.0 + 0.044715 * square))
        slope = 0.5 * (1.0 + bent) + (0.5 * 0.7978845608) * hidden * (1.0 - bent * bent) * (
            1.0 + 3.0 * 0.044715 * square
        )
        value = 0.5 * hidden * (1.0 + bent)
        for j in range(CHIPS):
            part = slice(j * tokens, (j + 1) * tokens)
            keep = mask_ref[j : j + 1, span]
            active_ref[part, span] = (value[part] * keep).astype(BF)
            slope_ref[part, span] = slope[part] * keep


def down_kernel(place, active_ref, grad_ref, kept_ref, *outs):
    chip, core = place[1], place[2]
    groups, cols, width = outs[0].shape
    grad = by_slot(grad_ref, chip) * kept_ref[...].astype(BF)
    half = groups * cols
    for k, out_ref in enumerate(outs):
        low = pl.multiple_of((core ^ k) * half, 128)
        for at in range(0, width, WIDE):
            value = t_dot(active_ref[:, pl.ds(low, half)], grad[:, at : at + WIDE]).astype(BF)
            for g in range(groups):
                out_ref[g, :, at : at + WIDE] = value[g * cols : (g + 1) * cols]


def reverse_kernel(*refs):
    place, grads_ref, kept_ref, slope_ref, near2, far2 = refs[:6]
    weights = refs[6:-10]
    grad_ref, sum_ref, own_ref = refs[-10:-7]
    sent = refs[-7:-4]
    w1_ref, w2_ref, sems1, sems2 = refs[-4:]
    second = place_second((near2, far2), w2_ref, sems2, place[0], place[2])
    first = place_first(weights, w1_ref, sems1, place[0], place[2])
    tokens = grads_ref.shape[1]
    grad = by_slot(grads_ref, place[1]) * kept_ref[...].astype(BF)
    for copy in second:
        copy.wait()
    for low in range(0, w2_ref.shape[0], WIDE):
        span = slice(low, low + WIDE)
        value = (dot_t(grad, w2_ref[span, :]) * slope_ref[:, span]).astype(BF)
        grad_ref[:, span] = value
        sum_ref[:, span] = jnp.sum(value.astype(F32), axis=0, keepdims=True)
    for copy in first:
        copy.wait()
    for low in range(0, w1_ref.shape[0], WIDE):
        span = slice(low, low + WIDE)
        part = dot_t(grad_ref[...], w1_ref[span, :])
        own_ref[:, span] = part[:tokens]
        for j in range(1, CHIPS):
            sent[j - 1][:, span] = part[j * tokens : (j + 1) * tokens].astype(BF)


def finish_kernel(*refs):
    place, xs = refs[0], refs[1 : 1 + PIECES]
    active_ref, grad_ref, near2, far2 = refs[1 + PIECES : 5 + PIECES]
    ups, (out_ref, w2_ref, sems) = refs[5 + PIECES : -3], refs[-3:]
    second = place_second((near2, far2), w2_ref, sems, place[0], place[2])
    tokens, width = xs[0].shape
    step = width // CHIPS
    for low in range(0, width, step):
        x = jnp.concatenate([x[:, low : low + step] for x in xs], axis=0)
        put_rows(t_dot(x, grad_ref[...]).astype(BF), ups, low, place[2], slice(None))
    for copy in second:
        copy.wait()
    for low in range(0, width, WIDE):
        span = slice(low, low + WIDE)
        part = dot(active_ref[...], w2_ref[:, span])
        for j in range(CHIPS):
            out_ref[place[1] ^ j, :, span] = part[j * tokens : (j + 1) * tokens].astype(BF)


def mixed_kernel(
    own_ref, got1, got2, got3, mixed_ref, sens_ref, gain_ref, wo, v_ref, probs_ref,
    mixgrad_ref, cgrad_ref, vgrad_ref, pair_ref, norm_ref, shift_ref, w_ref, low_ref, sem
):
    copy = fetch(wo, w_ref, sem)
    normal, inverse = norm_stats(mixed_ref[...])
    second = own_ref[...] + got1[...].astype(F32) + got2[...].astype(F32) + got3[...].astype(F32)
    second = second.astype(BF).astype(F32)
    part, norm_sum, shift_sum = norm_back(second, gain_ref[...], normal, inverse)
    norm_ref[...], shift_ref[...] = norm_sum, shift_sum
    mixed_grad = sens_ref[...].astype(F32) + part
    mixgrad_ref[...] = mixed_grad
    low_ref[...] = mixed_grad.astype(BF)
    copy.wait()
    width = v_ref.shape[1]
    share = width // CHIPS
    for low in range(0, width, WIDE):
        cgrad_ref[:, low : low + WIDE] = dot_t(low_ref[...], w_ref[low : low + WIDE, :]).astype(BF)
    for h in range(width // HEAD_DIM):
        span = slice(h * HEAD_DIM, (h + 1) * HEAD_DIM)
        vgrad_ref[:, span] = t_dot(probs_ref[h].astype(BF), cgrad_ref[:, span]).astype(BF)
    for c in range(CHIPS):
        pair_ref[c, :, :share] = low_ref[:, c * share : (c + 1) * share]
        pair_ref[c, :, share:] = vgrad_ref[:, c * share : (c + 1) * share]


def score_kernel(
    place, cgrad_ref, q_ref, k_ref, v_ref, probs_ref, cos_ref, sin_ref, qgrad_ref, kgrad_ref, *pieces
):
    cosine, sine = cos_ref[...], -sin_ref[...]
    width = v_ref.shape[1]
    for h in range(width // HEAD_DIM):
        span = slice(h * HEAD_DIM, (h + 1) * HEAD_DIM)
        probs = probs_ref[h]
        probs_grad = dot_t(cgrad_ref[:, span], v_ref[:, span])
        inner = jnp.sum(probs_grad * probs, axis=-1, keepdims=True)
        scores_grad = (probs * (probs_grad - inner)).astype(BF)
        scale = HEAD_DIM**-0.5
        qgrad_ref[:, span] = turned(dot(scores_grad, k_ref[:, span]) * scale, cosine, sine).astype(BF)
        kgrad_ref[:, span] = turned(t_dot(scores_grad, q_ref[:, span]) * scale, cosine, sine).astype(BF)
    share = width // CHIPS
    for j, piece in enumerate(pieces):
        low = pl.multiple_of((place[1] ^ j) * share, HEAD_DIM)
        piece[:, :share] = kgrad_ref[:, pl.ds(low, share)]
        piece[:, share:] = qgrad_ref[:, pl.ds(low, share)]


def leading_kernel(
    qgrad_ref, kgrad_ref, vgrad_ref, x_ref, gain_ref, mixgrad_ref, wq, wk, wv,
    out_ref, norm_ref, shift_ref, w_ref, lead_ref, sems
):
    copies = [fetch(w, w_ref.at[i], sems.at[i]) for i, w in enumerate((wq, wk, wv))]
    normal, inverse = norm_stats(x_ref[...].astype(F32))
    for copy in copies:
        copy.wait()
    for low in range(0, x_ref.shape[1], WIDE):
        span = slice(low, low + WIDE)
        lead_ref[:, span] = (
            dot_t(qgrad_ref[...], w_ref[0, span, :])
            + dot_t(kgrad_ref[...], w_ref[1, span, :])
            + dot_t(vgrad_ref[...], w_ref[2, span, :])
        )
    part, norm_sum, shift_sum = norm_back(lead_ref[...], gain_ref[...], normal, inverse)
    norm_ref[...], shift_ref[...] = norm_sum, shift_sum
    out_ref[...] = (mixgrad_ref[...] + part).astype(BF)


def outer_into(lefts, rights, outs, core):
    width, share = lefts[0].shape[1], rights[0].shape[1]
    step = width // CHIPS
    for i, (left_ref, right) in enumerate(zip(lefts, rights)):
        for low in range(0, width, step):
            value = t_dot(left_ref[:, low : low + step], right).astype(BF)
            put_rows(value, outs, low, core, slice(i * share, (i + 1) * share))


def early_kernel(place, both_ref, right_ref, *refs):
    outs, lefts = refs[:-2], refs[-2:]
    tokens = right_ref.shape[1]
    for i, left_ref in enumerate(lefts):
        for j in range(CHIPS):
            left_ref[j * tokens : (j + 1) * tokens] = both_ref[j, (1 - i) * tokens : (2 - i) * tokens]
    right = right_ref[...].reshape(CHIPS * tokens, right_ref.shape[2])
    share = right.shape[1] // 2
    outer_into(lefts, (right[:, :share], right[:, share:]), outs, place[2])


def late_kernel(place, both_ref, *refs):
    pieces, outs, left_ref = refs[:CHIPS], refs[CHIPS:-1], refs[-1]
    tokens = pieces[0].shape[0]
    for j in range(CHIPS):
        left_ref[j * tokens : (j + 1) * tokens] = both_ref[place[1] ^ j, :tokens]
    right = jnp.concatenate([piece[...] for piece in pieces], axis=0)
    outer_into((left_ref,), (right,), outs, place[2])


def per_device(
    sequence_elements,
    result_sensitivity,
    mixer_gain,
    mixer_offset,
    question_matrix,
    lookup_matrix,
    content_matrix,
    mixer_projection_matrix,
    feedforward_gain,
    feedforward_offset,
    expand_matrix,
    inner_neuron_offset,
    contract_matrix,
    feedforward_result_offset,
    sequence_level_choice,
    servers_per_level,
    accepted_row_limit,
    server_selection,
):
    devices = lax.axis_size("dp")
    me = lax.axis_index("dp")
    groups = devices // GROUP
    z, chip, core = me // GROUP, me % GROUP // 2, me % 2
    tokens, width = sequence_elements.shape
    heads = width // HEAD_DIM
    rows, feed = expand_matrix.shape
    cols = contract_matrix.shape[0]
    offset_len = feedforward_result_offset.shape[0]
    levels = jnp.arange(LEVELS)
    block = 2 * cols
    units = groups * block
    gain_first, shift_first, gain_second, shift_second = (
        v.astype(F32)[None, :] for v in (mixer_gain, mixer_offset, feedforward_gain, feedforward_offset)
    )
    cosine, sine = (jnp.asarray(t) for t in rope_tables(tokens))
    flat, wide = (tokens, width), (1, width)
    square = (width, width)
    all_rows = (CHIPS * tokens, units)
    weight_space = pltpu.VMEM(square, BF)
    triple_space = pltpu.VMEM((3,) + square, BF)
    hidden_space = pltpu.VMEM((width, units), BF)
    dma, dmas = pltpu.SemaphoreType.DMA, pltpu.SemaphoreType.DMA((3,))
    aligned = rows % 16 == 0
    firsts = pltpu.SemaphoreType.DMA((2 * groups * CHIPS if aligned else 1,))
    seconds = pltpu.SemaphoreType.DMA((2 * groups,))
    place = jnp.stack([z, chip, core]).astype(jnp.int32)
    fence = lax.optimization_barrier

    expand_chunks = expand_matrix.reshape(rows, groups, CHIPS, 2, cols).transpose(2, 0, 3, 1, 4)
    expand_pieces = exchange(expand_chunks.reshape(CHIPS, rows, units))
    contract_steps = [line_step(None, contract_matrix, 1)]
    group_grad = share_out(result_sensitivity)
    normed_first, query_rot, key_rot, value_rows = call(
        project_kernel,
        [(flat, BF)] * 4,
        (sequence_elements, gain_first, shift_first, cosine, sine, question_matrix, lookup_matrix, content_matrix),
        [VMEM] * 5 + [ANY] * 3,
        [triple_space, dmas], micros=8)
    normed_first, query_rot, key_rot, value_rows, expand_pieces = fence(
        (normed_first, query_rot, key_rot, value_rows, expand_pieces)
    )

    expand_plane = jnp.concatenate(in_order(expand_pieces), axis=0)
    expand_steps = [line_step(None, expand_plane, 1)]
    both_rows, mixed, normed_second, probs = call(
        attend_kernel,
        [((2 * tokens, width), BF), (flat, F32), (flat, BF), ((heads, tokens, tokens), F32)],
        (
            query_rot, key_rot, value_rows, sequence_elements, gain_second, shift_second, normed_first,
            mixer_projection_matrix,
        ),
        [VMEM] * 7 + [ANY],
        [weight_space, dma], micros=6)
    both_rows, mixed, normed_second, contract_steps = fence((both_rows, mixed, normed_second, contract_steps))

    half = tokens // 2
    upper, lower = spread(normed_second[:half]), None
    mark = normed_second[:16, :128]
    expand_steps, _ = fence((expand_steps, normed_second))
    expand_steps.append(line_step(expand_steps[-1], expand_plane, 2))
    level = sequence_level_choice[0]
    choice = server_selection.reshape(-1)
    info = jnp.concatenate(
        [
            feedforward_result_offset.astype(F32),
            inner_neuron_offset.astype(F32),
            level.astype(F32)[None],
            jnp.min(choice).astype(F32)[None],
            choice.astype(F32),
        ]
    )
    info = jnp.pad(info, (0, -info.shape[0] % 128))
    mark, upper, expand_steps, group_grad = pause(mark, upper, expand_steps, group_grad)
    lower = spread(after(normed_second[half:], mark))
    for s in range(3, groups):
        expand_steps.append(line_step(expand_steps[-1], expand_plane, s))
    table = after(jnp.broadcast_to(info, (devices, 1) + info.shape), mark)
    table = lax.all_to_all(table, "dp", 0, 0, tiled=True).reshape(devices, -1)
    mark, lower, expand_steps, table = pause(mark, lower, expand_steps, table)
    result_offset = table[:, :offset_len].reshape(-1)
    hidden_offsets = table[:, offset_len : offset_len + cols]
    all_levels = table[:, offset_len + cols].astype(jnp.int32)
    all_lowest = table[:, offset_len + cols + 1].astype(jnp.int32)
    near = me ^ (2 * jnp.arange(CHIPS))
    slot_levels = jnp.take(all_levels, near)
    slot_choice = jnp.take(table[:, offset_len + cols + 2 :], near, axis=0)[:, :tokens].astype(jnp.int32)
    slot_hot = slot_levels[:, None] == levels[None, :]
    size = jnp.sum(jnp.where(slot_hot, servers_per_level[None, :], 0), axis=1)[:, None]
    limit = jnp.sum(jnp.where(slot_hot, accepted_row_limit[None, :], 0), axis=1)[:, None]
    server = slot_choice % size
    before = jnp.arange(tokens)[None, :] < jnp.arange(tokens)[:, None]
    same = before[None] & (server[:, None, :] == server[:, :, None])
    local = jnp.sum(same.astype(jnp.int32), axis=2)
    low = all_lowest[None, None, :]
    size, server = size[:, :, None], server[:, :, None]
    seen = (low + tokens - 1 - server + size) // size - (low - 1 - server + size) // size
    earlier = (jnp.arange(devices)[None, :] < near[:, None]) & (all_levels[None, :] == slot_levels[:, None])
    arrival = local + jnp.sum(jnp.where(earlier[:, None, :], seen, 0), axis=2)
    slot_kept = (arrival < limit).astype(F32)
    kept = slot_kept[0][:, None]
    slot_kept = slot_kept.reshape(-1, 1)
    kept_sensitivity = (result_sensitivity.astype(F32) * kept).astype(BF)
    starts = (jnp.arange(groups) * CHIPS + chip) * block
    active_block = starts[None, :] < (feed // 8) * (1 << slot_levels[:, None])
    mask = jnp.tile(jnp.repeat(active_block.astype(F32), cols, axis=1), (1, 2))
    hidden_offset = lax.dynamic_index_in_dim(
        hidden_offsets.reshape(groups, CHIPS, 2, cols), chip, 1, keepdims=False
    )
    hidden_offset = hidden_offset.transpose(1, 0, 2).reshape(1, -1)
    row_slots = [normed_second] + [piece for pair in zip(upper[1:], lower[1:]) for piece in pair]
    group_both = lax.all_gather(after(both_rows, lower), "dp", axis_index_groups=quads())
    expand_mine = line_stack(expand_plane, expand_steps)
    expand_other = swap(expand_mine, 1)
    contract_steps[0] = after(contract_steps[0], mark)
    contract_steps.append(line_step(contract_steps[-1], contract_matrix, 2))
    mark, expand_other, contract_steps = pause(mark, expand_other, contract_steps)
    for s in range(3, groups):
        contract_steps.append(line_step(contract_steps[-1], contract_matrix, s))
    if aligned:
        first_weight = (expand_mine, expand_other)
    else:
        pair = jnp.stack([expand_mine, expand_other]).reshape(2, groups, CHIPS, rows, units)
        pair = jnp.take(pair, (jnp.arange(groups) - z) % groups, axis=1)
        first_weight = (jnp.where(core == 0, pair, pair[::-1]).transpose(1, 2, 0, 3, 4).reshape(width, units),)

    active, slope = call(
        hidden_kernel,
        [(all_rows, BF), (all_rows, F32)],
        (place, *row_slots, hidden_offset, mask, *first_weight),
        [SMEM] + [VMEM] * (PIECES + 2) + [ANY] * len(first_weight),
        [hidden_space, firsts],
        micros=30,
    )
    active, contract_steps = fence((active, contract_steps))
    sides = 2 if aligned else 1
    down_mine, down_other = call(
        down_kernel, [((groups, cols, width), BF)] * 2, (place, active, group_grad, slot_kept), [SMEM] + [VMEM] * 3, micros=8
    )
    down_got = swap(down_other, 1)
    contract_mine = line_stack(contract_matrix, contract_steps)
    contract_other = swap(contract_mine, 1)
    contract_both = (down_mine.astype(F32) + down_got.astype(F32)).astype(BF)
    contract_both, contract_other = fence((contract_both, contract_other))
    share_contract = lax.psum_scatter(contract_both, "dp", scatter_dimension=0, axis_index_groups=lines())
    hidden_grad, hidden_sum, second_own, *second_sent = call(
        reverse_kernel,
        [(all_rows, BF), ((1, units), F32), (flat, F32)] + [(flat, BF)] * 3,
        (place, group_grad, slot_kept, slope, contract_mine, contract_other, *first_weight),
        [SMEM] + [VMEM] * 3 + [ANY] * (2 + len(first_weight)),
        [hidden_space, pltpu.VMEM((units, width), BF), firsts, seconds],
        micros=15,
    )
    hidden_grad, second_sent = fence((hidden_grad, second_sent))
    second_got = [swap(second_sent[j - 1], 2 * j) for j in range(1, CHIPS)]
    half_shape = (groups, CHIPS * rows) if aligned else (width,)
    *up_part, branch_sent = call(
        finish_kernel,
        [(half_shape + (units,), BF)] * sides + [((CHIPS,) + flat, BF)],
        (place, *row_slots, active, hidden_grad, contract_mine, contract_other),
        [SMEM] + [VMEM] * (PIECES + 2) + [ANY] * 2,
        [pltpu.VMEM((units, width), BF), seconds],
        micros=13,
    )
    up_part, second_got, group_both = fence((up_part, second_got, group_both))

    def by_sides(parts):
        if aligned:
            return parts
        part = parts[0].reshape(groups, CHIPS, 2, rows, -1)
        return [
            lax.dynamic_index_in_dim(part, core ^ k, 2, keepdims=False).reshape(groups, CHIPS * rows, -1)
            for k in range(2)
        ]

    def add(mine, got):
        return (mine.astype(F32) + got.astype(F32)).astype(BF)

    up_mine, up_other = by_sides(up_part)
    up_got = swap(up_other, 1)

    share = width // CHIPS
    pair_shape = (tokens, 2 * share)
    mixed_grad, context_grad, value_grad, first_pair, midnorm_sum, midshift_sum = call(
        mixed_kernel,
        [(flat, F32), (flat, BF), (flat, BF), ((CHIPS,) + pair_shape, BF), (wide, F32), (wide, F32)],
        (
            second_own, *second_got, mixed, result_sensitivity, gain_second, mixer_projection_matrix,
            value_rows, probs,
        ),
        [VMEM] * 7 + [ANY] + [VMEM] * 2,
        [weight_space, pltpu.VMEM(flat, BF), dma],
        micros=8,
    )
    expand_both = add(up_mine, up_got)
    first_pair, context_grad, value_grad, expand_both, share_contract = fence(
        (first_pair, context_grad, value_grad, expand_both, share_contract)
    )
    expand_rows = lax.psum_scatter(expand_both, "dp", scatter_dimension=0, axis_index_groups=lines())
    first_pair = trade(first_pair)
    query_grad, key_grad, *second_pair = call(
        score_kernel,
        [(flat, BF)] * 2 + [(pair_shape, BF)] * CHIPS,
        (place, context_grad, query_rot, key_rot, value_rows, probs, cosine, sine),
        [SMEM] + [VMEM] * 7,
        micros=1,
    )
    second_pair = [piece if j == 0 else swap(piece, 2 * j) for j, piece in enumerate(second_pair)]
    query_grad, key_grad, first_pair = fence((query_grad, key_grad, first_pair))

    outer_shape = [(half_shape + (2 * share,), BF)] * sides
    left_space = pltpu.VMEM((CHIPS * tokens, width), BF)
    early = call(
        early_kernel, outer_shape, (place, group_both, first_pair), [SMEM] + [VMEM] * 2, [left_space] * 2, micros=6
    )
    early_mine, early_other = by_sides(early)
    early_both = add(early_mine, swap(early_other, 1))
    early_both, query_grad = fence((early_both, query_grad))
    early_sum = lax.psum_scatter(early_both, "dp", scatter_dimension=0, axis_index_groups=lines())
    layer_input_gradient, leadnorm_sum, leadshift_sum = call(
        leading_kernel,
        [(flat, BF), (wide, F32), (wide, F32)],
        (
            query_grad, key_grad, value_grad, sequence_elements, gain_first, mixed_grad,
            question_matrix, lookup_matrix, content_matrix,
        ),
        [VMEM] * 6 + [ANY] * 3,
        [triple_space, pltpu.VMEM(flat, F32), dmas],
        micros=13,
    )
    leadnorm_sum, second_pair = fence((leadnorm_sum, second_pair))
    late = call(
        late_kernel, outer_shape, (place, group_both, *second_pair), [SMEM] + [VMEM] * 5, [left_space], micros=1
    )
    late_mine, late_other = by_sides(late)
    branch = jnp.sum(trade(after(branch_sent, leadnorm_sum)).astype(F32), axis=0)
    late_both = add(late_mine, swap(late_other, 1))
    late_sum = line_sum(
        [lax.dynamic_index_in_dim(late_both, (z + s) % groups, 0, keepdims=False) for s in range(groups)]
    )
    branch = (branch + result_offset).astype(BF).astype(F32)
    layer_output = (mixed + kept * branch).astype(BF)

    def home(summed):
        return trade(summed.astype(BF).reshape(CHIPS, rows, -1))

    hidden_spot = (jnp.arange(CHIPS)[None, :, None, None] == chip).astype(F32)
    hidden_full = hidden_spot * hidden_sum.reshape(2, groups, cols).transpose(1, 0, 2)[:, None]
    result_sum = jnp.sum(kept_sensitivity.astype(F32), axis=0)
    vectors = [midnorm_sum, midshift_sum, leadnorm_sum, leadshift_sum, result_sum, hidden_full]
    vectors = jnp.concatenate([vector.reshape(devices, -1) for vector in vectors], axis=1)
    vectors = jnp.pad(vectors, ((0, 0), (0, -vectors.shape[1] % 128)))
    vectors = scatter_all(vectors.reshape(devices, -1, 128)).reshape(-1)
    small = [vectors[i * offset_len : (i + 1) * offset_len] for i in range(5)]
    share_hidden = vectors[5 * offset_len : 5 * offset_len + cols]

    expand_home = home(after(expand_rows, layer_output))
    share_expand = (
        expand_home.reshape(CHIPS, rows, 2, groups, cols).transpose(1, 3, 0, 2, 4).reshape(rows, feed).astype(F32)
    )
    last = jnp.concatenate([early_sum, after(late_sum.astype(BF), expand_home)], axis=1)
    last = home(last)

    def join(at):
        piece = last[:, :, at * share : (at + 1) * share]
        return piece.transpose(1, 0, 2).reshape(rows, width).astype(F32)

    share_mixing, share_value, share_key, share_query = (join(at) for at in range(4))
    return (
        layer_output,
        layer_input_gradient,
        small[2],
        small[3],
        share_query,
        share_key,
        share_value,
        share_mixing,
        small[0],
        small[1],
        share_expand,
        share_hidden,
        share_contract.astype(F32),
        small[4],
    )


def solution(mesh):
    split, line, whole = P("dp", None), P("dp"), P()
    return jax.shard_map(
        per_device,
        mesh=mesh,
        in_specs=(split, split) + (whole,) * 8 + (split, line, split, line, line, whole, whole, split),
        out_specs=(split, split, line, line, split, split, split, split, line, line, split, line, split, line),
        check_vma=False,
    )
```

```python
import jax
import jax.numpy as jnp
import numpy as np
from jax import lax
from jax.experimental import pallas as pl
from jax.experimental.pallas import tpu as pltpu
from jax.sharding import PartitionSpec as P

HEAD_DIM = 128
LEVELS = 4
GROUP = 8
CHIPS = 4
EPSILON = 1e-05
NEGATIVE = -1e30
BF = jnp.bfloat16
F32 = jnp.float32
WIDE = 512
SPACE = 6
PIECES = 7
VMEM_BYTES = 56 * 1024 * 1024


def dot(left, right, dims=((1,), (0,))):
    return lax.dot_general(left, right, (dims, ((), ())), preferred_element_type=F32)


def dot_t(left, right):
    return dot(left, right, ((1,), (1,)))


def t_dot(left, right):
    return dot(left, right, ((0,), (0,)))


def rope_tables(length):
    half = HEAD_DIM // 2
    rates = (10000.0 ** (-(np.arange(half, dtype=np.float64) * 2.0 / HEAD_DIM))).astype(np.float32)
    angles = np.arange(length, dtype=np.float32)[:, None] * rates[None, :]
    cosine, sine = np.cos(angles).astype(np.float32), np.sin(angles).astype(np.float32)
    return np.concatenate([cosine, cosine], axis=1), np.concatenate([-sine, sine], axis=1)


def norm_stats(values):
    center = values - jnp.mean(values, axis=-1, keepdims=True)
    inverse = lax.rsqrt(jnp.mean(center * center, axis=-1, keepdims=True) + EPSILON)
    return center * inverse, inverse


def norm_back(incoming, gain, normal, inverse):
    scaled = incoming * gain
    part = inverse * (
        scaled
        - jnp.mean(scaled, axis=-1, keepdims=True)
        - normal * jnp.mean(scaled * normal, axis=-1, keepdims=True)
    )
    return part, jnp.sum(incoming * normal, axis=0, keepdims=True), jnp.sum(incoming, axis=0, keepdims=True)


def swap(value, bit):
    count = lax.axis_size("dp")
    return lax.ppermute(value, "dp", [(i, i ^ bit) for i in range(count)])


def hop(value, step, near, far):
    groups = lax.axis_size("dp") // GROUP
    pairs = [
        (z * GROUP + t, (z + step) * GROUP + t)
        for z in range(max(near, 0), min(far, groups))
        if 0 <= z + step < groups
        for t in range(GROUP)
    ]
    return lax.ppermute(value, "dp", pairs)


def scatter_all(parts):
    count = lax.axis_size("dp")
    parts = jnp.take(parts, lax.axis_index("dp") ^ jnp.arange(count), axis=0)
    bit = count // 2
    while bit:
        parts = parts[:bit] + swap(parts[bit:], bit)
        bit //= 2
    return parts


def lines():
    groups = lax.axis_size("dp") // GROUP
    return [[z * GROUP + t for z in range(groups)] for t in range(GROUP)]


def spread(own):
    return [own, swap(own, 2), swap(own, 4), swap(own, 6)]


def exchange(chunks):
    chip = lax.axis_index("dp") % GROUP // 2
    got = []
    for j in range(CHIPS):
        chunk = lax.dynamic_index_in_dim(chunks, chip ^ j, 0, keepdims=False)
        got.append(chunk if j == 0 else swap(chunk, 2 * j))
    return got


def bars():
    groups = lax.axis_size("dp") // GROUP
    return [[z * GROUP + 2 * c + core for z in range(groups) for core in range(2)] for c in range(CHIPS)]


def quads():
    count = lax.axis_size("dp")
    return [
        [first + 2 * c + core for c in range(CHIPS)] for first in range(0, count, GROUP) for core in range(2)
    ]


def trade(chunks):
    return lax.all_to_all(chunks, "dp", 0, 0, tiled=True, axis_index_groups=quads())


def share_out(own):
    return trade(jnp.broadcast_to(own, (CHIPS,) + own.shape))


def in_order(slots):
    chip = lax.axis_index("dp") % GROUP // 2
    odd, high = chip % 2 == 1, chip // 2 == 1
    a, b, c, d = slots
    a, b, c, d = jnp.where(odd, b, a), jnp.where(odd, a, b), jnp.where(odd, d, c), jnp.where(odd, c, d)
    return [jnp.where(high, c, a), jnp.where(high, d, b), jnp.where(high, a, c), jnp.where(high, b, d)]


def line_step(sides, own, s):
    groups = lax.axis_size("dp") // GROUP
    up, down = sides if s > 1 else (own, own)
    return hop(up, 1, s - 1, groups - 1), hop(down, -1, 1, groups - s + 1)


def line_stack(own, steps):
    groups = lax.axis_size("dp") // GROUP
    z = lax.axis_index("dp") // GROUP
    return jnp.stack(
        [own]
        + [jnp.where(z + s < groups, steps[s - 1][1], steps[groups - s - 1][0]) for s in range(1, groups)]
    )


def line_sum(parts):
    groups = lax.axis_size("dp") // GROUP
    total = parts[0].astype(F32)
    for s in range(1, groups):
        pairs = [
            (z * GROUP + t, (z + s) % groups * GROUP + t) for z in range(groups) for t in range(GROUP)
        ]
        total = total + lax.ppermute(parts[s].astype(BF), "dp", pairs).astype(F32)
    return total


def after(value, *others):
    return lax.optimization_barrier((value,) + others)[0]


def core_sum(mine, other):
    return mine + swap(other.astype(BF), 1).astype(F32)


ANY = pl.BlockSpec(memory_space=pl.ANY)
VMEM = pl.BlockSpec(memory_space=pltpu.VMEM)
SMEM = pl.BlockSpec(memory_space=pltpu.SMEM)


def call(kernel, outs, args, places, scratch=(), micros=1):
    return pl.pallas_call(
        kernel,
        out_shape=tuple(jax.ShapeDtypeStruct(shape, kind) for shape, kind in outs),
        in_specs=list(places),
        out_specs=tuple(VMEM for _ in outs),
        scratch_shapes=list(scratch),
        compiler_params=pltpu.CompilerParams(vmem_limit_bytes=VMEM_BYTES),
        cost_estimate=pl.CostEstimate(flops=micros * 1000000000, bytes_accessed=1000, transcendentals=0),
    )(*args)


def fetch(source, target, sem):
    copy = pltpu.make_async_copy(source, target, sem)
    copy.start()
    return copy


def turned(values, cosine, sine):
    return values * cosine + pltpu.roll(values, HEAD_DIM // 2, 1) * sine


def pass_kernel(in_ref, out_ref):
    out_ref[...] = in_ref[...]


def pause(mark, *others):
    (mark,) = call(pass_kernel, [(mark.shape, mark.dtype)], (mark,), [VMEM], micros=SPACE)
    return lax.optimization_barrier((mark,) + others)


def project_kernel(
    x_ref, gain_ref, shift_ref, cos_ref, sin_ref, wq, wk, wv, normed_ref, q_ref, k_ref, v_ref, w_ref, sems
):
    copies = [fetch(w, w_ref.at[i], sems.at[i]) for i, w in enumerate((wq, wk, wv))]
    normal, _ = norm_stats(x_ref[...].astype(F32))
    normed_ref[...] = (normal * gain_ref[...] + shift_ref[...]).astype(BF)
    cosine, sine = cos_ref[...], sin_ref[...]
    for i, out in enumerate((q_ref, k_ref, v_ref)):
        copies[i].wait()
        for low in range(0, out.shape[1], WIDE):
            raw = dot(normed_ref[...], w_ref[i, :, low : low + WIDE])
            for h in range(0, WIDE, HEAD_DIM):
                head = raw[:, h : h + HEAD_DIM]
                if i < 2:
                    head = turned(head, cosine, sine)
                out[:, low + h : low + h + HEAD_DIM] = head.astype(BF)


def attend_kernel(
    q_ref, k_ref, v_ref, x_ref, gain_ref, shift_ref, first_ref, wo,
    both_ref, mixed_ref, normed_ref, probs_ref, w_ref, sem
):
    copy = fetch(wo, w_ref, sem)
    tokens, width = q_ref.shape
    both_ref[:tokens] = first_ref[...]
    row = lax.broadcasted_iota(jnp.int32, (tokens, tokens), 0)
    causal = row >= lax.broadcasted_iota(jnp.int32, (tokens, tokens), 1)
    for h in range(width // HEAD_DIM):
        span = slice(h * HEAD_DIM, (h + 1) * HEAD_DIM)
        scores = dot_t(q_ref[:, span], k_ref[:, span]) * HEAD_DIM**-0.5
        scores = jnp.where(causal, scores, NEGATIVE)
        weight = jnp.exp(scores - jnp.max(scores, axis=-1, keepdims=True))
        probs = weight / jnp.sum(weight, axis=-1, keepdims=True)
        probs_ref[h] = probs
        both_ref[tokens:, span] = dot(probs.astype(BF), v_ref[:, span]).astype(BF)
    copy.wait()
    for low in range(0, width, WIDE):
        span = slice(low, low + WIDE)
        mixed_ref[:, span] = x_ref[:, span].astype(F32) + dot(both_ref[tokens:], w_ref[:, span])
    normal, _ = norm_stats(mixed_ref[...])
    normed_ref[...] = (normal * gain_ref[...] + shift_ref[...]).astype(BF)


def place_first(weights, w_ref, sems, z, core):
    if len(weights) == 1:
        return [fetch(weights[0], w_ref, sems.at[0])]
    groups, rows = weights[0].shape[0], weights[0].shape[1] // CHIPS
    copies = []
    for k, source in enumerate(weights):
        side = core if k == 0 else 1 - core
        for g in range(groups):
            for c in range(CHIPS):
                low = pl.multiple_of(((lax.rem(z + g, groups) * CHIPS + c) * 2 + side) * rows, 16)
                copies.append(
                    fetch(
                        source.at[g, c * rows : (c + 1) * rows],
                        w_ref.at[pl.ds(low, rows)],
                        sems.at[len(copies)],
                    )
                )
    return copies


def place_second(weights, w_ref, sems, z, core):
    groups, cols, _ = weights[0].shape
    copies = []
    for k, source in enumerate(weights):
        side = core if k == 0 else 1 - core
        for g in range(groups):
            low = pl.multiple_of((side * groups + lax.rem(z + g, groups)) * cols, 16)
            copies.append(fetch(source.at[g], w_ref.at[pl.ds(low, cols)], sems.at[len(copies)]))
    return copies


def by_slot(array_ref, chip):
    return jnp.concatenate([array_ref[chip ^ j] for j in range(CHIPS)], axis=0)


def put_rows(value, outs, low, core, at):
    if len(outs[0].shape) == 2:
        outs[0][low : low + value.shape[0], at] = value
        return
    rows = outs[0].shape[1] // CHIPS
    if len(outs) == 1:
        for piece in range(value.shape[0] // rows):
            line, side = divmod(low // rows + piece, 2)
            g, c = divmod(line, CHIPS)
            outs[0][2 * g + side, c * rows : (c + 1) * rows, at] = value[piece * rows : (piece + 1) * rows]
        return
    for pair in range(value.shape[0] // rows // 2):
        g, c = divmod(low // rows // 2 + pair, CHIPS)
        first = value[2 * pair * rows : (2 * pair + 1) * rows]
        second = value[(2 * pair + 1) * rows : (2 * pair + 2) * rows]
        spot = slice(c * rows, (c + 1) * rows)
        outs[0][g, spot, at] = jnp.where(core == 0, first, second)
        outs[1][g, spot, at] = jnp.where(core == 0, second, first)


def hidden_kernel(*refs):
    place, xs = refs[0], refs[1 : 1 + PIECES]
    bias_ref, mask_ref = refs[1 + PIECES : 3 + PIECES]
    weights = refs[3 + PIECES : -4]
    active_ref, slope_ref, w_ref, sems = refs[-4:]
    copies = place_first(weights, w_ref, sems, place[0], place[2])
    x = jnp.concatenate([x[...] for x in xs], axis=0)
    tokens = xs[0].shape[0]
    for copy in copies:
        copy.wait()
    for low in range(0, w_ref.shape[1], WIDE):
        span = slice(low, low + WIDE)
        hidden = dot(x, w_ref[:, span]) + bias_ref[:, span]
        square = hidden * hidden
        bent = jnp.tanh(0.7978845608 * hidden * (1.0 + 0.044715 * square))
        slope = 0.5 * (1.0 + bent) + (0.5 * 0.7978845608) * hidden * (1.0 - bent * bent) * (
            1.0 + 3.0 * 0.044715 * square
        )
        value = 0.5 * hidden * (1.0 + bent)
        for j in range(CHIPS):
            part = slice(j * tokens, (j + 1) * tokens)
            keep = mask_ref[j : j + 1, span]
            active_ref[part, span] = (value[part] * keep).astype(BF)
            slope_ref[part, span] = slope[part] * keep


def down_kernel(place, active_ref, grad_ref, kept_ref, *outs):
    chip, core = place[1], place[2]
    groups, cols, width = outs[0].shape
    grad = by_slot(grad_ref, chip) * kept_ref[...].astype(BF)
    half = groups * cols
    for k, out_ref in enumerate(outs):
        low = pl.multiple_of((core ^ k) * half, 128)
        for at in range(0, width, WIDE):
            value = t_dot(active_ref[:, pl.ds(low, half)], grad[:, at : at + WIDE]).astype(BF)
            for g in range(groups):
                out_ref[g, :, at : at + WIDE] = value[g * cols : (g + 1) * cols]


def reverse_kernel(*refs):
    place, grads_ref, kept_ref, slope_ref, near2, far2 = refs[:6]
    weights = refs[6:-10]
    grad_ref, sum_ref, own_ref = refs[-10:-7]
    sent = refs[-7:-4]
    w1_ref, w2_ref, sems1, sems2 = refs[-4:]
    second = place_second((near2, far2), w2_ref, sems2, place[0], place[2])
    first = place_first(weights, w1_ref, sems1, place[0], place[2])
    tokens = grads_ref.shape[1]
    grad = by_slot(grads_ref, place[1]) * kept_ref[...].astype(BF)
    for copy in second:
        copy.wait()
    for low in range(0, w2_ref.shape[0], WIDE):
        span = slice(low, low + WIDE)
        value = (dot_t(grad, w2_ref[span, :]) * slope_ref[:, span]).astype(BF)
        grad_ref[:, span] = value
        sum_ref[:, span] = jnp.sum(value.astype(F32), axis=0, keepdims=True)
    for copy in first:
        copy.wait()
    for low in range(0, w1_ref.shape[0], WIDE):
        span = slice(low, low + WIDE)
        part = dot_t(grad_ref[...], w1_ref[span, :])
        own_ref[:, span] = part[:tokens]
        for j in range(1, CHIPS):
            sent[j - 1][:, span] = part[j * tokens : (j + 1) * tokens].astype(BF)


def finish_kernel(*refs):
    place, xs = refs[0], refs[1 : 1 + PIECES]
    active_ref, grad_ref, near2, far2 = refs[1 + PIECES : 5 + PIECES]
    ups, (out_ref, w2_ref, sems) = refs[5 + PIECES : -3], refs[-3:]
    second = place_second((near2, far2), w2_ref, sems, place[0], place[2])
    tokens, width = xs[0].shape
    step = width // CHIPS
    for low in range(0, width, step):
        x = jnp.concatenate([x[:, low : low + step] for x in xs], axis=0)
        put_rows(t_dot(x, grad_ref[...]).astype(BF), ups, low, place[2], slice(None))
    for copy in second:
        copy.wait()
    for low in range(0, width, WIDE):
        span = slice(low, low + WIDE)
        part = dot(active_ref[...], w2_ref[:, span])
        for j in range(CHIPS):
            out_ref[place[1] ^ j, :, span] = part[j * tokens : (j + 1) * tokens].astype(BF)


def mixed_kernel(
    own_ref, got1, got2, got3, mixed_ref, sens_ref, gain_ref, wo, v_ref, probs_ref,
    mixgrad_ref, cgrad_ref, vgrad_ref, pair_ref, norm_ref, shift_ref, w_ref, low_ref, sem
):
    copy = fetch(wo, w_ref, sem)
    normal, inverse = norm_stats(mixed_ref[...])
    second = own_ref[...] + got1[...].astype(F32) + got2[...].astype(F32) + got3[...].astype(F32)
    second = second.astype(BF).astype(F32)
    part, norm_sum, shift_sum = norm_back(second, gain_ref[...], normal, inverse)
    norm_ref[...], shift_ref[...] = norm_sum, shift_sum
    mixed_grad = sens_ref[...].astype(F32) + part
    mixgrad_ref[...] = mixed_grad
    low_ref[...] = mixed_grad.astype(BF)
    copy.wait()
    width = v_ref.shape[1]
    share = width // CHIPS
    for low in range(0, width, WIDE):
        cgrad_ref[:, low : low + WIDE] = dot_t(low_ref[...], w_ref[low : low + WIDE, :]).astype(BF)
    for h in range(width // HEAD_DIM):
        span = slice(h * HEAD_DIM, (h + 1) * HEAD_DIM)
        vgrad_ref[:, span] = t_dot(probs_ref[h].astype(BF), cgrad_ref[:, span]).astype(BF)
    for c in range(CHIPS):
        pair_ref[c, :, :share] = low_ref[:, c * share : (c + 1) * share]
        pair_ref[c, :, share:] = vgrad_ref[:, c * share : (c + 1) * share]


def score_kernel(
    place, cgrad_ref, q_ref, k_ref, v_ref, probs_ref, cos_ref, sin_ref, qgrad_ref, kgrad_ref, *pieces
):
    cosine, sine = cos_ref[...], -sin_ref[...]
    width = v_ref.shape[1]
    for h in range(width // HEAD_DIM):
        span = slice(h * HEAD_DIM, (h + 1) * HEAD_DIM)
        probs = probs_ref[h]
        probs_grad = dot_t(cgrad_ref[:, span], v_ref[:, span])
        inner = jnp.sum(probs_grad * probs, axis=-1, keepdims=True)
        scores_grad = (probs * (probs_grad - inner)).astype(BF)
        scale = HEAD_DIM**-0.5
        qgrad_ref[:, span] = turned(dot(scores_grad, k_ref[:, span]) * scale, cosine, sine).astype(BF)
        kgrad_ref[:, span] = turned(t_dot(scores_grad, q_ref[:, span]) * scale, cosine, sine).astype(BF)
    share = width // CHIPS
    for j, piece in enumerate(pieces):
        low = pl.multiple_of((place[1] ^ j) * share, HEAD_DIM)
        piece[:, :share] = kgrad_ref[:, pl.ds(low, share)]
        piece[:, share:] = qgrad_ref[:, pl.ds(low, share)]


def leading_kernel(
    qgrad_ref, kgrad_ref, vgrad_ref, x_ref, gain_ref, mixgrad_ref, wq, wk, wv,
    out_ref, norm_ref, shift_ref, w_ref, lead_ref, sems
):
    copies = [fetch(w, w_ref.at[i], sems.at[i]) for i, w in enumerate((wq, wk, wv))]
    normal, inverse = norm_stats(x_ref[...].astype(F32))
    for copy in copies:
        copy.wait()
    for low in range(0, x_ref.shape[1], WIDE):
        span = slice(low, low + WIDE)
        lead_ref[:, span] = (
            dot_t(qgrad_ref[...], w_ref[0, span, :])
            + dot_t(kgrad_ref[...], w_ref[1, span, :])
            + dot_t(vgrad_ref[...], w_ref[2, span, :])
        )
    part, norm_sum, shift_sum = norm_back(lead_ref[...], gain_ref[...], normal, inverse)
    norm_ref[...], shift_ref[...] = norm_sum, shift_sum
    out_ref[...] = (mixgrad_ref[...] + part).astype(BF)


def outer_into(lefts, rights, outs, core):
    width, share = lefts[0].shape[1], rights[0].shape[1]
    step = width // CHIPS
    for i, (left_ref, right) in enumerate(zip(lefts, rights)):
        for low in range(0, width, step):
            value = t_dot(left_ref[:, low : low + step], right).astype(BF)
            put_rows(value, outs, low, core, slice(i * share, (i + 1) * share))


def early_kernel(place, both_ref, right_ref, *refs):
    outs, lefts = refs[:-2], refs[-2:]
    tokens = right_ref.shape[1]
    for i, left_ref in enumerate(lefts):
        for j in range(CHIPS):
            left_ref[j * tokens : (j + 1) * tokens] = both_ref[j, (1 - i) * tokens : (2 - i) * tokens]
    right = right_ref[...].reshape(CHIPS * tokens, right_ref.shape[2])
    share = right.shape[1] // 2
    outer_into(lefts, (right[:, :share], right[:, share:]), outs, place[2])


def late_kernel(place, both_ref, *refs):
    pieces, outs, left_ref = refs[:CHIPS], refs[CHIPS:-1], refs[-1]
    tokens = pieces[0].shape[0]
    for j in range(CHIPS):
        left_ref[j * tokens : (j + 1) * tokens] = both_ref[place[1] ^ j, :tokens]
    right = jnp.concatenate([piece[...] for piece in pieces], axis=0)
    outer_into((left_ref,), (right,), outs, place[2])


def per_device(
    sequence_elements,
    result_sensitivity,
    mixer_gain,
    mixer_offset,
    question_matrix,
    lookup_matrix,
    content_matrix,
    mixer_projection_matrix,
    feedforward_gain,
    feedforward_offset,
    expand_matrix,
    inner_neuron_offset,
    contract_matrix,
    feedforward_result_offset,
    sequence_level_choice,
    servers_per_level,
    accepted_row_limit,
    server_selection,
):
    devices = lax.axis_size("dp")
    me = lax.axis_index("dp")
    groups = devices // GROUP
    z, chip, core = me // GROUP, me % GROUP // 2, me % 2
    tokens, width = sequence_elements.shape
    heads = width // HEAD_DIM
    rows, feed = expand_matrix.shape
    cols = contract_matrix.shape[0]
    offset_len = feedforward_result_offset.shape[0]
    levels = jnp.arange(LEVELS)
    block = 2 * cols
    units = groups * block
    gain_first, shift_first, gain_second, shift_second = (
        v.astype(F32)[None, :] for v in (mixer_gain, mixer_offset, feedforward_gain, feedforward_offset)
    )
    cosine, sine = (jnp.asarray(t) for t in rope_tables(tokens))
    flat, wide = (tokens, width), (1, width)
    square = (width, width)
    all_rows = (CHIPS * tokens, units)
    weight_space = pltpu.VMEM(square, BF)
    triple_space = pltpu.VMEM((3,) + square, BF)
    hidden_space = pltpu.VMEM((width, units), BF)
    dma, dmas = pltpu.SemaphoreType.DMA, pltpu.SemaphoreType.DMA((3,))
    aligned = rows % 16 == 0
    firsts = pltpu.SemaphoreType.DMA((2 * groups * CHIPS if aligned else 1,))
    seconds = pltpu.SemaphoreType.DMA((2 * groups,))
    place = jnp.stack([z, chip, core]).astype(jnp.int32)
    fence = lax.optimization_barrier

    expand_chunks = expand_matrix.reshape(rows, groups, CHIPS, 2, cols).transpose(2, 0, 3, 1, 4)
    expand_pieces = exchange(expand_chunks.reshape(CHIPS, rows, units))
    contract_steps = [line_step(None, contract_matrix, 1)]
    group_grad = share_out(result_sensitivity)
    normed_first, query_rot, key_rot, value_rows = call(
        project_kernel,
        [(flat, BF)] * 4,
        (sequence_elements, gain_first, shift_first, cosine, sine, question_matrix, lookup_matrix, content_matrix),
        [VMEM] * 5 + [ANY] * 3,
        [triple_space, dmas], micros=8)
    normed_first, query_rot, key_rot, value_rows, expand_pieces = fence(
        (normed_first, query_rot, key_rot, value_rows, expand_pieces)
    )

    expand_plane = jnp.concatenate(in_order(expand_pieces), axis=0)
    expand_steps = [line_step(None, expand_plane, 1)]
    both_rows, mixed, normed_second, probs = call(
        attend_kernel,
        [((2 * tokens, width), BF), (flat, F32), (flat, BF), ((heads, tokens, tokens), F32)],
        (
            query_rot, key_rot, value_rows, sequence_elements, gain_second, shift_second, normed_first,
            mixer_projection_matrix,
        ),
        [VMEM] * 7 + [ANY],
        [weight_space, dma], micros=6)
    both_rows, mixed, normed_second, contract_steps = fence((both_rows, mixed, normed_second, contract_steps))

    half = tokens // 2
    upper, lower = spread(normed_second[:half]), None
    mark = normed_second[:16, :128]
    expand_steps, _ = fence((expand_steps, normed_second))
    expand_steps.append(line_step(expand_steps[-1], expand_plane, 2))
    level = sequence_level_choice[0]
    choice = server_selection.reshape(-1)
    info = jnp.concatenate(
        [
            feedforward_result_offset.astype(F32),
            inner_neuron_offset.astype(F32),
            level.astype(F32)[None],
            jnp.min(choice).astype(F32)[None],
            choice.astype(F32),
        ]
    )
    info = jnp.pad(info, (0, -info.shape[0] % 128))
    mark, upper, expand_steps, group_grad = pause(mark, upper, expand_steps, group_grad)
    lower = spread(after(normed_second[half:], mark))
    for s in range(3, groups):
        expand_steps.append(line_step(expand_steps[-1], expand_plane, s))
    table = after(jnp.broadcast_to(info, (devices, 1) + info.shape), mark)
    table = lax.all_to_all(table, "dp", 0, 0, tiled=True).reshape(devices, -1)
    mark, lower, expand_steps, table = pause(mark, lower, expand_steps, table)
    result_offset = table[:, :offset_len].reshape(-1)
    hidden_offsets = table[:, offset_len : offset_len + cols]
    all_levels = table[:, offset_len + cols].astype(jnp.int32)
    all_lowest = table[:, offset_len + cols + 1].astype(jnp.int32)
    near = me ^ (2 * jnp.arange(CHIPS))
    slot_levels = jnp.take(all_levels, near)
    slot_choice = jnp.take(table[:, offset_len + cols + 2 :], near, axis=0)[:, :tokens].astype(jnp.int32)
    slot_hot = slot_levels[:, None] == levels[None, :]
    size = jnp.sum(jnp.where(slot_hot, servers_per_level[None, :], 0), axis=1)[:, None]
    limit = jnp.sum(jnp.where(slot_hot, accepted_row_limit[None, :], 0), axis=1)[:, None]
    server = slot_choice % size
    before = jnp.arange(tokens)[None, :] < jnp.arange(tokens)[:, None]
    same = before[None] & (server[:, None, :] == server[:, :, None])
    local = jnp.sum(same.astype(jnp.int32), axis=2)
    low = all_lowest[None, None, :]
    size, server = size[:, :, None], server[:, :, None]
    seen = (low + tokens - 1 - server + size) // size - (low - 1 - server + size) // size
    earlier = (jnp.arange(devices)[None, :] < near[:, None]) & (all_levels[None, :] == slot_levels[:, None])
    arrival = local + jnp.sum(jnp.where(earlier[:, None, :], seen, 0), axis=2)
    slot_kept = (arrival < limit).astype(F32)
    kept = slot_kept[0][:, None]
    slot_kept = slot_kept.reshape(-1, 1)
    kept_sensitivity = (result_sensitivity.astype(F32) * kept).astype(BF)
    starts = (jnp.arange(groups) * CHIPS + chip) * block
    active_block = starts[None, :] < (feed // 8) * (1 << slot_levels[:, None])
    mask = jnp.tile(jnp.repeat(active_block.astype(F32), cols, axis=1), (1, 2))
    hidden_offset = lax.dynamic_index_in_dim(
        hidden_offsets.reshape(groups, CHIPS, 2, cols), chip, 1, keepdims=False
    )
    hidden_offset = hidden_offset.transpose(1, 0, 2).reshape(1, -1)
    row_slots = [normed_second] + [piece for pair in zip(upper[1:], lower[1:]) for piece in pair]
    group_both = lax.all_gather(after(both_rows, lower), "dp", axis_index_groups=quads())
    expand_mine = line_stack(expand_plane, expand_steps)
    expand_other = swap(expand_mine, 1)
    contract_steps[0] = after(contract_steps[0], mark)
    contract_steps.append(line_step(contract_steps[-1], contract_matrix, 2))
    mark, expand_other, contract_steps = pause(mark, expand_other, contract_steps)
    for s in range(3, groups):
        contract_steps.append(line_step(contract_steps[-1], contract_matrix, s))
    if aligned:
        first_weight = (expand_mine, expand_other)
    else:
        pair = jnp.stack([expand_mine, expand_other]).reshape(2, groups, CHIPS, rows, units)
        pair = jnp.take(pair, (jnp.arange(groups) - z) % groups, axis=1)
        first_weight = (jnp.where(core == 0, pair, pair[::-1]).transpose(1, 2, 0, 3, 4).reshape(width, units),)

    active, slope = call(
        hidden_kernel,
        [(all_rows, BF), (all_rows, F32)],
        (place, *row_slots, hidden_offset, mask, *first_weight),
        [SMEM] + [VMEM] * (PIECES + 2) + [ANY] * len(first_weight),
        [hidden_space, firsts],
        micros=30,
    )
    active, contract_steps = fence((active, contract_steps))
    sides = 2 if aligned else 1
    down_mine, down_other = call(
        down_kernel, [((groups, cols, width), BF)] * 2, (place, active, group_grad, slot_kept), [SMEM] + [VMEM] * 3, micros=8
    )
    down_got = swap(down_other, 1)
    contract_mine = line_stack(contract_matrix, contract_steps)
    contract_other = swap(contract_mine, 1)
    contract_both = (down_mine.astype(F32) + down_got.astype(F32)).astype(BF)
    contract_both, contract_other = fence((contract_both, contract_other))
    share_contract = lax.psum_scatter(contract_both, "dp", scatter_dimension=0, axis_index_groups=lines())
    hidden_grad, hidden_sum, second_own, *second_sent = call(
        reverse_kernel,
        [(all_rows, BF), ((1, units), F32), (flat, F32)] + [(flat, BF)] * 3,
        (place, group_grad, slot_kept, slope, contract_mine, contract_other, *first_weight),
        [SMEM] + [VMEM] * 3 + [ANY] * (2 + len(first_weight)),
        [hidden_space, pltpu.VMEM((units, width), BF), firsts, seconds],
        micros=15,
    )
    hidden_grad, second_sent = fence((hidden_grad, second_sent))
    second_got = [swap(second_sent[j - 1], 2 * j) for j in range(1, CHIPS)]
    half_shape = (groups, CHIPS * rows) if aligned else (width,)
    bar_shape = (2 * groups, CHIPS * rows) if aligned else (width,)
    up_part, branch_sent = call(
        finish_kernel,
        [(bar_shape + (units,), BF), ((CHIPS,) + flat, BF)],
        (place, *row_slots, active, hidden_grad, contract_mine, contract_other),
        [SMEM] + [VMEM] * (PIECES + 2) + [ANY] * 2,
        [pltpu.VMEM((units, width), BF), seconds],
        micros=13,
    )
    up_part, second_got, group_both = fence((up_part, second_got, group_both))
    if not aligned:
        up_part = up_part.reshape(groups, CHIPS, 2, rows, units).transpose(0, 2, 1, 3, 4)
        up_part = up_part.reshape(2 * groups, CHIPS * rows, units)
    expand_rows = lax.psum_scatter(up_part, "dp", scatter_dimension=0, axis_index_groups=bars())

    def by_sides(parts):
        if aligned:
            return parts
        part = parts[0].reshape(groups, CHIPS, 2, rows, -1)
        return [
            lax.dynamic_index_in_dim(part, core ^ k, 2, keepdims=False).reshape(groups, CHIPS * rows, -1)
            for k in range(2)
        ]

    def add(mine, got):
        return (mine.astype(F32) + got.astype(F32)).astype(BF)


    share = width // CHIPS
    pair_shape = (tokens, 2 * share)
    mixed_grad, context_grad, value_grad, first_pair, midnorm_sum, midshift_sum = call(
        mixed_kernel,
        [(flat, F32), (flat, BF), (flat, BF), ((CHIPS,) + pair_shape, BF), (wide, F32), (wide, F32)],
        (
            second_own, *second_got, mixed, result_sensitivity, gain_second, mixer_projection_matrix,
            value_rows, probs,
        ),
        [VMEM] * 7 + [ANY] + [VMEM] * 2,
        [weight_space, pltpu.VMEM(flat, BF), dma],
        micros=8,
    )
    first_pair, context_grad, value_grad, share_contract = fence(
        (first_pair, context_grad, value_grad, share_contract)
    )
    first_pair = trade(first_pair)
    query_grad, key_grad, *second_pair = call(
        score_kernel,
        [(flat, BF)] * 2 + [(pair_shape, BF)] * CHIPS,
        (place, context_grad, query_rot, key_rot, value_rows, probs, cosine, sine),
        [SMEM] + [VMEM] * 7,
        micros=1,
    )
    second_pair = [piece if j == 0 else swap(piece, 2 * j) for j, piece in enumerate(second_pair)]
    query_grad, key_grad, first_pair = fence((query_grad, key_grad, first_pair))

    outer_shape = [(half_shape + (2 * share,), BF)] * sides
    left_space = pltpu.VMEM((CHIPS * tokens, width), BF)
    early = call(
        early_kernel, outer_shape, (place, group_both, first_pair), [SMEM] + [VMEM] * 2, [left_space] * 2, micros=6
    )
    early_mine, early_other = by_sides(early)
    early_both = add(early_mine, swap(early_other, 1))
    early_both, query_grad = fence((early_both, query_grad))
    early_sum = lax.psum_scatter(early_both, "dp", scatter_dimension=0, axis_index_groups=lines())
    layer_input_gradient, leadnorm_sum, leadshift_sum = call(
        leading_kernel,
        [(flat, BF), (wide, F32), (wide, F32)],
        (
            query_grad, key_grad, value_grad, sequence_elements, gain_first, mixed_grad,
            question_matrix, lookup_matrix, content_matrix,
        ),
        [VMEM] * 6 + [ANY] * 3,
        [triple_space, pltpu.VMEM(flat, F32), dmas],
        micros=13,
    )
    leadnorm_sum, second_pair = fence((leadnorm_sum, second_pair))
    late = call(
        late_kernel, outer_shape, (place, group_both, *second_pair), [SMEM] + [VMEM] * 5, [left_space], micros=1
    )
    late_mine, late_other = by_sides(late)
    branch = jnp.sum(trade(after(branch_sent, leadnorm_sum)).astype(F32), axis=0)
    late_both = add(late_mine, swap(late_other, 1))
    late_sum = line_sum(
        [lax.dynamic_index_in_dim(late_both, (z + s) % groups, 0, keepdims=False) for s in range(groups)]
    )
    branch = (branch + result_offset).astype(BF).astype(F32)
    layer_output = (mixed + kept * branch).astype(BF)

    def home(summed):
        return trade(summed.astype(BF).reshape(CHIPS, rows, -1))

    hidden_spot = (jnp.arange(CHIPS)[None, :, None, None] == chip).astype(F32)
    hidden_full = hidden_spot * hidden_sum.reshape(2, groups, cols).transpose(1, 0, 2)[:, None]
    result_sum = jnp.sum(kept_sensitivity.astype(F32), axis=0)
    vectors = [midnorm_sum, midshift_sum, leadnorm_sum, leadshift_sum, result_sum, hidden_full]
    vectors = jnp.concatenate([vector.reshape(devices, -1) for vector in vectors], axis=1)
    vectors = jnp.pad(vectors, ((0, 0), (0, -vectors.shape[1] % 128)))
    vectors = scatter_all(vectors.reshape(devices, -1, 128)).reshape(-1)
    small = [vectors[i * offset_len : (i + 1) * offset_len] for i in range(5)]
    share_hidden = vectors[5 * offset_len : 5 * offset_len + cols]

    expand_home = home(after(expand_rows, layer_output))
    share_expand = (
        expand_home.reshape(CHIPS, rows, 2, groups, cols).transpose(1, 3, 0, 2, 4).reshape(rows, feed).astype(F32)
    )
    last = jnp.concatenate([early_sum, after(late_sum.astype(BF), expand_home)], axis=1)
    last = home(last)

    def join(at):
        piece = last[:, :, at * share : (at + 1) * share]
        return piece.transpose(1, 0, 2).reshape(rows, width).astype(F32)

    share_mixing, share_value, share_key, share_query = (join(at) for at in range(4))
    return (
        layer_output,
        layer_input_gradient,
        small[2],
        small[3],
        share_query,
        share_key,
        share_value,
        share_mixing,
        small[0],
        small[1],
        share_expand,
        share_hidden,
        share_contract.astype(F32),
        small[4],
    )


def solution(mesh):
    split, line, whole = P("dp", None), P("dp"), P()
    return jax.shard_map(
        per_device,
        mesh=mesh,
        in_specs=(split, split) + (whole,) * 8 + (split, line, split, line, line, whole, whole, split),
        out_specs=(split, split, line, line, split, split, split, split, line, line, split, line, split, line),
        check_vma=False,
    )
```

```python
import jax
import jax.numpy as jnp
import numpy as np
from jax import lax
from jax.experimental import pallas as pl
from jax.experimental.pallas import tpu as pltpu
from jax.sharding import PartitionSpec as P

HEAD_DIM = 128
LEVELS = 4
GROUP = 8
CHIPS = 4
EPSILON = 1e-05
NEGATIVE = -1e30
BF = jnp.bfloat16
F32 = jnp.float32
WIDE = 512
SPACE = 6
PIECES = 7
VMEM_BYTES = 56 * 1024 * 1024


def dot(left, right, dims=((1,), (0,))):
    return lax.dot_general(left, right, (dims, ((), ())), preferred_element_type=F32)


def dot_t(left, right):
    return dot(left, right, ((1,), (1,)))


def t_dot(left, right):
    return dot(left, right, ((0,), (0,)))


def rope_tables(length):
    half = HEAD_DIM // 2
    rates = (10000.0 ** (-(np.arange(half, dtype=np.float64) * 2.0 / HEAD_DIM))).astype(np.float32)
    angles = np.arange(length, dtype=np.float32)[:, None] * rates[None, :]
    cosine, sine = np.cos(angles).astype(np.float32), np.sin(angles).astype(np.float32)
    return np.concatenate([cosine, cosine], axis=1), np.concatenate([-sine, sine], axis=1)


def norm_stats(values):
    center = values - jnp.mean(values, axis=-1, keepdims=True)
    inverse = lax.rsqrt(jnp.mean(center * center, axis=-1, keepdims=True) + EPSILON)
    return center * inverse, inverse


def norm_back(incoming, gain, normal, inverse):
    scaled = incoming * gain
    part = inverse * (
        scaled
        - jnp.mean(scaled, axis=-1, keepdims=True)
        - normal * jnp.mean(scaled * normal, axis=-1, keepdims=True)
    )
    return part, jnp.sum(incoming * normal, axis=0, keepdims=True), jnp.sum(incoming, axis=0, keepdims=True)


def swap(value, bit):
    count = lax.axis_size("dp")
    return lax.ppermute(value, "dp", [(i, i ^ bit) for i in range(count)])


def hop(value, step, near, far):
    groups = lax.axis_size("dp") // GROUP
    pairs = [
        (z * GROUP + t, (z + step) * GROUP + t)
        for z in range(max(near, 0), min(far, groups))
        if 0 <= z + step < groups
        for t in range(GROUP)
    ]
    return lax.ppermute(value, "dp", pairs)


def scatter_all(parts):
    count = lax.axis_size("dp")
    parts = jnp.take(parts, lax.axis_index("dp") ^ jnp.arange(count), axis=0)
    bit = count // 2
    while bit:
        parts = parts[:bit] + swap(parts[bit:], bit)
        bit //= 2
    return parts


def lines():
    groups = lax.axis_size("dp") // GROUP
    return [[z * GROUP + t for z in range(groups)] for t in range(GROUP)]


def spread(own):
    return [own, swap(own, 2), swap(own, 4), swap(own, 6)]


def exchange(chunks):
    chip = lax.axis_index("dp") % GROUP // 2
    got = []
    for j in range(CHIPS):
        chunk = lax.dynamic_index_in_dim(chunks, chip ^ j, 0, keepdims=False)
        got.append(chunk if j == 0 else swap(chunk, 2 * j))
    return got


def bars():
    groups = lax.axis_size("dp") // GROUP
    return [[z * GROUP + 2 * c + core for z in range(groups) for core in range(2)] for c in range(CHIPS)]


def quads():
    count = lax.axis_size("dp")
    return [
        [first + 2 * c + core for c in range(CHIPS)] for first in range(0, count, GROUP) for core in range(2)
    ]


def trade(chunks):
    return lax.all_to_all(chunks, "dp", 0, 0, tiled=True, axis_index_groups=quads())


def share_out(own):
    return trade(jnp.broadcast_to(own, (CHIPS,) + own.shape))


def in_order(slots):
    chip = lax.axis_index("dp") % GROUP // 2
    odd, high = chip % 2 == 1, chip // 2 == 1
    a, b, c, d = slots
    a, b, c, d = jnp.where(odd, b, a), jnp.where(odd, a, b), jnp.where(odd, d, c), jnp.where(odd, c, d)
    return [jnp.where(high, c, a), jnp.where(high, d, b), jnp.where(high, a, c), jnp.where(high, b, d)]


def line_step(sides, own, s):
    groups = lax.axis_size("dp") // GROUP
    up, down = sides if s > 1 else (own, own)
    return hop(up, 1, s - 1, groups - 1), hop(down, -1, 1, groups - s + 1)


def line_stack(own, steps):
    groups = lax.axis_size("dp") // GROUP
    z = lax.axis_index("dp") // GROUP
    return jnp.stack(
        [own]
        + [jnp.where(z + s < groups, steps[s - 1][1], steps[groups - s - 1][0]) for s in range(1, groups)]
    )


def line_sum(parts):
    groups = lax.axis_size("dp") // GROUP
    total = parts[0].astype(F32)
    for s in range(1, groups):
        pairs = [
            (z * GROUP + t, (z + s) % groups * GROUP + t) for z in range(groups) for t in range(GROUP)
        ]
        total = total + lax.ppermute(parts[s].astype(BF), "dp", pairs).astype(F32)
    return total


def after(value, *others):
    return lax.optimization_barrier((value,) + others)[0]


def core_sum(mine, other):
    return mine + swap(other.astype(BF), 1).astype(F32)


ANY = pl.BlockSpec(memory_space=pl.ANY)
VMEM = pl.BlockSpec(memory_space=pltpu.VMEM)
SMEM = pl.BlockSpec(memory_space=pltpu.SMEM)


def call(kernel, outs, args, places, scratch=(), micros=1):
    return pl.pallas_call(
        kernel,
        out_shape=tuple(jax.ShapeDtypeStruct(shape, kind) for shape, kind in outs),
        in_specs=list(places),
        out_specs=tuple(VMEM for _ in outs),
        scratch_shapes=list(scratch),
        compiler_params=pltpu.CompilerParams(vmem_limit_bytes=VMEM_BYTES),
        cost_estimate=pl.CostEstimate(flops=micros * 1000000000, bytes_accessed=1000, transcendentals=0),
    )(*args)


def fetch(source, target, sem):
    copy = pltpu.make_async_copy(source, target, sem)
    copy.start()
    return copy


def turned(values, cosine, sine):
    return values * cosine + pltpu.roll(values, HEAD_DIM // 2, 1) * sine


def pass_kernel(in_ref, out_ref):
    out_ref[...] = in_ref[...]


def pause(mark, *others):
    (mark,) = call(pass_kernel, [(mark.shape, mark.dtype)], (mark,), [VMEM], micros=SPACE)
    return lax.optimization_barrier((mark,) + others)


def project_kernel(
    x_ref, gain_ref, shift_ref, cos_ref, sin_ref, wq, wk, wv, normed_ref, q_ref, k_ref, v_ref, w_ref, sems
):
    copies = [fetch(w, w_ref.at[i], sems.at[i]) for i, w in enumerate((wq, wk, wv))]
    normal, _ = norm_stats(x_ref[...].astype(F32))
    normed_ref[...] = (normal * gain_ref[...] + shift_ref[...]).astype(BF)
    cosine, sine = cos_ref[...], sin_ref[...]
    for i, out in enumerate((q_ref, k_ref, v_ref)):
        copies[i].wait()
        for low in range(0, out.shape[1], WIDE):
            raw = dot(normed_ref[...], w_ref[i, :, low : low + WIDE])
            for h in range(0, WIDE, HEAD_DIM):
                head = raw[:, h : h + HEAD_DIM]
                if i < 2:
                    head = turned(head, cosine, sine)
                out[:, low + h : low + h + HEAD_DIM] = head.astype(BF)


def attend_kernel(
    q_ref, k_ref, v_ref, x_ref, gain_ref, shift_ref, first_ref, wo,
    both_ref, mixed_ref, normed_ref, probs_ref, w_ref, sem
):
    copy = fetch(wo, w_ref, sem)
    tokens, width = q_ref.shape
    both_ref[:tokens] = first_ref[...]
    row = lax.broadcasted_iota(jnp.int32, (tokens, tokens), 0)
    causal = row >= lax.broadcasted_iota(jnp.int32, (tokens, tokens), 1)
    for h in range(width // HEAD_DIM):
        span = slice(h * HEAD_DIM, (h + 1) * HEAD_DIM)
        scores = dot_t(q_ref[:, span], k_ref[:, span]) * HEAD_DIM**-0.5
        scores = jnp.where(causal, scores, NEGATIVE)
        weight = jnp.exp(scores - jnp.max(scores, axis=-1, keepdims=True))
        probs = weight / jnp.sum(weight, axis=-1, keepdims=True)
        probs_ref[h] = probs
        both_ref[tokens:, span] = dot(probs.astype(BF), v_ref[:, span]).astype(BF)
    copy.wait()
    for low in range(0, width, WIDE):
        span = slice(low, low + WIDE)
        mixed_ref[:, span] = x_ref[:, span].astype(F32) + dot(both_ref[tokens:], w_ref[:, span])
    normal, _ = norm_stats(mixed_ref[...])
    normed_ref[...] = (normal * gain_ref[...] + shift_ref[...]).astype(BF)


def place_first(weights, w_ref, sems, z, core):
    if len(weights) == 1:
        return [fetch(weights[0], w_ref, sems.at[0])]
    groups, rows = weights[0].shape[0], weights[0].shape[1] // CHIPS
    copies = []
    for k, source in enumerate(weights):
        side = core if k == 0 else 1 - core
        for g in range(groups):
            for c in range(CHIPS):
                low = pl.multiple_of(((lax.rem(z + g, groups) * CHIPS + c) * 2 + side) * rows, 16)
                copies.append(
                    fetch(
                        source.at[g, c * rows : (c + 1) * rows],
                        w_ref.at[pl.ds(low, rows)],
                        sems.at[len(copies)],
                    )
                )
    return copies


def place_second(weights, w_ref, sems, z, core):
    groups, cols, _ = weights[0].shape
    copies = []
    for k, source in enumerate(weights):
        side = core if k == 0 else 1 - core
        for g in range(groups):
            low = pl.multiple_of((side * groups + lax.rem(z + g, groups)) * cols, 16)
            copies.append(fetch(source.at[g], w_ref.at[pl.ds(low, cols)], sems.at[len(copies)]))
    return copies


def by_slot(array_ref, chip):
    return jnp.concatenate([array_ref[chip ^ j] for j in range(CHIPS)], axis=0)


def put_rows(value, outs, low, core, at):
    if len(outs[0].shape) == 2:
        outs[0][low : low + value.shape[0], at] = value
        return
    rows = outs[0].shape[1] // CHIPS
    if len(outs) == 1:
        for piece in range(value.shape[0] // rows):
            line, side = divmod(low // rows + piece, 2)
            g, c = divmod(line, CHIPS)
            outs[0][2 * g + side, c * rows : (c + 1) * rows, at] = value[piece * rows : (piece + 1) * rows]
        return
    for pair in range(value.shape[0] // rows // 2):
        g, c = divmod(low // rows // 2 + pair, CHIPS)
        first = value[2 * pair * rows : (2 * pair + 1) * rows]
        second = value[(2 * pair + 1) * rows : (2 * pair + 2) * rows]
        spot = slice(c * rows, (c + 1) * rows)
        outs[0][g, spot, at] = jnp.where(core == 0, first, second)
        outs[1][g, spot, at] = jnp.where(core == 0, second, first)


def hidden_kernel(*refs):
    place, xs = refs[0], refs[1 : 1 + PIECES]
    bias_ref, mask_ref = refs[1 + PIECES : 3 + PIECES]
    weights = refs[3 + PIECES : -4]
    active_ref, slope_ref, w_ref, sems = refs[-4:]
    copies = place_first(weights, w_ref, sems, place[0], place[2])
    x = jnp.concatenate([x[...] for x in xs], axis=0)
    tokens = xs[0].shape[0]
    for copy in copies:
        copy.wait()
    for low in range(0, w_ref.shape[1], WIDE):
        span = slice(low, low + WIDE)
        hidden = dot(x, w_ref[:, span]) + bias_ref[:, span]
        square = hidden * hidden
        bent = jnp.tanh(0.7978845608 * hidden * (1.0 + 0.044715 * square))
        slope = 0.5 * (1.0 + bent) + (0.5 * 0.7978845608) * hidden * (1.0 - bent * bent) * (
            1.0 + 3.0 * 0.044715 * square
        )
        value = 0.5 * hidden * (1.0 + bent)
        for j in range(CHIPS):
            part = slice(j * tokens, (j + 1) * tokens)
            keep = mask_ref[j : j + 1, span]
            active_ref[part, span] = (value[part] * keep).astype(BF)
            slope_ref[part, span] = (slope[part] * keep).astype(BF)


def down_kernel(place, active_ref, grad_ref, kept_ref, *outs):
    chip, core = place[1], place[2]
    groups, cols, width = outs[0].shape
    grad = by_slot(grad_ref, chip) * kept_ref[...].astype(BF)
    half = groups * cols
    for k, out_ref in enumerate(outs):
        low = pl.multiple_of((core ^ k) * half, 128)
        for at in range(0, width, WIDE):
            value = t_dot(active_ref[:, pl.ds(low, half)], grad[:, at : at + WIDE]).astype(BF)
            for g in range(groups):
                out_ref[g, :, at : at + WIDE] = value[g * cols : (g + 1) * cols]


def reverse_kernel(*refs):
    place, grads_ref, kept_ref, slope_ref, near2, far2 = refs[:6]
    weights = refs[6:-10]
    grad_ref, sum_ref, own_ref = refs[-10:-7]
    sent = refs[-7:-4]
    w1_ref, w2_ref, sems1, sems2 = refs[-4:]
    second = place_second((near2, far2), w2_ref, sems2, place[0], place[2])
    first = place_first(weights, w1_ref, sems1, place[0], place[2])
    tokens = grads_ref.shape[1]
    grad = by_slot(grads_ref, place[1]) * kept_ref[...].astype(BF)
    for copy in second:
        copy.wait()
    for low in range(0, w2_ref.shape[0], WIDE):
        span = slice(low, low + WIDE)
        value = (dot_t(grad, w2_ref[span, :]) * slope_ref[:, span].astype(F32)).astype(BF)
        grad_ref[:, span] = value
        sum_ref[:, span] = jnp.sum(value.astype(F32), axis=0, keepdims=True)
    for copy in first:
        copy.wait()
    for low in range(0, w1_ref.shape[0], WIDE):
        span = slice(low, low + WIDE)
        part = dot_t(grad_ref[...], w1_ref[span, :])
        own_ref[:, span] = part[:tokens]
        for j in range(1, CHIPS):
            sent[j - 1][:, span] = part[j * tokens : (j + 1) * tokens].astype(BF)


def finish_kernel(*refs):
    place, xs = refs[0], refs[1 : 1 + PIECES]
    active_ref, grad_ref, near2, far2 = refs[1 + PIECES : 5 + PIECES]
    ups, (out_ref, w2_ref, sems) = refs[5 + PIECES : -3], refs[-3:]
    second = place_second((near2, far2), w2_ref, sems, place[0], place[2])
    tokens, width = xs[0].shape
    step = width // CHIPS
    for low in range(0, width, step):
        x = jnp.concatenate([x[:, low : low + step] for x in xs], axis=0)
        put_rows(t_dot(x, grad_ref[...]).astype(BF), ups, low, place[2], slice(None))
    for copy in second:
        copy.wait()
    for low in range(0, width, WIDE):
        span = slice(low, low + WIDE)
        part = dot(active_ref[...], w2_ref[:, span])
        for j in range(CHIPS):
            out_ref[place[1] ^ j, :, span] = part[j * tokens : (j + 1) * tokens].astype(BF)


def mixed_kernel(
    own_ref, got1, got2, got3, mixed_ref, sens_ref, gain_ref, wo, v_ref, probs_ref,
    mixgrad_ref, cgrad_ref, vgrad_ref, pair_ref, norm_ref, shift_ref, w_ref, low_ref, sem
):
    copy = fetch(wo, w_ref, sem)
    normal, inverse = norm_stats(mixed_ref[...])
    second = own_ref[...] + got1[...].astype(F32) + got2[...].astype(F32) + got3[...].astype(F32)
    second = second.astype(BF).astype(F32)
    part, norm_sum, shift_sum = norm_back(second, gain_ref[...], normal, inverse)
    norm_ref[...], shift_ref[...] = norm_sum, shift_sum
    mixed_grad = sens_ref[...].astype(F32) + part
    mixgrad_ref[...] = mixed_grad
    low_ref[...] = mixed_grad.astype(BF)
    copy.wait()
    width = v_ref.shape[1]
    share = width // CHIPS
    for low in range(0, width, WIDE):
        cgrad_ref[:, low : low + WIDE] = dot_t(low_ref[...], w_ref[low : low + WIDE, :]).astype(BF)
    for h in range(width // HEAD_DIM):
        span = slice(h * HEAD_DIM, (h + 1) * HEAD_DIM)
        vgrad_ref[:, span] = t_dot(probs_ref[h].astype(BF), cgrad_ref[:, span]).astype(BF)
    for c in range(CHIPS):
        pair_ref[c, :, :share] = low_ref[:, c * share : (c + 1) * share]
        pair_ref[c, :, share:] = vgrad_ref[:, c * share : (c + 1) * share]


def score_kernel(
    place, cgrad_ref, q_ref, k_ref, v_ref, probs_ref, cos_ref, sin_ref, qgrad_ref, kgrad_ref, *pieces
):
    cosine, sine = cos_ref[...], -sin_ref[...]
    width = v_ref.shape[1]
    for h in range(width // HEAD_DIM):
        span = slice(h * HEAD_DIM, (h + 1) * HEAD_DIM)
        probs = probs_ref[h]
        probs_grad = dot_t(cgrad_ref[:, span], v_ref[:, span])
        inner = jnp.sum(probs_grad * probs, axis=-1, keepdims=True)
        scores_grad = (probs * (probs_grad - inner)).astype(BF)
        scale = HEAD_DIM**-0.5
        qgrad_ref[:, span] = turned(dot(scores_grad, k_ref[:, span]) * scale, cosine, sine).astype(BF)
        kgrad_ref[:, span] = turned(t_dot(scores_grad, q_ref[:, span]) * scale, cosine, sine).astype(BF)
    share = width // CHIPS
    for j, piece in enumerate(pieces):
        low = pl.multiple_of((place[1] ^ j) * share, HEAD_DIM)
        piece[:, :share] = kgrad_ref[:, pl.ds(low, share)]
        piece[:, share:] = qgrad_ref[:, pl.ds(low, share)]


def leading_kernel(
    qgrad_ref, kgrad_ref, vgrad_ref, x_ref, gain_ref, mixgrad_ref, wq, wk, wv,
    out_ref, norm_ref, shift_ref, w_ref, lead_ref, sems
):
    copies = [fetch(w, w_ref.at[i], sems.at[i]) for i, w in enumerate((wq, wk, wv))]
    normal, inverse = norm_stats(x_ref[...].astype(F32))
    for copy in copies:
        copy.wait()
    for low in range(0, x_ref.shape[1], WIDE):
        span = slice(low, low + WIDE)
        lead_ref[:, span] = (
            dot_t(qgrad_ref[...], w_ref[0, span, :])
            + dot_t(kgrad_ref[...], w_ref[1, span, :])
            + dot_t(vgrad_ref[...], w_ref[2, span, :])
        )
    part, norm_sum, shift_sum = norm_back(lead_ref[...], gain_ref[...], normal, inverse)
    norm_ref[...], shift_ref[...] = norm_sum, shift_sum
    out_ref[...] = (mixgrad_ref[...] + part).astype(BF)


def outer_into(lefts, rights, outs, core):
    width, share = lefts[0].shape[1], rights[0].shape[1]
    step = width // CHIPS
    for i, (left_ref, right) in enumerate(zip(lefts, rights)):
        for low in range(0, width, step):
            value = t_dot(left_ref[:, low : low + step], right).astype(BF)
            put_rows(value, outs, low, core, slice(i * share, (i + 1) * share))


def early_kernel(place, both_ref, right_ref, *refs):
    outs, lefts = refs[:-2], refs[-2:]
    tokens = right_ref.shape[1]
    for i, left_ref in enumerate(lefts):
        for j in range(CHIPS):
            left_ref[j * tokens : (j + 1) * tokens] = both_ref[j, (1 - i) * tokens : (2 - i) * tokens]
    right = right_ref[...].reshape(CHIPS * tokens, right_ref.shape[2])
    share = right.shape[1] // 2
    outer_into(lefts, (right[:, :share], right[:, share:]), outs, place[2])


def late_kernel(place, both_ref, *refs):
    pieces, outs, left_ref = refs[:CHIPS], refs[CHIPS:-1], refs[-1]
    tokens = pieces[0].shape[0]
    for j in range(CHIPS):
        left_ref[j * tokens : (j + 1) * tokens] = both_ref[place[1] ^ j, :tokens]
    right = jnp.concatenate([piece[...] for piece in pieces], axis=0)
    outer_into((left_ref,), (right,), outs, place[2])


def per_device(
    sequence_elements,
    result_sensitivity,
    mixer_gain,
    mixer_offset,
    question_matrix,
    lookup_matrix,
    content_matrix,
    mixer_projection_matrix,
    feedforward_gain,
    feedforward_offset,
    expand_matrix,
    inner_neuron_offset,
    contract_matrix,
    feedforward_result_offset,
    sequence_level_choice,
    servers_per_level,
    accepted_row_limit,
    server_selection,
):
    devices = lax.axis_size("dp")
    me = lax.axis_index("dp")
    groups = devices // GROUP
    z, chip, core = me // GROUP, me % GROUP // 2, me % 2
    tokens, width = sequence_elements.shape
    heads = width // HEAD_DIM
    rows, feed = expand_matrix.shape
    cols = contract_matrix.shape[0]
    offset_len = feedforward_result_offset.shape[0]
    levels = jnp.arange(LEVELS)
    block = 2 * cols
    units = groups * block
    gain_first, shift_first, gain_second, shift_second = (
        v.astype(F32)[None, :] for v in (mixer_gain, mixer_offset, feedforward_gain, feedforward_offset)
    )
    cosine, sine = (jnp.asarray(t) for t in rope_tables(tokens))
    flat, wide = (tokens, width), (1, width)
    square = (width, width)
    all_rows = (CHIPS * tokens, units)
    weight_space = pltpu.VMEM(square, BF)
    triple_space = pltpu.VMEM((3,) + square, BF)
    hidden_space = pltpu.VMEM((width, units), BF)
    dma, dmas = pltpu.SemaphoreType.DMA, pltpu.SemaphoreType.DMA((3,))
    aligned = rows % 16 == 0
    firsts = pltpu.SemaphoreType.DMA((2 * groups * CHIPS if aligned else 1,))
    seconds = pltpu.SemaphoreType.DMA((2 * groups,))
    place = jnp.stack([z, chip, core]).astype(jnp.int32)
    fence = lax.optimization_barrier

    expand_chunks = expand_matrix.reshape(rows, groups, CHIPS, 2, cols).transpose(2, 0, 3, 1, 4)
    expand_pieces = exchange(expand_chunks.reshape(CHIPS, rows, units))
    contract_steps = [line_step(None, contract_matrix, 1)]
    group_grad = share_out(result_sensitivity)
    normed_first, query_rot, key_rot, value_rows = call(
        project_kernel,
        [(flat, BF)] * 4,
        (sequence_elements, gain_first, shift_first, cosine, sine, question_matrix, lookup_matrix, content_matrix),
        [VMEM] * 5 + [ANY] * 3,
        [triple_space, dmas], micros=8)
    normed_first, query_rot, key_rot, value_rows, expand_pieces = fence(
        (normed_first, query_rot, key_rot, value_rows, expand_pieces)
    )

    expand_plane = jnp.concatenate(in_order(expand_pieces), axis=0)
    expand_steps = [line_step(None, expand_plane, 1)]
    both_rows, mixed, normed_second, probs = call(
        attend_kernel,
        [((2 * tokens, width), BF), (flat, F32), (flat, BF), ((heads, tokens, tokens), F32)],
        (
            query_rot, key_rot, value_rows, sequence_elements, gain_second, shift_second, normed_first,
            mixer_projection_matrix,
        ),
        [VMEM] * 7 + [ANY],
        [weight_space, dma], micros=6)
    both_rows, mixed, normed_second, contract_steps = fence((both_rows, mixed, normed_second, contract_steps))

    half = tokens // 2
    upper, lower = spread(normed_second[:half]), None
    mark = normed_second[:16, :128]
    expand_steps, _ = fence((expand_steps, normed_second))
    expand_steps.append(line_step(expand_steps[-1], expand_plane, 2))
    level = sequence_level_choice[0]
    choice = server_selection.reshape(-1)
    info = jnp.concatenate(
        [
            feedforward_result_offset.astype(F32),
            inner_neuron_offset.astype(F32),
            level.astype(F32)[None],
            jnp.min(choice).astype(F32)[None],
            choice.astype(F32),
        ]
    )
    info = jnp.pad(info, (0, -info.shape[0] % 128))
    mark, upper, expand_steps, group_grad = pause(mark, upper, expand_steps, group_grad)
    lower = spread(after(normed_second[half:], mark))
    for s in range(3, groups):
        expand_steps.append(line_step(expand_steps[-1], expand_plane, s))
    table = after(jnp.broadcast_to(info, (devices, 1) + info.shape), mark)
    table = lax.all_to_all(table, "dp", 0, 0, tiled=True).reshape(devices, -1)
    mark, lower, expand_steps, table = pause(mark, lower, expand_steps, table)
    result_offset = table[:, :offset_len].reshape(-1)
    hidden_offsets = table[:, offset_len : offset_len + cols]
    all_levels = table[:, offset_len + cols].astype(jnp.int32)
    all_lowest = table[:, offset_len + cols + 1].astype(jnp.int32)
    near = me ^ (2 * jnp.arange(CHIPS))
    slot_levels = jnp.take(all_levels, near)
    slot_choice = jnp.take(table[:, offset_len + cols + 2 :], near, axis=0)[:, :tokens].astype(jnp.int32)
    slot_hot = slot_levels[:, None] == levels[None, :]
    size = jnp.sum(jnp.where(slot_hot, servers_per_level[None, :], 0), axis=1)[:, None]
    limit = jnp.sum(jnp.where(slot_hot, accepted_row_limit[None, :], 0), axis=1)[:, None]
    server = slot_choice % size
    before = jnp.arange(tokens)[None, :] < jnp.arange(tokens)[:, None]
    same = before[None] & (server[:, None, :] == server[:, :, None])
    local = jnp.sum(same.astype(jnp.int32), axis=2)
    low = all_lowest[None, None, :]
    size, server = size[:, :, None], server[:, :, None]
    seen = (low + tokens - 1 - server + size) // size - (low - 1 - server + size) // size
    earlier = (jnp.arange(devices)[None, :] < near[:, None]) & (all_levels[None, :] == slot_levels[:, None])
    arrival = local + jnp.sum(jnp.where(earlier[:, None, :], seen, 0), axis=2)
    slot_kept = (arrival < limit).astype(F32)
    kept = slot_kept[0][:, None]
    slot_kept = slot_kept.reshape(-1, 1)
    kept_sensitivity = (result_sensitivity.astype(F32) * kept).astype(BF)
    starts = (jnp.arange(groups) * CHIPS + chip) * block
    active_block = starts[None, :] < (feed // 8) * (1 << slot_levels[:, None])
    mask = jnp.tile(jnp.repeat(active_block.astype(F32), cols, axis=1), (1, 2))
    hidden_offset = lax.dynamic_index_in_dim(
        hidden_offsets.reshape(groups, CHIPS, 2, cols), chip, 1, keepdims=False
    )
    hidden_offset = hidden_offset.transpose(1, 0, 2).reshape(1, -1)
    row_slots = [normed_second] + [piece for pair in zip(upper[1:], lower[1:]) for piece in pair]
    group_both = lax.all_gather(after(both_rows, lower), "dp", axis_index_groups=quads())
    expand_mine = line_stack(expand_plane, expand_steps)
    expand_other = swap(expand_mine, 1)
    contract_steps[0] = after(contract_steps[0], mark)
    contract_steps.append(line_step(contract_steps[-1], contract_matrix, 2))
    mark, expand_other, contract_steps = pause(mark, expand_other, contract_steps)
    for s in range(3, groups):
        contract_steps.append(line_step(contract_steps[-1], contract_matrix, s))
    if aligned:
        first_weight = (expand_mine, expand_other)
    else:
        pair = jnp.stack([expand_mine, expand_other]).reshape(2, groups, CHIPS, rows, units)
        pair = jnp.take(pair, (jnp.arange(groups) - z) % groups, axis=1)
        first_weight = (jnp.where(core == 0, pair, pair[::-1]).transpose(1, 2, 0, 3, 4).reshape(width, units),)

    active, slope = call(
        hidden_kernel,
        [(all_rows, BF), (all_rows, BF)],
        (place, *row_slots, hidden_offset, mask, *first_weight),
        [SMEM] + [VMEM] * (PIECES + 2) + [ANY] * len(first_weight),
        [hidden_space, firsts],
        micros=30,
    )
    active, contract_steps = fence((active, contract_steps))
    sides = 2 if aligned else 1
    down_mine, down_other = call(
        down_kernel, [((groups, cols, width), BF)] * 2, (place, active, group_grad, slot_kept), [SMEM] + [VMEM] * 3, micros=8
    )
    down_got = swap(down_other, 1)
    contract_mine = line_stack(contract_matrix, contract_steps)
    contract_other = swap(contract_mine, 1)
    contract_both = (down_mine.astype(F32) + down_got.astype(F32)).astype(BF)
    contract_both, contract_other = fence((contract_both, contract_other))
    share_contract = lax.psum_scatter(contract_both, "dp", scatter_dimension=0, axis_index_groups=lines())
    hidden_grad, hidden_sum, second_own, *second_sent = call(
        reverse_kernel,
        [(all_rows, BF), ((1, units), F32), (flat, F32)] + [(flat, BF)] * 3,
        (place, group_grad, slot_kept, slope, contract_mine, contract_other, *first_weight),
        [SMEM] + [VMEM] * 3 + [ANY] * (2 + len(first_weight)),
        [hidden_space, pltpu.VMEM((units, width), BF), firsts, seconds],
        micros=15,
    )
    hidden_grad, second_sent = fence((hidden_grad, second_sent))
    second_got = [swap(second_sent[j - 1], 2 * j) for j in range(1, CHIPS)]
    half_shape = (groups, CHIPS * rows) if aligned else (width,)
    bar_shape = (2 * groups, CHIPS * rows) if aligned else (width,)
    up_part, branch_sent = call(
        finish_kernel,
        [(bar_shape + (units,), BF), ((CHIPS,) + flat, BF)],
        (place, *row_slots, active, hidden_grad, contract_mine, contract_other),
        [SMEM] + [VMEM] * (PIECES + 2) + [ANY] * 2,
        [pltpu.VMEM((units, width), BF), seconds],
        micros=13,
    )
    up_part, second_got, group_both = fence((up_part, second_got, group_both))
    if not aligned:
        up_part = up_part.reshape(groups, CHIPS, 2, rows, units).transpose(0, 2, 1, 3, 4)
        up_part = up_part.reshape(2 * groups, CHIPS * rows, units)
    expand_rows = lax.psum_scatter(up_part, "dp", scatter_dimension=0, axis_index_groups=bars())

    def by_sides(parts):
        if aligned:
            return parts
        part = parts[0].reshape(groups, CHIPS, 2, rows, -1)
        return [
            lax.dynamic_index_in_dim(part, core ^ k, 2, keepdims=False).reshape(groups, CHIPS * rows, -1)
            for k in range(2)
        ]

    def add(mine, got):
        return (mine.astype(F32) + got.astype(F32)).astype(BF)


    share = width // CHIPS
    pair_shape = (tokens, 2 * share)
    mixed_grad, context_grad, value_grad, first_pair, midnorm_sum, midshift_sum = call(
        mixed_kernel,
        [(flat, F32), (flat, BF), (flat, BF), ((CHIPS,) + pair_shape, BF), (wide, F32), (wide, F32)],
        (
            second_own, *second_got, mixed, result_sensitivity, gain_second, mixer_projection_matrix,
            value_rows, probs,
        ),
        [VMEM] * 7 + [ANY] + [VMEM] * 2,
        [weight_space, pltpu.VMEM(flat, BF), dma],
        micros=8,
    )
    first_pair, context_grad, value_grad, share_contract = fence(
        (first_pair, context_grad, value_grad, share_contract)
    )
    first_pair = trade(first_pair)
    query_grad, key_grad, *second_pair = call(
        score_kernel,
        [(flat, BF)] * 2 + [(pair_shape, BF)] * CHIPS,
        (place, context_grad, query_rot, key_rot, value_rows, probs, cosine, sine),
        [SMEM] + [VMEM] * 7,
        micros=1,
    )
    second_pair = [piece if j == 0 else swap(piece, 2 * j) for j, piece in enumerate(second_pair)]
    query_grad, key_grad, first_pair = fence((query_grad, key_grad, first_pair))

    outer_shape = [(half_shape + (2 * share,), BF)] * sides
    left_space = pltpu.VMEM((CHIPS * tokens, width), BF)
    early = call(
        early_kernel, outer_shape, (place, group_both, first_pair), [SMEM] + [VMEM] * 2, [left_space] * 2, micros=6
    )
    early_mine, early_other = by_sides(early)
    early_both = add(early_mine, swap(early_other, 1))
    early_both, query_grad = fence((early_both, query_grad))
    early_sum = lax.psum_scatter(early_both, "dp", scatter_dimension=0, axis_index_groups=lines())
    layer_input_gradient, leadnorm_sum, leadshift_sum = call(
        leading_kernel,
        [(flat, BF), (wide, F32), (wide, F32)],
        (
            query_grad, key_grad, value_grad, sequence_elements, gain_first, mixed_grad,
            question_matrix, lookup_matrix, content_matrix,
        ),
        [VMEM] * 6 + [ANY] * 3,
        [triple_space, pltpu.VMEM(flat, F32), dmas],
        micros=13,
    )
    leadnorm_sum, second_pair = fence((leadnorm_sum, second_pair))
    late = call(
        late_kernel, outer_shape, (place, group_both, *second_pair), [SMEM] + [VMEM] * 5, [left_space], micros=1
    )
    late_mine, late_other = by_sides(late)
    branch = jnp.sum(trade(after(branch_sent, leadnorm_sum)).astype(F32), axis=0)
    late_both = add(late_mine, swap(late_other, 1))
    late_sum = line_sum(
        [lax.dynamic_index_in_dim(late_both, (z + s) % groups, 0, keepdims=False) for s in range(groups)]
    )
    branch = (branch + result_offset).astype(BF).astype(F32)
    layer_output = (mixed + kept * branch).astype(BF)

    def home(summed):
        return trade(summed.astype(BF).reshape(CHIPS, rows, -1))

    hidden_spot = (jnp.arange(CHIPS)[None, :, None, None] == chip).astype(F32)
    hidden_full = hidden_spot * hidden_sum.reshape(2, groups, cols).transpose(1, 0, 2)[:, None]
    result_sum = jnp.sum(kept_sensitivity.astype(F32), axis=0)
    vectors = [midnorm_sum, midshift_sum, leadnorm_sum, leadshift_sum, result_sum, hidden_full]
    vectors = jnp.concatenate([vector.reshape(devices, -1) for vector in vectors], axis=1)
    vectors = jnp.pad(vectors, ((0, 0), (0, -vectors.shape[1] % 128)))
    vectors = scatter_all(vectors.reshape(devices, -1, 128)).reshape(-1)
    small = [vectors[i * offset_len : (i + 1) * offset_len] for i in range(5)]
    share_hidden = vectors[5 * offset_len : 5 * offset_len + cols]

    expand_home = home(after(expand_rows, layer_output))
    share_expand = (
        expand_home.reshape(CHIPS, rows, 2, groups, cols).transpose(1, 3, 0, 2, 4).reshape(rows, feed).astype(F32)
    )
    last = jnp.concatenate([early_sum, after(late_sum.astype(BF), expand_home)], axis=1)
    last = home(last)

    def join(at):
        piece = last[:, :, at * share : (at + 1) * share]
        return piece.transpose(1, 0, 2).reshape(rows, width).astype(F32)

    share_mixing, share_value, share_key, share_query = (join(at) for at in range(4))
    return (
        layer_output,
        layer_input_gradient,
        small[2],
        small[3],
        share_query,
        share_key,
        share_value,
        share_mixing,
        small[0],
        small[1],
        share_expand,
        share_hidden,
        share_contract.astype(F32),
        small[4],
    )


def solution(mesh):
    split, line, whole = P("dp", None), P("dp"), P()
    return jax.shard_map(
        per_device,
        mesh=mesh,
        in_specs=(split, split) + (whole,) * 8 + (split, line, split, line, line, whole, whole, split),
        out_specs=(split, split, line, line, split, split, split, split, line, line, split, line, split, line),
        check_vma=False,
    )
```
